128 devices in a mesh: lon: 16 (over y, z_hi, core), lat: 8 (over x, z_lo).
Axes of the slice: x: 4, y: 4, z: 4 (z_hi: 2, z_lo: 2; z = z_hi * 2 + z_lo), core: 2. Of those that a mesh axis runs over, the one named last changes fastest.
Arguments:
- grid_state: bfloat16 [64, 1024, 256], P('lat', 'lon'), may hold values from -6 to 6
- encodings: bfloat16 [12288, 2, 256], P(('lon', 'lat')), may hold values from -6 to 6
- routes: int32 [12288, 2], replicated, may hold values from 0 to 127, all different within a row; in each aligned block of 96 rows (0 to 95, 96 to 191, ...) at most 2 rows name the same one
- w_query: bfloat16 [256, 256], replicated, may hold values from -0.375 to 0.375
- w_key: bfloat16 [256, 256], replicated, may hold values from -0.375 to 0.375
- w_value: bfloat16 [256, 256], replicated, may hold values from -0.375 to 0.375
- w_out: bfloat16 [256, 256], replicated, may hold values from -0.375 to 0.375
- kernels: bfloat16 [2, 7, 7, 256], replicated, may hold values from -0.875 to 0.875
- w_expand: bfloat16 [2, 256, 1024], replicated, may hold values from -0.375 to 0.375
- w_reduce: bfloat16 [2, 1024, 256], replicated, may hold values from -0.1875 to 0.1875
- cotangent: bfloat16 [64, 1024, 256], P('lat', 'lon'), may hold values from -6 to 6
Outputs:
- analysis: bfloat16 [64, 1024, 256], P('lat', 'lon')
- grad_encodings: float32 [12288, 2, 256], P(('lon', 'lat'))
- grad_attention: float32 [4, 256, 256], replicated
- grad_kernels: float32 [2, 7, 7, 256], replicated
- grad_expand: float32 [2, 256, 1024], replicated
- grad_reduce: float32 [2, 1024, 256], replicated
The draws below stay inside these ranges and needn't reach their ends.
Inputs may be any that keep to these rules, and one draw needn't show every extreme that they name: `routes`: each block names 2 different tiles; among the 96 blocks of one device at most 2 name the same tile, and exactly 2 in some device; every tile is named by some block.
All inputs are finite; a program needn't handle non-finite values.
Results may differ from the reference program's by a relative error of at most 0.022.
Values may be sent and summed in bfloat16 or wider, within the bound.
A program may use at most 128 MiB of HBM per device.

```python
import math
from functools import partial
import jax
import jax.numpy as jnp
import numpy as np
from jax import lax

C = 256
HEADS = 8
EXPAND = 1024
CLAT = 8
CLON = 64
OBLK = 2
TOP = 2
CAP = 2
BLOCKS = 2
BLK_DEV = 96
OBS = 12288
NLAT = 64
NLON = 1024
N_LON = 16
N_LAT = 8
DEVICES = 128


def block_scale(own_key, dims, split, smallest, largest):
    gain, own = 1.0, jax.random.fold_in(own_key, 6)
    for position, parts in split:
        steps = jnp.exp(jax.random.uniform(jax.random.fold_in(own, position), (parts,), jnp.float32, smallest / len(split), largest / len(split)))
        gain = gain * jnp.repeat(steps, dims[position] // parts).reshape([-1 if axis == position else 1 for axis in range(len(dims))])
    return gain


def assign_block(rng, own, number, rows, amount, top, most, skew):
    ranking = jax.random.permutation(rng, amount)
    packed, common = portions_of(amount, rows * top, most, skew, True), portions_of(amount, rows * top, most, skew, False)
    places = jnp.arange(amount)

    def named(lengths, rotation):
        used = int((lengths > 0).sum())
        fixed = max(1, used // 4)
        moved = fixed + (places - fixed + rotation * (used - fixed)) % max(1, amount - fixed)
        return jnp.zeros((amount,), jnp.int32).at[ranking[jnp.where(places < fixed, places, moved)]].set(jnp.asarray(lengths, jnp.int32))

    lengths = jnp.where(number % 4 == 0, named(packed, number // 4), named(common, number - number // 4 - 1))
    mixed = jax.random.permutation(jax.random.fold_in(own, 3), amount)
    source_of, taker = mixed[0:amount // 2 * 2:2], mixed[1:amount // 2 * 2:2]
    margin = jnp.minimum(lengths[source_of] - 1, most - lengths[taker]) // 2
    margin = jnp.where((source_of == ranking[0]) | (taker == ranking[0]) | (lengths[taker] == 0), 0, jnp.maximum(margin, 0))
    moved = jax.random.randint(jax.random.fold_in(own, 4), (amount // 2,), 0, 1 << 20) % (margin + 1)
    lengths = lengths.at[source_of].add(-moved).at[taker].add(moved)
    members = jnp.searchsorted(jnp.cumsum(lengths), jnp.arange(rows * top), side="right").astype(jnp.int32)
    table = members.reshape(top, rows).T
    table = table[jax.random.permutation(jax.random.fold_in(own, 1), rows)]
    rotation = jax.random.randint(jax.random.fold_in(own, 2), (rows, 1), 0, top)
    return jnp.take_along_axis(table, (jnp.arange(top)[None, :] + rotation) % top, axis=1)


def portions_of(amount, total, bound, skew, full):
    weights = [(1 << 20) // math.isqrt(grade ** skew) + 1 for grade in range(1, amount + 1)]
    largest = bound if full else min(bound, max(-(-total // amount), total * weights[0] // sum(weights)))
    least = 1 if total - largest >= amount - 1 else 0
    given, surplus = [largest] + [least] * (amount - 1), total - largest - least * (amount - 1)
    while surplus > 0:
        free = [i for i in range(1, amount) if given[i] < largest] or [i for i in range(1, amount) if given[i] < bound]
        pool, left = sum([weights[i] for i in free]), surplus
        for i in free:
            addition = min(bound - given[i], max(1, left * weights[i] // pool), surplus)
            given[i] = given[i] + addition
            surplus = surplus - addition
    return np.array(given)


def gaussian(stream_key, shape, scale, most, split=(), held_as=jnp.bfloat16):
    gain = block_scale(stream_key, shape, split, -0.22, 0.18) if split else 1.0
    array = jax.random.normal(stream_key, shape, jnp.float32) * scale * gain
    return jnp.minimum(jnp.maximum(array, -most), most).astype(held_as)


def setup_inputs(seed: int = 0) -> dict:
    key_list = jax.random.split(jax.random.key(seed), 12)
    grid_state = gaussian(key_list[0], (NLAT, NLON, C), 1.0, 6.0, ((0, 8), (1, 16)))
    encodings = gaussian(key_list[1], (OBS, OBLK, C), 1.0, 6.0, ((0, 128),))
    routes_keys = jax.random.split(jax.random.fold_in(key_list[2], 1), OBS // BLK_DEV)
    routes_turns = jax.random.permutation(jax.random.fold_in(key_list[2], 3), OBS // BLK_DEV)
    routes = jax.vmap(lambda own, number: assign_block(jax.random.fold_in(key_list[2], 2), own, number, BLK_DEV, DEVICES, TOP, CAP, 2))(routes_keys, routes_turns).reshape((OBS, TOP))
    w_query = gaussian(key_list[3], (C, C), C ** -0.5, 0.375)
    w_key = gaussian(key_list[4], (C, C), C ** -0.5, 0.375)
    w_value = gaussian(key_list[5], (C, C), C ** -0.5, 0.375)
    w_out = gaussian(key_list[6], (C, C), C ** -0.5, 0.375)
    kernels = gaussian(key_list[7], (BLOCKS, 7, 7, C), 49 ** -0.5, 0.875)
    w_expand = gaussian(key_list[8], (BLOCKS, C, EXPAND), C ** -0.5, 0.375)
    w_reduce = gaussian(key_list[9], (BLOCKS, EXPAND, C), EXPAND ** -0.5, 0.1875)
    cotangent = gaussian(key_list[10], (NLAT, NLON, C), 1.0, 6.0, ((0, 8), (1, 16)))
    return {"grid_state": grid_state, "encodings": encodings, "routes": routes, "w_query": w_query, "w_key": w_key, "w_value": w_value, "w_out": w_out, "kernels": kernels, "w_expand": w_expand, "w_reduce": w_reduce, "cotangent": cotangent}


EPSILON = 1e-06

def layer_norm(inputs):
    centred = inputs - lax.optimization_barrier(jnp.mean(inputs, axis=-1, keepdims=True))
    spread = lax.optimization_barrier(jnp.mean(centred * centred, axis=-1, keepdims=True))
    return centred * lax.rsqrt(spread + EPSILON)

def inner(first, second):
    return lax.dot_general(first, second, (((1,), (1,)), ((), ())), preferred_element_type=jnp.float32)

def outer_sum(first, second):
    return lax.dot_general(first, second, (((0,), (0,)), ((), ())), preferred_element_type=jnp.float32)

def split_heads(matrix, heads):
    return jnp.moveaxis(matrix.reshape(matrix.shape[0], heads, -1), 1, 0)

def merge_heads(stacked):
    return jnp.moveaxis(stacked, 0, 1).reshape(stacked.shape[1], -1)

def head_weights(queries, key_rows, live, scale):
    scores = inner(queries, key_rows) * scale
    raised = jnp.exp(scores) * live[None, :]
    return raised / lax.optimization_barrier(jnp.sum(raised, axis=-1, keepdims=True))

def attend_forward(queries, key_rows, value_rows, live, heads):
    scale = 1.0 / math.sqrt(queries.shape[1] // heads)

    def one_head(pieces):
        weights = head_weights(pieces[0], pieces[1], live, scale)
        return jnp.dot(weights.astype(jnp.bfloat16), pieces[2], preferred_element_type=jnp.float32).astype(jnp.bfloat16)
    return merge_heads(lax.map(one_head, (split_heads(queries, heads), split_heads(key_rows, heads), split_heads(value_rows, heads))))

def attend_backward(queries, key_rows, value_rows, live, grad_context, heads):
    scale = 1.0 / math.sqrt(queries.shape[1] // heads)

    def one_head(pieces):
        head_q, head_k, head_v, head_g = pieces
        weights = head_weights(head_q, head_k, live, scale)
        grad_probs = inner(head_g, head_v)
        grad_values = outer_sum(weights.astype(jnp.bfloat16), head_g)
        grad_scores = weights * (grad_probs - lax.optimization_barrier(jnp.sum(grad_probs * weights, axis=-1, keepdims=True)))
        grad_scores = (grad_scores * scale).astype(jnp.bfloat16)
        grad_queries = jnp.dot(grad_scores, head_k, preferred_element_type=jnp.float32)
        grad_keys = outer_sum(grad_scores, head_q)
        return (grad_queries, grad_keys, grad_values)
    results = lax.map(one_head, (split_heads(queries, heads), split_heads(key_rows, heads), split_heads(value_rows, heads), split_heads(grad_context, heads)))
    return (merge_heads(results[0]), merge_heads(results[1]), merge_heads(results[2]))

def mix_forward(state_rows, mixed, expand_w, reduce_w):
    normed = layer_norm(mixed).astype(jnp.bfloat16)
    wide = jax.nn.gelu(jnp.dot(normed, expand_w, preferred_element_type=jnp.float32)).astype(jnp.bfloat16)
    return (state_rows.astype(jnp.float32) + jnp.dot(wide, reduce_w, preferred_element_type=jnp.float32)).astype(jnp.bfloat16)

def mix_backward(mixed, expand_w, reduce_w, gradient):
    normed_full, norm_back = jax.vjp(layer_norm, mixed)
    normed = normed_full.astype(jnp.bfloat16)
    pre_gelu = jnp.dot(normed, expand_w, preferred_element_type=jnp.float32)
    gelu_out, gelu_back = jax.vjp(jax.nn.gelu, pre_gelu)
    wide = gelu_out.astype(jnp.bfloat16)
    grad_low = gradient.astype(jnp.bfloat16)
    grad_reduce = outer_sum(wide, grad_low)
    grad_wide = inner(grad_low, reduce_w)
    grad_pre = gelu_back(grad_wide)[0].astype(jnp.bfloat16)
    grad_expand = outer_sum(normed, grad_pre)
    grad_mixed = norm_back(inner(grad_pre, expand_w))[0]
    return (grad_mixed, grad_expand, grad_reduce)

def mix_map(pieces, expand_w, reduce_w):
    return mix_forward(pieces[0], pieces[1], expand_w, reduce_w)

def mix_back_map(pieces, expand_w, reduce_w):
    return mix_backward(pieces[0], expand_w, reduce_w, pieces[1])

def depthwise(padded, kernel, height, breadth):
    total = jnp.zeros((height, breadth, padded.shape[2]), jnp.float32)
    for shift_row in range(7):
        for shift_col in range(7):
            window = padded[shift_row:shift_row + height, shift_col:shift_col + breadth]
            total = total + window.astype(jnp.float32) * kernel[shift_row, shift_col].astype(jnp.float32)
    return total

def kernel_grad(padded, grad_low, height, breadth):
    grad_full = grad_low.astype(jnp.float32)
    partial_sums = []
    for shift_row in range(7):
        for shift_col in range(7):
            window = padded[shift_row:shift_row + height, shift_col:shift_col + breadth]
            partial_sums.append(lax.optimization_barrier(jnp.sum(window.astype(jnp.float32) * grad_full, axis=(0, 1))))
    return jnp.stack(partial_sums).reshape(7, 7, -1)

def dispatch_matrix(own_routes, devices, slots):
    count_blocks, fanout = own_routes.shape
    targets = own_routes.reshape(count_blocks * fanout)
    hits = (targets[:, None] == jnp.arange(devices, dtype=jnp.int32)[None, :]).astype(jnp.int32)
    earlier = jnp.cumsum(hits, axis=0, dtype=jnp.int32) - hits
    ranks = lax.optimization_barrier(jnp.sum(earlier * hits, axis=1, dtype=jnp.int32))
    slot_ids = targets * slots + ranks
    slot_hot = (slot_ids[:, None] == jnp.arange(devices * slots, dtype=jnp.int32)[None, :]).astype(jnp.float32)
    owners = jnp.arange(count_blocks * fanout, dtype=jnp.int32) // fanout
    block_hot = (owners[:, None] == jnp.arange(count_blocks, dtype=jnp.int32)[None, :]).astype(jnp.float32)
    return lax.dot_general(slot_hot, block_hot, (((0,), (0,)), ((), ())), precision=lax.Precision.HIGHEST, preferred_element_type=jnp.float32)

def source_send(chosen, block_rows):
    return jnp.dot(chosen.astype(jnp.bfloat16), block_rows, preferred_element_type=jnp.float32).astype(jnp.bfloat16)

def source_backward(returned, chosen, enc_slots, key_w, value_w):
    channels = enc_slots.shape[1]
    grad_keys = returned[:, :channels]
    grad_values = returned[:, channels:]
    grad_key_w = outer_sum(enc_slots, grad_keys)
    grad_value_w = outer_sum(enc_slots, grad_values)
    slot_grad = inner(grad_keys, key_w) + inner(grad_values, value_w)
    grad_blocks = lax.dot_general(chosen, slot_grad.reshape(chosen.shape[0], -1), (((0,), (0,)), ((), ())), precision=lax.Precision.HIGHEST, preferred_element_type=jnp.float32)
    return (grad_blocks, grad_key_w, grad_value_w)

def to_tiles(grid):
    return grid.reshape(N_LAT, CLAT, N_LON, CLON, -1).transpose(2, 0, 1, 3, 4).reshape(N_LON * N_LAT, CLAT * CLON, -1)

def to_grid(tiles):
    return tiles.reshape(N_LON, N_LAT, CLAT, CLON, -1).transpose(1, 2, 0, 3, 4).reshape(N_LAT * CLAT, N_LON * CLON, -1)

def pad_grid(grid):
    wrapped = jnp.concatenate([grid[:, -3:], grid, grid[:, :3]], axis=1)
    return jnp.pad(wrapped, ((3, 3), (0, 0), (0, 0)))

def reference(grid_state, encodings, routes, w_query, w_key, w_value, w_out, kernels, w_expand, w_reduce, cotangent):
    devices = N_LON * N_LAT
    height, breadth, channels = grid_state.shape
    tokens = encodings.shape[1]
    blocks = encodings.shape[0] // devices
    token_rows = encodings.reshape(-1, channels)
    key_own = jnp.dot(token_rows, w_key, preferred_element_type=jnp.float32).astype(jnp.bfloat16)
    value_own = jnp.dot(token_rows, w_value, preferred_element_type=jnp.float32).astype(jnp.bfloat16)
    pairs = jnp.concatenate([key_own, value_own], axis=1).reshape(devices, blocks, tokens * 2 * channels).astype(jnp.float32)
    per_source = routes.reshape(devices, blocks, -1)

    def source_dispatch(own_routes):
        return dispatch_matrix(own_routes, devices, CAP)
    chosen = jax.vmap(source_dispatch)(per_source)
    counts = lax.optimization_barrier(jnp.sum((per_source.reshape(devices, 1, -1) == jnp.arange(devices, dtype=jnp.int32)[None, :, None]).astype(jnp.int32), axis=2, dtype=jnp.int32))
    cap_index = jnp.arange(CAP, dtype=jnp.int32)

    def tile_keys(tile_index):
        picked_map = lax.dynamic_slice_in_dim(chosen, tile_index * CAP, CAP, 1)
        picked = jnp.einsum('scb,sbk->sck', picked_map, pairs).astype(jnp.bfloat16).reshape(-1, 2 * channels)
        live = (cap_index[None, :] < counts[:, tile_index][:, None]).astype(jnp.float32)
        return (picked[:, :channels], picked[:, channels:], jnp.repeat(live.reshape(-1), tokens))

    def tile_queries(tile_state):
        normed = layer_norm(tile_state.astype(jnp.float32)).astype(jnp.bfloat16)
        return (normed, jnp.dot(normed, w_query, preferred_element_type=jnp.float32).astype(jnp.bfloat16))

    def tile_front(pieces):
        tile_state, tile_index = pieces
        key_rows, value_rows, live = tile_keys(tile_index)
        normed, queries = tile_queries(tile_state)
        context = attend_forward(queries, key_rows, value_rows, live, HEADS)
        attended = (tile_state.astype(jnp.float32) + jnp.dot(context, w_out, preferred_element_type=jnp.float32)).astype(jnp.bfloat16)
        return (attended, context)
    tiles = to_tiles(grid_state)
    tile_ids = jnp.arange(devices, dtype=jnp.int32)
    attended, contexts = lax.map(tile_front, (tiles, tile_ids))
    current = to_grid(attended)
    saved = []
    for block_index in range(BLOCKS):
        padded = pad_grid(current)
        mixed = depthwise(padded, kernels[block_index], height, breadth)
        saved.append((padded, mixed))
        updated = lax.map(partial(mix_map, expand_w=w_expand[block_index], reduce_w=w_reduce[block_index]), (to_tiles(current), to_tiles(mixed)))
        current = to_grid(updated)
    analysis = current
    gradient = cotangent.astype(jnp.float32)
    grad_kernels = [None] * BLOCKS
    grad_expands = [None] * BLOCKS
    grad_reduces = [None] * BLOCKS
    for block_index in reversed(range(BLOCKS)):
        padded, mixed = saved[block_index]
        grad_mixed, grad_expand_tiles, grad_reduce_tiles = lax.map(partial(mix_back_map, expand_w=w_expand[block_index], reduce_w=w_reduce[block_index]), (to_tiles(mixed), to_tiles(gradient)))
        grad_low = to_grid(grad_mixed).astype(jnp.bfloat16)
        grad_kernels[block_index] = kernel_grad(padded, grad_low, height, breadth)
        grad_expands[block_index] = lax.optimization_barrier(jnp.sum(grad_expand_tiles, axis=0))
        grad_reduces[block_index] = lax.optimization_barrier(jnp.sum(grad_reduce_tiles, axis=0))
        gradient = gradient + depthwise(pad_grid(grad_low), kernels[block_index][::-1, ::-1], height, breadth)

    def tile_back(pieces):
        tile_state, context, grad_tile, tile_index = pieces
        key_rows, value_rows, live = tile_keys(tile_index)
        normed, queries = tile_queries(tile_state)
        grad_low = grad_tile.astype(jnp.bfloat16)
        grad_out_w = outer_sum(context, grad_low)
        grad_context = inner(grad_low, w_out).astype(jnp.bfloat16)
        grad_queries, grad_keys, grad_values = attend_backward(queries, key_rows, value_rows, live, grad_context, HEADS)
        grad_query_w = outer_sum(normed, grad_queries.astype(jnp.bfloat16))
        returned = jnp.concatenate([grad_keys.astype(jnp.bfloat16), grad_values.astype(jnp.bfloat16)], axis=1).reshape(devices, -1)
        return (returned, grad_query_w, grad_out_w)
    returned, grad_query_tiles, grad_out_tiles = lax.map(tile_back, (tiles, contexts, to_tiles(gradient), tile_ids))
    returned = jnp.swapaxes(returned, 0, 1)

    def source_back(pieces):
        back_rows, picked_map, block_rows = pieces
        enc_slots = source_send(picked_map, block_rows).reshape(-1, channels)
        return source_backward(back_rows.reshape(-1, 2 * channels), picked_map, enc_slots, w_key, w_value)
    grad_blocks, grad_key_tiles, grad_value_tiles = lax.map(source_back, (returned, chosen, encodings.reshape(devices, blocks, tokens * channels)))
    grad_encodings = grad_blocks.reshape(devices * blocks, tokens, channels)
    grad_attention = jnp.stack([lax.optimization_barrier(jnp.sum(grad_query_tiles, axis=0)), lax.optimization_barrier(jnp.sum(grad_key_tiles, axis=0)), lax.optimization_barrier(jnp.sum(grad_value_tiles, axis=0)), lax.optimization_barrier(jnp.sum(grad_out_tiles, axis=0))])
    return (analysis, grad_encodings, grad_attention, jnp.stack(grad_kernels), jnp.stack(grad_expands), jnp.stack(grad_reduces))
```

```python
import functools
import math

import jax
import jax.numpy as jnp
from jax import lax
from jax.experimental import pallas as pl
from jax.experimental.pallas import tpu as pltpu
from jax.sharding import PartitionSpec as P

MESH = pl.DeviceIdType.MESH
F32 = jnp.float32
BF16 = jnp.bfloat16

HEADS = 8
DEPTH = 32
CH = 256
WIDE = 1024
ROWS = 8
COLS = 64
CELLS = ROWS * COLS
NLON = 16
NLAT = 8
NYZ = 8
DEVICES = NLON * NLAT
BLOCKS_DEV = 96
SLOTS = 512
EPSILON = 1e-06
SCALE = 1.0 / math.sqrt(DEPTH)
GELU_0 = math.sqrt(2.0 / math.pi)
GELU_1 = GELU_0 * 0.044715
PAD_ROWS = ROWS + 6
PAD_COLS = 80
BIG = 2048
KROWS = 128


def mm(a, b):
    return jnp.dot(a, b, preferred_element_type=F32)


def mm_nt(a, b):
    return lax.dot_general(a, b, (((1,), (1,)), ((), ())), preferred_element_type=F32)


def mm_tn(a, b):
    return lax.dot_general(a, b, (((0,), (0,)), ((), ())), preferred_element_type=F32)


def loop(low, high, body):
    def step(index, carry):
        body(index)
        return carry

    lax.fori_loop(low, high, step, 0)


def aligned(value, by):
    return pl.multiple_of(value, by)


class Exchange:
    def __init__(self, place, source, half, level_1, part, level_2, total, sems, rows):
        self.lon, self.lat, self.core, self.yz = place
        self.source, self.half, self.level_1 = source, half, level_1
        self.part, self.level_2, self.total = part, level_2, total
        self.sems = sems
        self.r1, self.r2, self.r3 = rows // 2, rows // 16, rows // 128

    def copy(self, src, dst, index, lon, lat):
        return pltpu.make_async_remote_copy(
            src_ref=src,
            dst_ref=dst,
            send_sem=self.sems.at[0, index],
            recv_sem=self.sems.at[1, index],
            device_id=(lon, lat),
            device_id_type=MESH,
        )

    def pair(self):
        return self.lon + 1 - 2 * self.core

    def lat_peer(self, k):
        return lax.rem(self.lat + k, NLAT)

    def lat_from(self, k):
        return lax.rem(self.lat + NLAT - k, NLAT)

    def yz_peer(self, k):
        return lax.rem(self.yz + k, NYZ)

    def yz_from(self, k):
        return lax.rem(self.yz + NYZ - k, NYZ)

    def copy_0(self):
        other = aligned((1 - self.core) * self.r1, self.r1)
        return self.copy(
            self.source.at[pl.ds(other, self.r1)], self.half.at[...], 0, self.pair(), self.lat
        )

    def start_0(self):
        self.copy_0().start()

    def copy_1(self, k):
        peer = self.lat_peer(k)
        return self.copy(
            self.half.at[pl.ds(aligned(peer * self.r2, self.r2), self.r2)],
            self.level_1.at[k],
            k,
            self.lon,
            peer,
        )

    def start_1(self):
        self.copy_0().wait()
        mine = aligned(self.core * self.r1, self.r1)
        step = self.r1 // 4

        def add(i):
            at = aligned(i * step, step)
            self.half[pl.ds(at, step)] = (
                self.half[pl.ds(at, step)].astype(F32)
                + self.source[pl.ds(aligned(mine + at, step), step)].astype(F32)
            ).astype(BF16)

        loop(0, 4, add)
        loop(1, NLAT, lambda k: self.copy_1(k).start())

    def copy_2(self, k):
        peer = self.yz_peer(k)
        return self.copy(
            self.part.at[pl.ds(aligned(peer * self.r3, self.r3), self.r3)],
            self.level_2.at[k],
            8 + k,
            peer * 2 + self.core,
            self.lat,
        )

    def start_2(self):
        loop(1, NLAT, lambda k: self.copy_1(k).wait())
        total = self.half[pl.ds(aligned(self.lat * self.r2, self.r2), self.r2)].astype(F32)
        for k in range(1, NLAT):
            total = total + self.level_1[k].astype(F32)
        self.part[...] = total.astype(BF16)
        loop(1, NYZ, lambda k: self.copy_2(k).start())

    def offset(self, core, lat, yz):
        return core * self.r1 + lat * self.r2 + yz * self.r3

    def copy_3(self, k):
        rows = pl.ds(aligned(self.offset(self.core, self.lat, self.yz), self.r3), self.r3)
        return self.copy(
            self.total.at[rows],
            self.total.at[rows],
            16 + k,
            self.yz_peer(k) * 2 + self.core,
            self.lat,
        )

    def start_3(self):
        loop(1, NYZ, lambda k: self.copy_2(k).wait())
        total = self.part[pl.ds(aligned(self.yz * self.r3, self.r3), self.r3)].astype(F32)
        for k in range(1, NYZ):
            total = total + self.level_2[k].astype(F32)
        rows = pl.ds(aligned(self.offset(self.core, self.lat, self.yz), self.r3), self.r3)
        self.total[rows] = total.astype(BF16)
        loop(1, NYZ, lambda k: self.copy_3(k).start())

    def copy_4(self, k):
        rows = pl.ds(aligned(self.offset(self.core, self.lat, 0), self.r2), self.r2)
        return self.copy(
            self.total.at[rows], self.total.at[rows], 24 + k, self.lon, self.lat_peer(k)
        )

    def start_4(self):
        def settle(k):
            self.copy_3(k).wait_send()
            rows = pl.ds(
                aligned(self.offset(self.core, self.lat, self.yz_from(k)), self.r3), self.r3
            )
            self.copy(
                self.total.at[rows], self.total.at[rows], 16 + k, self.lon, self.lat
            ).wait_recv()

        loop(1, NYZ, settle)
        loop(1, NLAT, lambda k: self.copy_4(k).start())

    def copy_5(self):
        rows = pl.ds(aligned(self.core * self.r1, self.r1), self.r1)
        return self.copy(self.total.at[rows], self.total.at[rows], 8, self.pair(), self.lat)

    def start_5(self):
        def settle(k):
            self.copy_4(k).wait_send()
            rows = pl.ds(aligned(self.offset(self.core, self.lat_from(k), 0), self.r2), self.r2)
            self.copy(
                self.total.at[rows], self.total.at[rows], 24 + k, self.lon, self.lat
            ).wait_recv()

        loop(1, NLAT, settle)
        self.copy_5().start()

    def finish(self):
        self.copy_5().wait_send()
        rows = pl.ds(aligned((1 - self.core) * self.r1, self.r1), self.r1)
        self.copy(
            self.total.at[rows], self.total.at[rows], 8, self.lon, self.lat
        ).wait_recv()


class SmallExchange:
    def __init__(self, place, source, level_1, part, level_2, total, sems):
        self.lon, self.lat, self.core, self.yz = place
        self.source, self.level_1, self.part = source, level_1, part
        self.level_2, self.total, self.sems = level_2, total, sems

    def copy(self, src, dst, index, lon, lat):
        return pltpu.make_async_remote_copy(
            src_ref=src,
            dst_ref=dst,
            send_sem=self.sems.at[0, index],
            recv_sem=self.sems.at[1, index],
            device_id=(lon, lat),
            device_id_type=MESH,
        )

    def copy_0(self, k):
        peer = lax.rem(self.lat + k, NLAT)
        return self.copy(
            self.source.at[pl.ds(aligned(peer * 16, 16), 16)], self.level_1.at[k], k, self.lon, peer
        )

    def start_0(self):
        loop(1, NLAT, lambda k: self.copy_0(k).start())

    def copy_1(self, k):
        peer = lax.rem(self.lon + k, NLON)
        return self.copy(self.part.at[...], self.level_2.at[k], 8 + k, peer, self.lat)

    def start_1(self):
        loop(1, NLAT, lambda k: self.copy_0(k).wait())
        total = self.source[pl.ds(aligned(self.lat * 16, 16), 16)].astype(F32)
        for k in range(1, NLAT):
            total = total + self.level_1[k].astype(F32)
        self.part[...] = total.astype(BF16)
        loop(1, NLON, lambda k: self.copy_1(k).start())

    def copy_2(self, k):
        rows = pl.ds(aligned(self.lat * 16, 16), 16)
        peer = lax.rem(self.lat + k, NLAT)
        return self.copy(self.total.at[rows], self.total.at[rows], 24 + k, self.lon, peer)

    def start_2(self):
        loop(1, NLON, lambda k: self.copy_1(k).wait())
        self.level_2[0] = self.part[...]
        total = jnp.zeros((16, CH), F32)
        for index in range(NLON):
            slot = lax.rem(self.lon - index + NLON, NLON)
            total = total + self.level_2[slot].astype(F32)
        self.total[pl.ds(aligned(self.lat * 16, 16), 16)] = total.astype(BF16)
        loop(1, NLAT, lambda k: self.copy_2(k).start())

    def finish(self):
        def settle(k):
            self.copy_2(k).wait_send()
            rows = pl.ds(aligned(lax.rem(self.lat + NLAT - k, NLAT) * 16, 16), 16)
            self.copy(
                self.total.at[rows], self.total.at[rows], 24 + k, self.lon, self.lat
            ).wait_recv()

        loop(1, NLAT, settle)


class Halo:
    def __init__(self, place, tile, rows, cols, corners, sems):
        self.lon, self.lat = place[0], place[1]
        self.tile, self.rows, self.cols, self.corners, self.sems = tile, rows, cols, corners, sems

    def copies(self):
        east, west = lax.rem(self.lon + 1, NLON), lax.rem(self.lon + NLON - 1, NLON)
        south, north = lax.rem(self.lat + 1, NLAT), lax.rem(self.lat + NLAT - 1, NLAT)
        top, bottom, whole = pl.ds(0, 3), pl.ds(ROWS - 3, 3), pl.ds(0, ROWS)
        left, right, wide = pl.ds(0, 16), pl.ds(COLS - 16, 16), pl.ds(0, COLS)
        plan = [
            (top, wide, self.rows.at[1], self.lon, north),
            (bottom, wide, self.rows.at[0], self.lon, south),
            (whole, left, self.cols.at[1], west, self.lat),
            (whole, right, self.cols.at[0], east, self.lat),
            (top, left, self.corners.at[3], west, north),
            (top, right, self.corners.at[2], east, north),
            (bottom, left, self.corners.at[1], west, south),
            (bottom, right, self.corners.at[0], east, south),
        ]
        return [
            pltpu.make_async_remote_copy(
                src_ref=self.tile.at[r, c],
                dst_ref=dst,
                send_sem=self.sems.at[0, index],
                recv_sem=self.sems.at[1, index],
                device_id=(lon, lat),
                device_id_type=MESH,
            )
            for index, (r, c, dst, lon, lat) in enumerate(plan)
        ]

    def start(self):
        for copy in self.copies():
            copy.start()

    def fill_inner(self, padded):
        for row in range(ROWS):
            cells = self.tile[row].astype(F32)
            for half in range(2):
                padded[half, 3 + row, 8 : 8 + COLS, :] = cells[:, half * 128 : half * 128 + 128]

    def fill_edges(self, padded):
        for copy in self.copies():
            copy.wait()
        has_north = jnp.where(self.lat > 0, 1.0, 0.0).astype(F32)
        has_south = jnp.where(self.lat < NLAT - 1, 1.0, 0.0).astype(F32)
        for half in range(2):
            lanes = slice(half * 128, half * 128 + 128)
            for row in range(ROWS):
                padded[half, 3 + row, 0:8, :] = self.cols[0, row, 8:16, lanes].astype(F32)
                padded[half, 3 + row, 72:80, :] = self.cols[1, row, 0:8, lanes].astype(F32)
            for row in range(3):
                for side, there, start in ((0, has_north, 0), (1, has_south, 3 + ROWS)):
                    padded[half, start + row, 8 : 8 + COLS, :] = (
                        self.rows[side, row, :, lanes].astype(F32) * there
                    )
                    padded[half, start + row, 0:8, :] = (
                        self.corners[2 * side, row, 8:16, lanes].astype(F32) * there
                    )
                    padded[half, start + row, 72:80, :] = (
                        self.corners[2 * side + 1, row, 0:8, lanes].astype(F32) * there
                    )


def correlate(padded, taps, block, flipped, store):
    def one_half(half):
        for chunk in range(4):
            sums = [None] * ROWS
            for b in range(7):
                rows = [
                    padded[half, row, chunk * 16 + b + 5 : chunk * 16 + b + 21, :]
                    for row in range(PAD_ROWS)
                ]
                for a in range(7):
                    tap_id = (6 - a) * 7 + (6 - b) if flipped else a * 7 + b
                    tap = taps[half, tap_id, block : block + 1, :]
                    for row in range(ROWS):
                        term = rows[row + a] * tap
                        sums[row] = term if sums[row] is None else sums[row] + term
            store(half, chunk, sums)

    loop(0, 2, one_half)


def kernel_grads(padded, inner, results, block):
    def one_half(half):
        for b in range(7):
            sums = [None] * 7
            for chunk in range(8):
                rows = [
                    padded[half, row, chunk * 8 + b + 5 : chunk * 8 + b + 13, :]
                    for row in range(PAD_ROWS)
                ]
                grads = [
                    inner[half, row, chunk * 8 : chunk * 8 + 8, :] for row in range(ROWS)
                ]
                for a in range(7):
                    for row in range(ROWS):
                        term = rows[row + a] * grads[row]
                        sums[a] = term if sums[a] is None else sums[a] + term
            for a in range(7):
                results[half, pl.ds(block * 56 + a * 7 + b, 1), :] = jnp.sum(
                    sums[a], axis=0, keepdims=True
                )

    loop(0, 2, one_half)


def iota(shape, dim):
    return lax.broadcasted_iota(jnp.int32, shape, dim)


def one_hot(condition):
    return jnp.where(condition, 1.0, 0.0).astype(BF16)


def normalise(values):
    centred = values - jnp.mean(values, axis=-1, keepdims=True)
    spread = jnp.mean(centred * centred, axis=-1, keepdims=True)
    scale = lax.rsqrt(spread + EPSILON)
    return centred * scale, scale


def kernel(
    grid_ref,
    enc_ref,
    routes_ref,
    wq_ref,
    wk_ref,
    wv_ref,
    wo_ref,
    kernels_ref,
    we_ref,
    wr_ref,
    cot_ref,
    analysis_ref,
    grad_enc_ref,
    out_attention,
    out_kernels,
    out_1,
    out_0,
    chosen_ref,
    send_a,
    recv_a,
    send_b,
    recv_b,
    back_b,
    got_b,
    back_a,
    got_a,
    live_ref,
    normed_ref,
    q_ref,
    qt_ref,
    k_ref,
    kt_ref,
    v_ref,
    vt_ref,
    probs_ref,
    ctx_t_ref,
    st_ref,
    gl_ref,
    pad_ref,
    pad_back,
    inner_ref,
    taps_ref,
    kgrad_ref,
    xhat_ref,
    rstd_ref,
    nrm_ref,
    wide_ref,
    dgelu_ref,
    gpre_ref,
    grad_ref,
    low_ref,
    gctx_ref,
    gt_ref,
    dq_t_ref,
    dk_ref,
    dv_ref,
    halo_rows,
    halo_cols,
    halo_corners,
    x_attention,
    x_kernels,
    x_1,
    x_0,
    half_att,
    half_1,
    half_0,
    l1_att,
    l1_1,
    l1_0,
    part_att,
    part_1,
    part_0,
    l2_att,
    l2_1,
    l2_0,
    l1_k,
    part_k,
    l2_k,
    a2a_sems,
    halo_sems,
    sems_att,
    sems_1,
    sems_0,
    sems_k,
):
    lon, lat = lax.axis_index("lon"), lax.axis_index("lat")
    core, yz = lax.rem(lon, 2), lon // 2
    place = (lon, lat, core, yz)
    me = lon * NLAT + lat

    barrier = pltpu.get_barrier_semaphore()

    def greet(to_lon, to_lat):
        pl.semaphore_signal(barrier, inc=1, device_id=(to_lon, to_lat), device_id_type=MESH)

    loop(1, NLAT, lambda k: greet(lon, lax.rem(lat + k, NLAT)))
    loop(1, NLON, lambda k: greet(lax.rem(lon + k, NLON), lat))
    for dx in (1, NLON - 1):
        for dy in (1, NLAT - 1):
            greet(lax.rem(lon + dx, NLON), lax.rem(lat + dy, NLAT))

    row_id = iota((DEVICES, BLOCKS_DEV), 0)
    tile_id = lax.rem(row_id, NLON) * NLAT + row_id // NLON
    hits = (routes_ref[0, pl.ds(me, 1), :] == tile_id) | (
        routes_ref[1, pl.ds(me, 1), :] == tile_id
    )
    before = one_hot(iota((BLOCKS_DEV, BLOCKS_DEV), 0) < iota((BLOCKS_DEV, BLOCKS_DEV), 1))
    hot = one_hot(hits)
    earlier = mm(hot, before)
    for c in range(2):
        chosen = jnp.where(jnp.abs(earlier - c) < 0.5, hot.astype(F32), 0.0).astype(BF16)
        chosen_ref[c] = chosen
        send_a[:, c * 512 : c * 512 + 512] = mm(chosen, enc_ref[...]).astype(BF16)

    pl.semaphore_wait(barrier, NLAT - 1 + NLON - 1 + 4)

    def a2a(src, dst, index, to_lon, to_lat):
        return pltpu.make_async_remote_copy(
            src_ref=src,
            dst_ref=dst,
            send_sem=a2a_sems.at[0, index],
            recv_sem=a2a_sems.at[1, index],
            device_id=(to_lon, to_lat),
            device_id_type=MESH,
        )

    def block(index):
        return pl.ds(aligned(index * 16, 16), 16)

    def along_lat(src, dst, base, k, incoming):
        peer = lax.rem(lat + (NLAT - k if incoming else k), NLAT)
        if incoming:
            return a2a(src.at[block(peer)], dst.at[block(peer)], base + k, lon, lat)
        return a2a(src.at[block(peer)], dst.at[block(lat)], base + k, lon, peer)

    def along_lon(src, dst, base, k, incoming):
        peer = lax.rem(lon + (NLON - k if incoming else k), NLON)
        if incoming:
            return a2a(src.at[block(peer)], dst.at[block(peer)], base + k, lon, lat)
        return a2a(src.at[block(peer)], dst.at[block(lon)], base + k, peer, lat)

    def start_hop(route, src, dst, base, count):
        loop(1, count, lambda k: route(src, dst, base, k, False).start())

    def end_hop(route, src, dst, base, count):
        def settle(k):
            route(src, dst, base, k, False).wait_send()
            route(src, dst, base, k, True).wait_recv()

        loop(1, count, settle)

    start_hop(along_lat, send_a, recv_a, 0, NLAT)
    recv_a[block(lat)] = send_a[block(lat)]

    normed = normalise(grid_ref[...].astype(F32))[0].astype(BF16)
    normed_ref[...] = normed
    queries = mm(normed, wq_ref[...]).astype(BF16)
    q_ref[...] = queries
    qt_ref[...] = queries.T
    mine = jnp.where(routes_ref[0] == me, 1.0, 0.0) + jnp.where(routes_ref[1] == me, 1.0, 0.0)
    counts = jnp.broadcast_to(jnp.sum(mine, axis=1, keepdims=True), (DEVICES, CH)).astype(BF16)
    slot = iota((256, DEVICES), 0)
    expand = one_hot((slot // 16) * NLAT + lax.rem(slot, NLAT) == iota((256, DEVICES), 1))
    rank = (lax.rem(iota((256, CH), 0), 16) // NLAT).astype(F32)
    live = jnp.where(mm(expand, counts) > rank + 0.5, 1.0, 0.0)
    live_ref[0:256] = live
    live_ref[256:512] = live
    for a in range(7):
        for b in range(7):
            tap = kernels_ref[a, b].astype(F32)
            for half in range(2):
                taps_ref[half, a * 7 + b] = tap[:, half * 128 : half * 128 + 128]

    out_row, in_row = iota((256, 256), 0), iota((256, 256), 1)
    shuffle = one_hot(
        (lax.rem(out_row, 16) // NLAT) * 128 + lax.rem(out_row, NLAT) * 16 + out_row // 16 == in_row
    )
    end_hop(along_lat, send_a, recv_a, 0, NLAT)
    send_b[...] = (
        mm(shuffle[:, :128], recv_a[:, :512]) + mm(shuffle[:, 128:], recv_a[:, 512:])
    ).astype(BF16)
    start_hop(along_lon, send_b, recv_b, 8, NLON)
    recv_b[block(lon)] = send_b[block(lon)]
    end_hop(along_lon, send_b, recv_b, 8, NLON)

    for token in range(2):
        tokens = recv_b[:, token * CH : token * CH + CH]
        rows = slice(token * 256, token * 256 + 256)
        k_ref[rows] = mm(tokens, wk_ref[...]).astype(BF16)
        v_ref[rows] = mm(tokens, wv_ref[...]).astype(BF16)
    kt_ref[...] = k_ref[...].T
    vt_ref[...] = v_ref[...].T

    def head_mask(head):
        return jnp.where(iota((1, CH), 1) // DEPTH == head, 1.0, 0.0).astype(BF16)

    def head_rows(head):
        return pl.ds(aligned(head * DEPTH, DEPTH), DEPTH)

    def attend(head):
        keys = k_ref[...] * head_mask(head)
        for part in range(2):
            cells = slice(part * 256, part * 256 + 256)
            raised = jnp.exp(mm(keys, qt_ref[:, cells]) * SCALE) * live_ref[...]
            weights = raised * (1.0 / jnp.sum(raised, axis=0, keepdims=True))
            probs = weights.astype(BF16)
            probs_ref[head, :, cells] = probs
            ctx_t_ref[head_rows(head), cells] = mm(vt_ref[head_rows(head), :], probs).astype(BF16)

    loop(0, HEADS, attend)

    state = (grid_ref[...].astype(F32) + mm_tn(ctx_t_ref[...], wo_ref[...])).astype(BF16)
    st_ref[0] = state.reshape(ROWS, COLS, CH)

    def halo(index, tile):
        return Halo(
            place,
            tile,
            halo_rows.at[index],
            halo_cols.at[index],
            halo_corners.at[index],
            halo_sems.at[index],
        )

    for layer in range(2):
        edge = halo(layer, st_ref.at[layer])
        edge.start()
        padded = pad_ref.at[layer]
        edge.fill_inner(padded)
        edge.fill_edges(padded)

        def store_mixed(half, chunk, sums):
            for row in range(ROWS):
                inner_ref[half, row, chunk * 16 : chunk * 16 + 16, :] = sums[row]

        correlate(padded, taps_ref, layer, False, store_mixed)

        def mix(row_pair):
            top = aligned(row_pair * 2, 2)
            mixed = jnp.concatenate(
                [inner_ref[0, pl.ds(top, 2)], inner_ref[1, pl.ds(top, 2)]], axis=-1
            ).reshape(128, CH)
            xhat, scale = normalise(mixed)
            rows = pl.ds(aligned(row_pair * 128, 128), 128)
            xhat_ref[layer, rows] = xhat
            rstd_ref[layer, rows] = jnp.broadcast_to(scale, (128, 128))
            normed_low = xhat.astype(BF16)
            nrm_ref[layer, rows] = normed_low
            pre = mm(normed_low, we_ref[layer])
            square = pre * pre
            curve = jnp.tanh(pre * (GELU_0 + GELU_1 * square))
            gate = 0.5 + 0.5 * curve
            wide = (pre * gate).astype(BF16)
            dgelu_ref[layer, rows] = gate + 0.5 * pre * (1.0 - curve * curve) * (
                GELU_0 + 3.0 * GELU_1 * square
            )
            wide_ref[layer, rows] = wide
            before_mix = st_ref[layer, pl.ds(top, 2)].reshape(128, CH).astype(F32)
            after = (before_mix + mm(wide, wr_ref[layer])).astype(BF16)
            if layer == 0:
                st_ref[1, pl.ds(top, 2)] = after.reshape(2, COLS, CH)
            else:
                analysis_ref[rows] = after

        loop(0, 4, mix)

    kgrad_ref[...] = jnp.zeros_like(kgrad_ref)
    reduce_1 = Exchange(place, x_1, half_1, l1_1, part_1, l2_1, out_1, sems_1, BIG)
    reduce_0 = Exchange(place, x_0, half_0, l1_0, part_0, l2_0, out_0, sems_0, BIG)
    reduce_att = Exchange(
        place, x_attention, half_att, l1_att, part_att, l2_att, out_attention, sems_att, BIG
    )
    reduce_k = SmallExchange(place, x_kernels, l1_k, part_k, l2_k, out_kernels, sems_k)

    grad_ref[...] = cot_ref[...].astype(F32)
    for layer in (1, 0):
        sums = x_1 if layer == 1 else x_0

        def unmix(row_pair):
            top = aligned(row_pair * 2, 2)
            rows = pl.ds(aligned(row_pair * 128, 128), 128)
            low = grad_ref[rows].astype(BF16)
            low_ref[rows] = low
            grad_pre = (mm_nt(low, wr_ref[layer]) * dgelu_ref[layer, rows]).astype(BF16)
            gpre_ref[rows] = grad_pre
            grad_norm = mm_nt(grad_pre, we_ref[layer])
            xhat = xhat_ref[layer, rows]
            centred = (
                grad_norm
                - jnp.mean(grad_norm, axis=-1, keepdims=True)
                - xhat * jnp.mean(grad_norm * xhat, axis=-1, keepdims=True)
            )
            grad_mixed = (centred * rstd_ref[layer, rows][:, :1]).astype(BF16)
            gl_ref[layer, pl.ds(top, 2)] = grad_mixed.reshape(2, COLS, CH)

        loop(0, 4, unmix)
        edge = halo(2 + layer, gl_ref.at[layer])
        edge.start()
        if layer == 0:
            reduce_1.start_2()
        edge.fill_inner(pad_back)

        for piece in range(4):
            lanes = slice(piece * 256, piece * 256 + 256)
            rows = slice(piece * 256, piece * 256 + 256)
            sums[rows] = mm_tn(nrm_ref[layer], gpre_ref[:, lanes]).astype(BF16)
            more = slice(1024 + piece * 256, 1280 + piece * 256)
            sums[more] = mm_tn(wide_ref[layer, :, lanes], low_ref[...]).astype(BF16)
        if layer == 1:
            reduce_1.start_0()
        else:
            reduce_1.start_3()
            reduce_0.start_0()

        for half in range(2):
            inner_ref[half] = pad_back[half, 3 : 3 + ROWS, 8 : 8 + COLS, :]
        kernel_grads(pad_ref.at[layer], inner_ref, kgrad_ref, layer)

        edge.fill_edges(pad_back)

        def add_direct(half, chunk, sums):
            for row in range(ROWS):
                inner_ref[half, row, chunk * 16 : chunk * 16 + 16, :] = sums[row]

        correlate(pad_back, taps_ref, layer, True, add_direct)
        for half in range(2):
            lanes = slice(half * 128, half * 128 + 128)
            grad_ref[:, lanes] = grad_ref[:, lanes] + inner_ref[half].reshape(CELLS, 128)
        if layer == 1:
            reduce_1.start_1()

    x_kernels[0:112, 0:128] = kgrad_ref[0].astype(BF16)
    x_kernels[0:112, 128:256] = kgrad_ref[1].astype(BF16)
    x_kernels[112:128] = jnp.zeros((16, CH), BF16)
    reduce_k.start_0()
    reduce_0.start_1()
    reduce_1.start_4()

    def put_attention(index, matrix):
        for half in range(2):
            row = (index * 2 + half) * 256
            x_attention[row : row + 256] = matrix[:, half * 128 : half * 128 + 128].astype(BF16)

    low = grad_ref[...].astype(BF16)
    put_attention(3, mm(ctx_t_ref[...], low))
    gctx = mm_nt(low, wo_ref[...]).astype(BF16)
    gctx_ref[...] = gctx
    gt_ref[...] = gctx.T
    dk_ref[...] = jnp.zeros_like(dk_ref)
    dv_ref[...] = jnp.zeros_like(dv_ref)

    def unattend(head):
        mask = head_mask(head)
        values = v_ref[...] * mask
        for part in range(2):
            cells = slice(part * 256, part * 256 + 256)
            probs = probs_ref[head, :, cells]
            weights = probs.astype(F32)
            grad_probs = mm(values, gt_ref[:, cells])
            mean = jnp.sum(weights * grad_probs, axis=0, keepdims=True)
            grad_scores = (weights * (grad_probs - mean)).astype(BF16)
            dv_ref[...] += mm(probs, gctx_ref[cells] * mask)
            dk_ref[...] += mm(grad_scores, q_ref[cells] * mask)
            dq_t_ref[head_rows(head), cells] = (
                mm(kt_ref[head_rows(head), :], grad_scores) * SCALE
            ).astype(BF16)

    loop(0, HEADS // 2, unattend)
    reduce_1.start_5()
    reduce_0.start_2()
    reduce_k.start_1()
    loop(HEADS // 2, HEADS, unattend)
    reduce_0.start_3()
    reduce_k.start_2()

    grad_keys = (dk_ref[...] * SCALE).astype(BF16)
    grad_values = dv_ref[...].astype(BF16)
    for token in range(2):
        rows = slice(token * 256, token * 256 + 256)
        back_b[:, token * CH : token * CH + CH] = (
            mm_nt(grad_keys[rows], wk_ref[...]) + mm_nt(grad_values[rows], wv_ref[...])
        ).astype(BF16)
    start_hop(along_lon, back_b, got_b, 24, NLON)
    got_b[block(lon)] = back_b[block(lon)]

    put_attention(0, mm(dq_t_ref[...], normed_ref[...]).T)
    for index, grads in ((1, grad_keys), (2, grad_values)):
        put_attention(
            index,
            mm_tn(recv_b[:, :CH], grads[:256]) + mm_tn(recv_b[:, CH:], grads[256:]),
        )
    reduce_att.start_0()
    reduce_0.start_4()

    end_hop(along_lon, back_b, got_b, 24, NLON)
    for c in range(2):
        back_a[:, c * 512 : c * 512 + 512] = mm_tn(
            shuffle[:, c * 128 : c * 128 + 128], got_b[...]
        ).astype(BF16)
    start_hop(along_lat, back_a, got_a, 40, NLAT)
    got_a[block(lat)] = back_a[block(lat)]
    reduce_att.start_1()
    reduce_0.start_5()
    reduce_k.finish()
    end_hop(along_lat, back_a, got_a, 40, NLAT)
    grad_enc_ref[...] = mm_tn(chosen_ref[0], got_a[:, :512]) + mm_tn(chosen_ref[1], got_a[:, 512:])
    reduce_att.start_2()
    reduce_1.finish()
    reduce_att.start_3()
    reduce_0.finish()
    reduce_att.start_4()
    reduce_att.start_5()
    reduce_att.finish()


def fused(*operands):
    vm = pl.BlockSpec(memory_space=pltpu.VMEM)

    def b(*shape):
        return pltpu.VMEM(shape, BF16)

    def f(*shape):
        return pltpu.VMEM(shape, F32)

    def sem(*shape):
        return pltpu.SemaphoreType.DMA(shape)

    scratch = [
        b(2, DEVICES, BLOCKS_DEV),
        b(128, 1024),
        b(128, 1024),
        b(256, 512),
        b(256, 512),
        b(256, 512),
        b(256, 512),
        b(128, 1024),
        b(128, 1024),
        f(SLOTS, 256),
        b(CELLS, CH),
        b(CELLS, CH),
        b(CH, CELLS),
        b(SLOTS, CH),
        b(CH, SLOTS),
        b(SLOTS, CH),
        b(CH, SLOTS),
        b(HEADS, SLOTS, CELLS),
        b(CH, CELLS),
        b(2, ROWS, COLS, CH),
        b(2, ROWS, COLS, CH),
        f(2, 2, PAD_ROWS, PAD_COLS, 128),
        f(2, PAD_ROWS, PAD_COLS, 128),
        f(2, ROWS, COLS, 128),
        f(2, 49, 2, 128),
        f(2, 112, 128),
        f(2, CELLS, CH),
        f(2, CELLS, 128),
        b(2, CELLS, CH),
        b(2, CELLS, WIDE),
        f(2, CELLS, WIDE),
        b(CELLS, WIDE),
        f(CELLS, CH),
        b(CELLS, CH),
        b(CELLS, CH),
        b(CH, CELLS),
        b(CH, CELLS),
        f(SLOTS, CH),
        f(SLOTS, CH),
        b(4, 2, 3, COLS, CH),
        b(4, 2, ROWS, 16, CH),
        b(4, 4, 3, 16, CH),
        b(BIG, 128),
        b(KROWS, CH),
        b(BIG, CH),
        b(BIG, CH),
        b(BIG // 2, 128),
        b(BIG // 2, CH),
        b(BIG // 2, CH),
        b(NLAT, BIG // 16, 128),
        b(NLAT, BIG // 16, CH),
        b(NLAT, BIG // 16, CH),
        b(BIG // 16, 128),
        b(BIG // 16, CH),
        b(BIG // 16, CH),
        b(NYZ, BIG // 128, 128),
        b(NYZ, BIG // 128, CH),
        b(NYZ, BIG // 128, CH),
        b(NLAT, 16, CH),
        b(16, CH),
        b(NLON, 16, CH),
        sem(2, 48),
        sem(4, 2, 8),
        sem(2, 32),
        sem(2, 32),
        sem(2, 32),
        sem(2, 32),
    ]
    return pl.pallas_call(
        kernel,
        out_shape=[
            jax.ShapeDtypeStruct((CELLS, CH), BF16),
            jax.ShapeDtypeStruct((BLOCKS_DEV, 512), F32),
            jax.ShapeDtypeStruct((BIG, 128), BF16),
            jax.ShapeDtypeStruct((KROWS, CH), BF16),
            jax.ShapeDtypeStruct((BIG, CH), BF16),
            jax.ShapeDtypeStruct((BIG, CH), BF16),
        ],
        in_specs=[vm] * len(operands),
        out_specs=[vm] * 6,
        scratch_shapes=scratch,
        compiler_params=pltpu.CompilerParams(
            collective_id=0, has_side_effects=True, vmem_limit_bytes=56 * 1024 * 1024
        ),
        name="assimilate",
    )(*operands)


def local(
    grid_state,
    encodings,
    routes,
    w_query,
    w_key,
    w_value,
    w_out,
    kernels,
    w_expand,
    w_reduce,
    cotangent,
):
    analysis, grad_enc, attention, taps, sums_1, sums_0 = fused(
        grid_state.reshape(CELLS, CH),
        encodings.reshape(BLOCKS_DEV, 2 * CH),
        routes.T.reshape(2, DEVICES, BLOCKS_DEV),
        w_query,
        w_key,
        w_value,
        w_out,
        kernels.transpose(1, 2, 0, 3),
        w_expand,
        w_reduce,
        cotangent.reshape(CELLS, CH),
    )
    attention = attention.astype(F32).reshape(4, 2, CH, 128).transpose(0, 2, 1, 3)
    taps = taps[:112].astype(F32).reshape(2, 56, CH)[:, :49].reshape(2, 7, 7, CH)
    both = jnp.stack([sums_0, sums_1]).astype(F32)
    expand = both[:, :1024].reshape(2, 4, CH, CH).transpose(0, 2, 1, 3).reshape(2, CH, WIDE)
    reduce = both[:, 1024:]
    return (
        analysis.reshape(ROWS, COLS, CH),
        grad_enc.reshape(BLOCKS_DEV, 2, CH),
        attention.reshape(4, CH, CH),
        taps,
        expand,
        reduce,
    )


def solution(mesh):
    in_specs = (
        P("lat", "lon", None),
        P(("lon", "lat"), None, None),
        P(),
        P(),
        P(),
        P(),
        P(),
        P(),
        P(),
        P(),
        P("lat", "lon", None),
    )
    out_specs = (P("lat", "lon", None), P(("lon", "lat"), None, None), P(), P(), P(), P())
    return jax.shard_map(local, mesh=mesh, in_specs=in_specs, out_specs=out_specs, check_vma=False)
```

```python
import functools
import math

import jax
import jax.numpy as jnp
from jax import lax
from jax.experimental import pallas as pl
from jax.experimental.pallas import tpu as pltpu
from jax.sharding import PartitionSpec as P

MESH = pl.DeviceIdType.MESH
F32 = jnp.float32
BF16 = jnp.bfloat16

HEADS = 8
DEPTH = 32
CH = 256
WIDE = 1024
ROWS = 8
COLS = 64
CELLS = ROWS * COLS
NLON = 16
NLAT = 8
NYZ = 8
DEVICES = NLON * NLAT
BLOCKS_DEV = 96
SLOTS = 512
EPSILON = 1e-06
SCALE = 1.0 / math.sqrt(DEPTH)
GELU_0 = math.sqrt(2.0 / math.pi)
GELU_1 = GELU_0 * 0.044715
PAD_ROWS = ROWS + 6
PAD_COLS = 80
BIG = 2048
KROWS = 128


def mm(a, b):
    return jnp.dot(a, b, preferred_element_type=F32)


def mm_nt(a, b):
    return lax.dot_general(a, b, (((1,), (1,)), ((), ())), preferred_element_type=F32)


def mm_tn(a, b):
    return lax.dot_general(a, b, (((0,), (0,)), ((), ())), preferred_element_type=F32)


def loop(low, high, body):
    def step(index, carry):
        body(index)
        return carry

    lax.fori_loop(low, high, step, 0)


def aligned(value, by):
    return pl.multiple_of(value, by)


class Exchange:
    def __init__(
        self, place, lat_first, whole, source, half, level_1, part, level_2, total, sems, rows
    ):
        self.lon, self.lat, self.core, self.yz = place
        self.lat_first, self.whole = lat_first, whole
        self.first, self.second = (self.lat, self.yz) if lat_first else (self.yz, self.lat)
        self.source, self.half, self.level_1 = source, half, level_1
        self.part, self.level_2, self.total = part, level_2, total
        self.sems = sems
        self.r1, self.r2, self.r3 = rows // 2, rows // 16, rows // 128

    def copy(self, src, dst, index, device):
        return pltpu.make_async_remote_copy(
            src_ref=src,
            dst_ref=dst,
            send_sem=self.sems.at[0, index],
            recv_sem=self.sems.at[1, index],
            device_id=device,
            device_id_type=MESH,
        )

    def pair(self):
        return (self.lon + 1 - 2 * self.core, self.lat)

    def device(self, on_lat, position):
        if on_lat:
            return (self.lon, position)
        return (position * 2 + self.core, self.lat)

    def to_first(self, k):
        return lax.rem(self.first + k, 8)

    def from_first(self, k):
        return lax.rem(self.first + 8 - k, 8)

    def to_second(self, k):
        return lax.rem(self.second + k, 8)

    def from_second(self, k):
        return lax.rem(self.second + 8 - k, 8)

    def copy_0(self):
        other = aligned((1 - self.core) * self.r1, self.r1)
        return self.copy(self.source.at[pl.ds(other, self.r1)], self.half, 0, self.pair())

    def start_0(self):
        self.copy_0().start()

    def copy_1(self, k):
        peer = self.to_first(k)
        return self.copy(
            self.half.at[pl.ds(aligned(peer * self.r2, self.r2), self.r2)],
            self.level_1.at[k],
            k,
            self.device(self.lat_first, peer),
        )

    def start_1(self):
        self.copy_0().wait()
        mine = aligned(self.core * self.r1, self.r1)
        step = self.r1 // 4

        def add(i):
            at = aligned(i * step, step)
            self.half[pl.ds(at, step)] = (
                self.half[pl.ds(at, step)].astype(F32)
                + self.source[pl.ds(aligned(mine + at, step), step)].astype(F32)
            ).astype(BF16)

        loop(0, 4, add)
        loop(1, 8, lambda k: self.copy_1(k).start())

    def copy_2(self, k):
        peer = self.to_second(k)
        device = self.device(not self.lat_first, peer)
        if self.whole:
            return self.copy(self.part, self.level_2.at[k], 8 + k, device)
        return self.copy(
            self.part.at[pl.ds(aligned(peer * self.r3, self.r3), self.r3)],
            self.level_2.at[k],
            8 + k,
            device,
        )

    def start_2(self):
        loop(1, 8, lambda k: self.copy_1(k).wait())
        total = self.half[pl.ds(aligned(self.first * self.r2, self.r2), self.r2)].astype(F32)
        for k in range(1, 8):
            total = total + self.level_1[k].astype(F32)
        self.part[...] = total.astype(BF16)
        loop(1, 8, lambda k: self.copy_2(k).start())

    def offset(self, first, second):
        return self.core * self.r1 + first * self.r2 + second * self.r3

    def copy_3(self, k):
        rows = pl.ds(aligned(self.offset(self.first, self.second), self.r3), self.r3)
        device = self.device(not self.lat_first, self.to_second(k))
        return self.copy(self.total.at[rows], self.total.at[rows], 16 + k, device)

    def start_3(self):
        loop(1, 8, lambda k: self.copy_2(k).wait())
        if self.whole:
            self.level_2[0] = self.part[...]
            total = jnp.zeros(self.part.shape, F32)
            for index in range(8):
                total = total + self.level_2[lax.rem(self.second + 8 - index, 8)].astype(F32)
            rows = pl.ds(aligned(self.offset(self.first, 0), self.r2), self.r2)
            self.total[rows] = total.astype(BF16)
            loop(1, 8, lambda k: self.copy_4(k).start())
            return
        total = self.part[pl.ds(aligned(self.second * self.r3, self.r3), self.r3)].astype(F32)
        for k in range(1, 8):
            total = total + self.level_2[k].astype(F32)
        rows = pl.ds(aligned(self.offset(self.first, self.second), self.r3), self.r3)
        self.total[rows] = total.astype(BF16)
        loop(1, 8, lambda k: self.copy_3(k).start())

    def copy_4(self, k):
        rows = pl.ds(aligned(self.offset(self.first, 0), self.r2), self.r2)
        device = self.device(self.lat_first, self.to_first(k))
        return self.copy(self.total.at[rows], self.total.at[rows], 24 + k, device)

    def start_4(self):
        def settle(k):
            self.copy_3(k).wait_send()
            rows = pl.ds(aligned(self.offset(self.first, self.from_second(k)), self.r3), self.r3)
            self.copy(
                self.total.at[rows], self.total.at[rows], 16 + k, (self.lon, self.lat)
            ).wait_recv()

        loop(1, 8, settle)
        loop(1, 8, lambda k: self.copy_4(k).start())

    def copy_5(self):
        rows = pl.ds(aligned(self.core * self.r1, self.r1), self.r1)
        return self.copy(self.total.at[rows], self.total.at[rows], 8, self.pair())

    def start_5(self):
        def settle(k):
            self.copy_4(k).wait_send()
            rows = pl.ds(aligned(self.offset(self.from_first(k), 0), self.r2), self.r2)
            self.copy(
                self.total.at[rows], self.total.at[rows], 24 + k, (self.lon, self.lat)
            ).wait_recv()

        loop(1, 8, settle)
        self.copy_5().start()

    def finish(self):
        self.copy_5().wait_send()
        rows = pl.ds(aligned((1 - self.core) * self.r1, self.r1), self.r1)
        self.copy(
            self.total.at[rows], self.total.at[rows], 8, (self.lon, self.lat)
        ).wait_recv()


class SmallExchange:
    def __init__(self, place, source, level_1, part, level_2, total, sems):
        self.lon, self.lat, self.core, self.yz = place
        self.source, self.level_1, self.part = source, level_1, part
        self.level_2, self.total, self.sems = level_2, total, sems

    def copy(self, src, dst, index, lon, lat):
        return pltpu.make_async_remote_copy(
            src_ref=src,
            dst_ref=dst,
            send_sem=self.sems.at[0, index],
            recv_sem=self.sems.at[1, index],
            device_id=(lon, lat),
            device_id_type=MESH,
        )

    def copy_0(self, k):
        peer = lax.rem(self.lat + k, NLAT)
        return self.copy(
            self.source.at[pl.ds(aligned(peer * 16, 16), 16)], self.level_1.at[k], k, self.lon, peer
        )

    def start_0(self):
        loop(1, NLAT, lambda k: self.copy_0(k).start())

    def copy_1(self, k):
        peer = lax.rem(self.lon + k, NLON)
        return self.copy(self.part.at[...], self.level_2.at[k], 8 + k, peer, self.lat)

    def start_1(self):
        loop(1, NLAT, lambda k: self.copy_0(k).wait())
        total = self.source[pl.ds(aligned(self.lat * 16, 16), 16)].astype(F32)
        for k in range(1, NLAT):
            total = total + self.level_1[k].astype(F32)
        self.part[...] = total.astype(BF16)
        loop(1, NLON, lambda k: self.copy_1(k).start())

    def copy_2(self, k):
        rows = pl.ds(aligned(self.lat * 16, 16), 16)
        peer = lax.rem(self.lat + k, NLAT)
        return self.copy(self.total.at[rows], self.total.at[rows], 24 + k, self.lon, peer)

    def start_2(self):
        loop(1, NLON, lambda k: self.copy_1(k).wait())
        self.level_2[0] = self.part[...]
        total = jnp.zeros((16, CH), F32)
        for index in range(NLON):
            slot = lax.rem(self.lon - index + NLON, NLON)
            total = total + self.level_2[slot].astype(F32)
        self.total[pl.ds(aligned(self.lat * 16, 16), 16)] = total.astype(BF16)
        loop(1, NLAT, lambda k: self.copy_2(k).start())

    def finish(self):
        def settle(k):
            self.copy_2(k).wait_send()
            rows = pl.ds(aligned(lax.rem(self.lat + NLAT - k, NLAT) * 16, 16), 16)
            self.copy(
                self.total.at[rows], self.total.at[rows], 24 + k, self.lon, self.lat
            ).wait_recv()

        loop(1, NLAT, settle)


class Halo:
    def __init__(self, place, tile, packed, rows, cols, corners, sems):
        self.lon, self.lat = place[0], place[1]
        self.tile, self.packed, self.rows = tile, packed, rows
        self.cols, self.corners, self.sems = cols, corners, sems

    def copies(self, wanted=range(8)):
        east, west = lax.rem(self.lon + 1, NLON), lax.rem(self.lon + NLON - 1, NLON)
        south, north = lax.rem(self.lat + 1, NLAT), lax.rem(self.lat + NLAT - 1, NLAT)
        upper, lower = pl.ds(0, 16), pl.ds(16, 16)
        plan = [
            (self.tile.at[pl.ds(0, 3)], self.rows.at[1], self.lon, north),
            (self.tile.at[pl.ds(ROWS - 3, 3)], self.rows.at[0], self.lon, south),
            (self.packed.at[0], self.cols.at[1], west, self.lat),
            (self.packed.at[1], self.cols.at[0], east, self.lat),
            (self.packed.at[0, upper], self.corners.at[3], west, north),
            (self.packed.at[1, upper], self.corners.at[2], east, north),
            (self.packed.at[0, lower], self.corners.at[1], west, south),
            (self.packed.at[1, lower], self.corners.at[0], east, south),
        ]
        return [
            pltpu.make_async_remote_copy(
                src_ref=src,
                dst_ref=dst,
                send_sem=self.sems.at[0, index],
                recv_sem=self.sems.at[1, index],
                device_id=(lon, lat),
                device_id_type=MESH,
            )
            for index, (src, dst, lon, lat) in enumerate(plan)
            if index in wanted
        ]

    def start(self):
        for copy in self.copies((0, 1)):
            copy.start()
        first = [self.tile[row, 0:16, :].astype(F32)[0:4] for row in range(ROWS)]
        last = [self.tile[row, COLS - 16 : COLS, :].astype(F32)[12:16] for row in range(ROWS)]
        self.packed[0] = jnp.concatenate(first, axis=0).astype(BF16)
        self.packed[1] = jnp.concatenate(last, axis=0).astype(BF16)
        for copy in self.copies(range(2, 8)):
            copy.start()

    def fill_inner(self, padded):
        for row in range(ROWS):
            cells = self.tile[row].astype(F32)
            for half in range(2):
                padded[half, 3 + row, 8 : 8 + COLS, :] = cells[:, half * 128 : half * 128 + 128]

    def fill_sides(self, padded):
        for copy in self.copies((2, 3)):
            copy.wait()
        for side, col in ((0, 4), (1, 8 + COLS)):
            cells = self.cols[side].astype(F32)
            for row in range(ROWS):
                for half in range(2):
                    padded[half, 3 + row, col : col + 4, :] = cells[
                        row * 4 : row * 4 + 4, half * 128 : half * 128 + 128
                    ]

    def fill_ends(self, padded):
        for copy in self.copies((0, 1, 4, 5, 6, 7)):
            copy.wait()
        has_north = jnp.where(self.lat > 0, 1.0, 0.0).astype(F32)
        has_south = jnp.where(self.lat < NLAT - 1, 1.0, 0.0).astype(F32)
        for end, there, start, skip in ((0, has_north, 0, 1), (1, has_south, 3 + ROWS, 0)):
            corners = [self.corners[2 * end + side].astype(F32) * there for side in range(2)]
            for row in range(3):
                cells = self.rows[end, row].astype(F32) * there
                at = (row + skip) * 4
                for half in range(2):
                    lanes = slice(half * 128, half * 128 + 128)
                    padded[half, start + row, 8 : 8 + COLS, :] = cells[:, lanes]
                    padded[half, start + row, 4:8, :] = corners[0][at : at + 4, lanes]
                    padded[half, start + row, 8 + COLS : 12 + COLS, :] = corners[1][at : at + 4, lanes]


def correlate(padded, taps, block, flipped, inside, result, chunks):
    def one_half(half):
        for chunk in chunks:
            cols = slice(chunk * 16, chunk * 16 + 16)
            sums = [None if inside else result[half, row, cols, :] for row in range(ROWS)]
            for b in range(7):
                rows = {}
                for a in range(7):
                    tap_id = (6 - a) * 7 + (6 - b) if flipped else a * 7 + b
                    tap = taps[half, tap_id, block : block + 1, :]
                    for row in range(ROWS):
                        if (3 <= row + a < 3 + ROWS) != inside:
                            continue
                        if row + a not in rows:
                            first = chunk * 16 + b + 5
                            rows[row + a] = padded[half, row + a, first : first + 16, :]
                        term = rows[row + a] * tap
                        sums[row] = term if sums[row] is None else sums[row] + term
            for row in range(ROWS):
                if inside or row < 3 or row >= ROWS - 3:
                    result[half, row, cols, :] = sums[row]

    loop(0, 2, one_half)


def kernel_grads(padded, inner, results, block):
    def one_half(half):
        for b in range(7):
            sums = [None] * 7
            for chunk in range(8):
                rows = [
                    padded[half, row, chunk * 8 + b + 5 : chunk * 8 + b + 13, :]
                    for row in range(PAD_ROWS)
                ]
                grads = [
                    inner[half, row, chunk * 8 : chunk * 8 + 8, :] for row in range(ROWS)
                ]
                for a in range(7):
                    for row in range(ROWS):
                        term = rows[row + a] * grads[row]
                        sums[a] = term if sums[a] is None else sums[a] + term
            for a in range(7):
                results[half, pl.ds((a * 7 + b) * 2 + block, 1), :] = jnp.sum(
                    sums[a], axis=0, keepdims=True
                )

    loop(0, 2, one_half)


def iota(shape, dim):
    return lax.broadcasted_iota(jnp.int32, shape, dim)


def one_hot(condition):
    return jnp.where(condition, 1.0, 0.0).astype(BF16)


def normalise(values):
    centred = values - jnp.mean(values, axis=-1, keepdims=True)
    spread = jnp.mean(centred * centred, axis=-1, keepdims=True)
    scale = lax.rsqrt(spread + EPSILON)
    return centred * scale, scale


def kernel(
    grid_hbm,
    enc_hbm,
    routes_hbm,
    wq_hbm,
    wk_hbm,
    wv_hbm,
    wo_hbm,
    kernels_hbm,
    we_hbm,
    wr_hbm,
    cot_hbm,
    analysis_ref,
    grad_enc_ref,
    out_attention,
    out_kernels,
    out_1,
    out_0,
    grid_ref,
    enc_ref,
    routes_ref,
    wq_ref,
    wk_ref,
    wv_ref,
    wo_ref,
    kernels_ref,
    we_ref,
    wr_ref,
    cot_ref,
    load_sems,
    chosen_ref,
    send_a,
    recv_a,
    send_b,
    recv_b,
    back_b,
    got_b,
    back_a,
    got_a,
    live_ref,
    group_ref,
    normed_ref,
    q_ref,
    qt_ref,
    k_ref,
    kt_ref,
    v_ref,
    vt_ref,
    probs_ref,
    ctx_t_ref,
    st_ref,
    gl_ref,
    pad_ref,
    pad_back,
    inner_ref,
    taps_ref,
    kgrad_ref,
    xhat_ref,
    rstd_ref,
    nrm_ref,
    wide_ref,
    dgelu_ref,
    gpre_ref,
    grad_ref,
    low_ref,
    gctx_ref,
    gt_ref,
    dq_t_ref,
    dk_ref,
    dv_ref,
    halo_packed,
    halo_rows,
    halo_cols,
    halo_corners,
    x_attention,
    x_kernels,
    x_1,
    x_0,
    half_att,
    half_1,
    half_0,
    l1_att,
    l1_1,
    l1_0,
    part_att,
    part_1,
    part_0,
    l2_att,
    l2_1,
    l2_0,
    l1_k,
    part_k,
    l2_k,
    a2a_sems,
    halo_sems,
    sems_att,
    sems_1,
    sems_0,
    sems_k,
):
    lon, lat = lax.axis_index("lon"), lax.axis_index("lat")
    core, yz = lax.rem(lon, 2), lon // 2
    place = (lon, lat, core, yz)
    me = lon * NLAT + lat

    pairs = (
        (routes_hbm, routes_ref),
        (enc_hbm, enc_ref),
        (grid_hbm, grid_ref),
        (wq_hbm, wq_ref),
        (kernels_hbm, kernels_ref),
        (wk_hbm, wk_ref),
        (wv_hbm, wv_ref),
        (wo_hbm, wo_ref),
        (we_hbm, we_ref),
        (wr_hbm, wr_ref),
        (cot_hbm, cot_ref),
    )
    loads = [
        pltpu.make_async_copy(source, target, load_sems.at[index])
        for index, (source, target) in enumerate(pairs)
    ]
    for load in loads:
        load.start()

    barrier = pltpu.get_barrier_semaphore()

    def greet(to_lon, to_lat):
        pl.semaphore_signal(barrier, inc=1, device_id=(to_lon, to_lat), device_id_type=MESH)

    loop(1, NLAT, lambda k: greet(lon, lax.rem(lat + k, NLAT)))
    loop(1, NLON, lambda k: greet(lax.rem(lon + k, NLON), lat))
    for dx in (1, NLON - 1):
        for dy in (1, NLAT - 1):
            greet(lax.rem(lon + dx, NLON), lax.rem(lat + dy, NLAT))

    loads[0].wait()
    loads[1].wait()
    chunk = jnp.minimum(me * BLOCKS_DEV // 128, DEVICES * BLOCKS_DEV // 128 - 2)
    shift = me * BLOCKS_DEV - chunk * 128
    window = routes_ref[:, pl.ds(aligned(chunk * 128, 128), 256)].astype(F32).astype(BF16)
    pick = one_hot(iota((256, BLOCKS_DEV), 0) == iota((256, BLOCKS_DEV), 1) + shift)
    own = mm(window, pick).astype(jnp.int32)
    row_id = iota((DEVICES, BLOCKS_DEV), 0)
    tile_id = lax.rem(row_id, NLON) * NLAT + row_id // NLON
    hits = (own[0:1] == tile_id) | (own[1:2] == tile_id)
    before = one_hot(iota((BLOCKS_DEV, BLOCKS_DEV), 0) < iota((BLOCKS_DEV, BLOCKS_DEV), 1))
    hot = one_hot(hits)
    earlier = mm(hot, before)
    tokens_f32 = enc_ref[...].astype(F32)
    for c in range(2):
        chosen = jnp.where(jnp.abs(earlier - c) < 0.5, hot.astype(F32), 0.0).astype(BF16)
        chosen_ref[c] = chosen
        for token in range(2):
            at = c * 512 + token * CH
            send_a[:, at : at + CH] = mm(chosen, tokens_f32[:, token, :].astype(BF16)).astype(BF16)

    pl.semaphore_wait(barrier, NLAT - 1 + NLON - 1 + 4)

    def a2a(src, dst, index, to_lon, to_lat):
        return pltpu.make_async_remote_copy(
            src_ref=src,
            dst_ref=dst,
            send_sem=a2a_sems.at[0, index],
            recv_sem=a2a_sems.at[1, index],
            device_id=(to_lon, to_lat),
            device_id_type=MESH,
        )

    def block(index):
        return pl.ds(aligned(index * 16, 16), 16)

    def along_lat(src, dst, base, k, incoming):
        peer = lax.rem(lat + (NLAT - k if incoming else k), NLAT)
        if incoming:
            return a2a(src.at[block(peer)], dst.at[block(peer)], base + k, lon, lat)
        return a2a(src.at[block(peer)], dst.at[block(lat)], base + k, lon, peer)

    def along_lon(src, dst, base, k, incoming):
        peer = lax.rem(lon + (NLON - k if incoming else k), NLON)
        if incoming:
            return a2a(src.at[block(peer)], dst.at[block(peer)], base + k, lon, lat)
        return a2a(src.at[block(peer)], dst.at[block(lon)], base + k, peer, lat)

    def start_hop(route, src, dst, base, count):
        loop(1, count, lambda k: route(src, dst, base, k, False).start())

    def end_hop(route, src, dst, base, count):
        def settle(k):
            route(src, dst, base, k, False).wait_send()
            route(src, dst, base, k, True).wait_recv()

        loop(1, count, settle)

    start_hop(along_lat, send_a, recv_a, 0, NLAT)
    recv_a[block(lat)] = send_a[block(lat)]

    loads[2].wait()
    loads[3].wait()
    normed = normalise(grid_ref[...].astype(F32))[0].astype(BF16)
    normed_ref[...] = normed
    queries = mm(normed, wq_ref[...]).astype(BF16)
    q_ref[...] = queries
    qt_ref[...] = queries.T
    mine = jnp.sum(jnp.where(routes_ref[...] == me, 1.0, 0.0), axis=0, keepdims=True)
    for group in range(32):
        group_ref[group : group + 1, :] = mine[:, group * 384 : group * 384 + 384]
    fold = one_hot(iota((384, 128), 0) // BLOCKS_DEV == iota((384, 128), 1))
    counts = mm(group_ref[...].astype(BF16), fold).astype(BF16)
    slot = iota((256, 32), 0)
    source = (slot // 16) * NLAT + lax.rem(slot, NLAT)
    spread = mm(one_hot(source // 4 == iota((256, 32), 1)), counts)
    slot = iota((256, 128), 0)
    source = (slot // 16) * NLAT + lax.rem(slot, NLAT)
    count = jnp.sum(
        jnp.where(lax.rem(source, 4) == iota((256, 128), 1), spread, 0.0), axis=1, keepdims=True
    )
    rank = (lax.rem(iota((256, CH), 0), 16) // NLAT).astype(F32)
    live = jnp.where(jnp.broadcast_to(count, (256, CH)) > rank + 0.5, 1.0, 0.0)
    live_ref[0:256] = live
    live_ref[256:512] = live
    loads[4].wait()
    for a in range(7):
        for b in range(7):
            tap = kernels_ref[a, b].astype(F32)
            for half in range(2):
                taps_ref[half, a * 7 + b] = tap[:, half * 128 : half * 128 + 128]

    out_row, in_row = iota((256, 256), 0), iota((256, 256), 1)
    shuffle = one_hot(
        (lax.rem(out_row, 16) // NLAT) * 128 + lax.rem(out_row, NLAT) * 16 + out_row // 16 == in_row
    )
    end_hop(along_lat, send_a, recv_a, 0, NLAT)
    send_b[...] = (
        mm(shuffle[:, :128], recv_a[:, :512]) + mm(shuffle[:, 128:], recv_a[:, 512:])
    ).astype(BF16)
    start_hop(along_lon, send_b, recv_b, 8, NLON)
    recv_b[block(lon)] = send_b[block(lon)]
    end_hop(along_lon, send_b, recv_b, 8, NLON)

    loads[5].wait()
    loads[6].wait()
    for token in range(2):
        tokens = recv_b[:, token * CH : token * CH + CH]
        rows = slice(token * 256, token * 256 + 256)
        k_ref[rows] = mm(tokens, wk_ref[...]).astype(BF16)
        v_ref[rows] = mm(tokens, wv_ref[...]).astype(BF16)
    kt_ref[...] = k_ref[...].T
    vt_ref[...] = v_ref[...].T

    def head_mask(head):
        return jnp.where(iota((1, CH), 1) // DEPTH == head, 1.0, 0.0).astype(BF16)

    def head_rows(head):
        return pl.ds(aligned(head * DEPTH, DEPTH), DEPTH)

    def attend(head):
        keys = k_ref[...] * head_mask(head)
        for part in range(2):
            cells = slice(part * 256, part * 256 + 256)
            raised = jnp.exp(mm(keys, qt_ref[:, cells]) * SCALE) * live_ref[...]
            weights = raised * (1.0 / jnp.sum(raised, axis=0, keepdims=True))
            probs = weights.astype(BF16)
            probs_ref[head, :, cells] = probs
            ctx_t_ref[head_rows(head), cells] = mm(vt_ref[head_rows(head), :], probs).astype(BF16)

    loop(0, HEADS, attend)

    for load in loads[7:]:
        load.wait()
    state = (grid_ref[...].astype(F32) + mm_tn(ctx_t_ref[...], wo_ref[...])).astype(BF16)
    st_ref[0] = state.reshape(ROWS, COLS, CH)

    def halo(index, tile):
        return Halo(
            place,
            tile,
            halo_packed.at[index],
            halo_rows.at[index],
            halo_cols.at[index],
            halo_corners.at[index],
            halo_sems.at[index],
        )

    for layer in range(2):
        edge = halo(layer, st_ref.at[layer])
        edge.start()
        padded = pad_ref.at[layer]
        edge.fill_inner(padded)

        correlate(padded, taps_ref, layer, False, True, inner_ref, (1, 2))
        edge.fill_sides(padded)
        correlate(padded, taps_ref, layer, False, True, inner_ref, (0, 3))
        edge.fill_ends(padded)
        correlate(padded, taps_ref, layer, False, False, inner_ref, range(4))

        def mix(row_pair):
            top = aligned(row_pair * 2, 2)
            mixed = jnp.concatenate(
                [inner_ref[0, pl.ds(top, 2)], inner_ref[1, pl.ds(top, 2)]], axis=-1
            ).reshape(128, CH)
            xhat, scale = normalise(mixed)
            rows = pl.ds(aligned(row_pair * 128, 128), 128)
            xhat_ref[layer, rows] = xhat
            rstd_ref[layer, rows] = jnp.broadcast_to(scale, (128, 128))
            normed_low = xhat.astype(BF16)
            nrm_ref[layer, rows] = normed_low
            pre = mm(normed_low, we_ref[layer])
            square = pre * pre
            curve = jnp.tanh(pre * (GELU_0 + GELU_1 * square))
            gate = 0.5 + 0.5 * curve
            wide = (pre * gate).astype(BF16)
            dgelu_ref[layer, rows] = gate + 0.5 * pre * (1.0 - curve * curve) * (
                GELU_0 + 3.0 * GELU_1 * square
            )
            wide_ref[layer, rows] = wide
            before_mix = st_ref[layer, pl.ds(top, 2)].reshape(128, CH).astype(F32)
            after = (before_mix + mm(wide, wr_ref[layer])).astype(BF16)
            if layer == 0:
                st_ref[1, pl.ds(top, 2)] = after.reshape(2, COLS, CH)
            else:
                analysis_ref[rows] = after

        loop(0, 4, mix)

    kgrad_ref[...] = jnp.zeros_like(kgrad_ref)
    reduce_1 = Exchange(
        place, True, False, x_1, half_1, l1_1, part_1, l2_1, out_1, sems_1, BIG
    )
    reduce_0 = Exchange(
        place, False, False, x_0, half_0, l1_0, part_0, l2_0, out_0, sems_0, BIG
    )
    reduce_att = Exchange(
        place, True, True, x_attention, half_att, l1_att, part_att, l2_att, out_attention, sems_att, BIG
    )
    reduce_k = SmallExchange(place, x_kernels, l1_k, part_k, l2_k, out_kernels, sems_k)

    grad_ref[...] = cot_ref[...].astype(F32)
    for layer in (1, 0):
        sums = x_1 if layer == 1 else x_0

        def unmix(row_pair):
            top = aligned(row_pair * 2, 2)
            rows = pl.ds(aligned(row_pair * 128, 128), 128)
            low = grad_ref[rows].astype(BF16)
            low_ref[rows] = low
            grad_pre = (mm_nt(low, wr_ref[layer]) * dgelu_ref[layer, rows]).astype(BF16)
            gpre_ref[rows] = grad_pre
            grad_norm = mm_nt(grad_pre, we_ref[layer])
            xhat = xhat_ref[layer, rows]
            centred = (
                grad_norm
                - jnp.mean(grad_norm, axis=-1, keepdims=True)
                - xhat * jnp.mean(grad_norm * xhat, axis=-1, keepdims=True)
            )
            grad_mixed = (centred * rstd_ref[layer, rows][:, :1]).astype(BF16)
            gl_ref[layer, pl.ds(top, 2)] = grad_mixed.reshape(2, COLS, CH)

        loop(0, 4, unmix)
        edge = halo(2 + layer, gl_ref.at[layer])
        edge.start()
        edge.fill_inner(pad_back)

        for piece in range(4):
            lanes = slice(piece * 256, piece * 256 + 256)
            rows = slice(piece * 256, piece * 256 + 256)
            sums[rows] = mm_tn(nrm_ref[layer], gpre_ref[:, lanes]).astype(BF16)
            more = slice(1024 + piece * 256, 1280 + piece * 256)
            sums[more] = mm_tn(wide_ref[layer, :, lanes], low_ref[...]).astype(BF16)
        if layer == 1:
            reduce_1.start_0()
        else:
            reduce_0.start_0()
            reduce_1.start_2()

        for half in range(2):
            inner_ref[half] = pad_back[half, 3 : 3 + ROWS, 8 : 8 + COLS, :]
        kernel_grads(pad_ref.at[layer], inner_ref, kgrad_ref, layer)
        if layer == 1:
            reduce_1.start_1()
        else:
            reduce_0.start_1()

        correlate(pad_back, taps_ref, layer, True, True, inner_ref, (1, 2))
        edge.fill_sides(pad_back)
        correlate(pad_back, taps_ref, layer, True, True, inner_ref, (0, 3))
        edge.fill_ends(pad_back)
        correlate(pad_back, taps_ref, layer, True, False, inner_ref, range(4))
        for half in range(2):
            lanes = slice(half * 128, half * 128 + 128)
            grad_ref[:, lanes] = grad_ref[:, lanes] + inner_ref[half].reshape(CELLS, 128)

    x_kernels[0:112, 0:128] = kgrad_ref[0].astype(BF16)
    x_kernels[0:112, 128:256] = kgrad_ref[1].astype(BF16)
    x_kernels[112:128] = jnp.zeros((16, CH), BF16)
    reduce_k.start_0()
    reduce_1.start_3()

    def put_attention(index, matrix):
        for half in range(2):
            row = (index * 2 + half) * 256
            x_attention[row : row + 256] = matrix[:, half * 128 : half * 128 + 128].astype(BF16)

    low = grad_ref[...].astype(BF16)
    put_attention(3, mm(ctx_t_ref[...], low))
    gctx = mm_nt(low, wo_ref[...]).astype(BF16)
    gctx_ref[...] = gctx
    gt_ref[...] = gctx.T
    dk_ref[...] = jnp.zeros_like(dk_ref)
    dv_ref[...] = jnp.zeros_like(dv_ref)

    def unattend(head):
        mask = head_mask(head)
        values = v_ref[...] * mask
        for part in range(2):
            cells = slice(part * 256, part * 256 + 256)
            probs = probs_ref[head, :, cells]
            weights = probs.astype(F32)
            grad_probs = mm(values, gt_ref[:, cells])
            mean = jnp.sum(weights * grad_probs, axis=0, keepdims=True)
            grad_scores = (weights * (grad_probs - mean)).astype(BF16)
            dv_ref[...] += mm(probs, gctx_ref[cells] * mask)
            dk_ref[...] += mm(grad_scores, q_ref[cells] * mask)
            dq_t_ref[head_rows(head), cells] = (
                mm(kt_ref[head_rows(head), :], grad_scores) * SCALE
            ).astype(BF16)

    loop(0, 4, unattend)
    reduce_k.start_1()
    reduce_1.start_4()
    reduce_0.start_2()
    loop(4, HEADS, unattend)
    reduce_0.start_3()

    grad_keys = (dk_ref[...] * SCALE).astype(BF16)
    grad_values = dv_ref[...].astype(BF16)
    for token in range(2):
        rows = slice(token * 256, token * 256 + 256)
        back_b[:, token * CH : token * CH + CH] = (
            mm_nt(grad_keys[rows], wk_ref[...]) + mm_nt(grad_values[rows], wv_ref[...])
        ).astype(BF16)
    start_hop(along_lon, back_b, got_b, 24, NLON)
    got_b[block(lon)] = back_b[block(lon)]

    put_attention(0, mm(dq_t_ref[...], normed_ref[...]).T)
    for index, grads in ((1, grad_keys), (2, grad_values)):
        put_attention(
            index,
            mm_tn(recv_b[:, :CH], grads[:256]) + mm_tn(recv_b[:, CH:], grads[256:]),
        )
    reduce_att.start_0()
    reduce_k.start_2()
    reduce_att.start_1()
    reduce_1.start_5()
    reduce_0.start_4()

    end_hop(along_lon, back_b, got_b, 24, NLON)
    for c in range(2):
        back_a[:, c * 512 : c * 512 + 512] = mm_tn(
            shuffle[:, c * 128 : c * 128 + 128], got_b[...]
        ).astype(BF16)
    start_hop(along_lat, back_a, got_a, 40, NLAT)
    got_a[block(lat)] = back_a[block(lat)]
    reduce_att.start_2()
    end_hop(along_lat, back_a, got_a, 40, NLAT)
    grad_enc_ref[...] = mm_tn(chosen_ref[0], got_a[:, :512]) + mm_tn(chosen_ref[1], got_a[:, 512:])
    reduce_1.finish()
    reduce_k.finish()
    reduce_att.start_3()
    reduce_0.start_5()
    reduce_att.start_5()
    reduce_0.finish()
    reduce_att.finish()


def fused(*operands):
    vm = pl.BlockSpec(memory_space=pltpu.VMEM)

    def b(*shape):
        return pltpu.VMEM(shape, BF16)

    def f(*shape):
        return pltpu.VMEM(shape, F32)

    def sem(*shape):
        return pltpu.SemaphoreType.DMA(shape)

    loaded = [pltpu.VMEM(operand.shape, operand.dtype) for operand in operands]
    scratch = loaded + [
        sem(len(operands)),
        b(2, DEVICES, BLOCKS_DEV),
        b(128, 1024),
        b(128, 1024),
        b(256, 512),
        b(256, 512),
        b(256, 512),
        b(256, 512),
        b(128, 1024),
        b(128, 1024),
        f(SLOTS, 256),
        f(32, 384),
        b(CELLS, CH),
        b(CELLS, CH),
        b(CH, CELLS),
        b(SLOTS, CH),
        b(CH, SLOTS),
        b(SLOTS, CH),
        b(CH, SLOTS),
        b(HEADS, SLOTS, CELLS),
        b(CH, CELLS),
        b(2, ROWS, COLS, CH),
        b(2, ROWS, COLS, CH),
        f(2, 2, PAD_ROWS, PAD_COLS, 128),
        f(2, PAD_ROWS, PAD_COLS, 128),
        f(2, ROWS, COLS, 128),
        f(2, 49, 2, 128),
        f(2, 112, 128),
        f(2, CELLS, CH),
        f(2, CELLS, 128),
        b(2, CELLS, CH),
        b(2, CELLS, WIDE),
        f(2, CELLS, WIDE),
        b(CELLS, WIDE),
        f(CELLS, CH),
        b(CELLS, CH),
        b(CELLS, CH),
        b(CH, CELLS),
        b(CH, CELLS),
        f(SLOTS, CH),
        f(SLOTS, CH),
        b(4, 2, 32, CH),
        b(4, 2, 3, COLS, CH),
        b(4, 2, 32, CH),
        b(4, 4, 16, CH),
        b(BIG, 128),
        b(KROWS, CH),
        b(BIG, CH),
        b(BIG, CH),
        b(BIG // 2, 128),
        b(BIG // 2, CH),
        b(BIG // 2, CH),
        b(NLAT, BIG // 16, 128),
        b(NLAT, BIG // 16, CH),
        b(NLAT, BIG // 16, CH),
        b(BIG // 16, 128),
        b(BIG // 16, CH),
        b(BIG // 16, CH),
        b(NYZ, BIG // 16, 128),
        b(NYZ, BIG // 128, CH),
        b(NYZ, BIG // 128, CH),
        b(NLAT, 16, CH),
        b(16, CH),
        b(NLON, 16, CH),
        sem(2, 48),
        sem(4, 2, 8),
        sem(2, 32),
        sem(2, 32),
        sem(2, 32),
        sem(2, 32),
    ]
    return pl.pallas_call(
        kernel,
        out_shape=[
            jax.ShapeDtypeStruct((CELLS, CH), BF16),
            jax.ShapeDtypeStruct((BLOCKS_DEV, 512), F32),
            jax.ShapeDtypeStruct((BIG, 128), BF16),
            jax.ShapeDtypeStruct((KROWS, CH), BF16),
            jax.ShapeDtypeStruct((BIG, CH), BF16),
            jax.ShapeDtypeStruct((BIG, CH), BF16),
        ],
        in_specs=[pl.BlockSpec(memory_space=pltpu.HBM)] * len(operands),
        out_specs=[vm] * 6,
        scratch_shapes=scratch,
        compiler_params=pltpu.CompilerParams(
            collective_id=0, has_side_effects=True, vmem_limit_bytes=56 * 1024 * 1024
        ),
        name="assimilate",
    )(*operands)


def finishing(
    analysis_ref,
    grad_enc_ref,
    attention_ref,
    taps_ref,
    sums_1,
    sums_0,
    out_analysis,
    out_enc,
    out_attention,
    out_taps,
    out_expand,
    out_reduce,
    taps_f32,
):
    out_analysis[...] = analysis_ref[...]
    for token in range(2):
        out_enc[:, token, :] = grad_enc_ref[:, token * CH : token * CH + CH]
    for index in range(4):
        for half in range(2):
            row = (index * 2 + half) * 256
            out_attention[index, :, half * 128 : half * 128 + 128] = attention_ref[
                row : row + 256
            ].astype(F32)
    taps_f32[...] = taps_ref[...].astype(F32)
    for a in range(7):
        for b in range(7):
            row = (a * 7 + b) * 2
            out_taps[a, b] = taps_f32[row : row + 2]
    for layer, sums in enumerate((sums_0, sums_1)):
        for piece in range(4):
            rows = slice(piece * 256, piece * 256 + 256)
            out_expand[layer, :, rows] = sums[rows].astype(F32)
        out_reduce[layer] = sums[1024:].astype(F32)


def finished(*operands):
    vm = pl.BlockSpec(memory_space=pltpu.VMEM)
    return pl.pallas_call(
        finishing,
        out_shape=[
            jax.ShapeDtypeStruct((CELLS, CH), BF16),
            jax.ShapeDtypeStruct((BLOCKS_DEV, 2, CH), F32),
            jax.ShapeDtypeStruct((4, CH, CH), F32),
            jax.ShapeDtypeStruct((7, 7, 2, CH), F32),
            jax.ShapeDtypeStruct((2, CH, WIDE), F32),
            jax.ShapeDtypeStruct((2, WIDE, CH), F32),
        ],
        in_specs=[vm] * 6,
        out_specs=[vm] * 6,
        scratch_shapes=[pltpu.VMEM((KROWS, CH), F32)],
        compiler_params=pltpu.CompilerParams(vmem_limit_bytes=56 * 1024 * 1024),
        name="finish",
    )(*operands)


def local(
    grid_state,
    encodings,
    routes,
    w_query,
    w_key,
    w_value,
    w_out,
    kernels,
    w_expand,
    w_reduce,
    cotangent,
):
    results = fused(
        grid_state.reshape(CELLS, CH),
        encodings,
        routes.T,
        w_query,
        w_key,
        w_value,
        w_out,
        kernels.transpose(1, 2, 0, 3),
        w_expand,
        w_reduce,
        cotangent.reshape(CELLS, CH),
    )
    analysis, grad_enc, attention, taps, expand, reduce = finished(*results)
    return (
        analysis.reshape(ROWS, COLS, CH),
        grad_enc,
        attention,
        taps.transpose(2, 0, 1, 3),
        expand,
        reduce,
    )


def solution(mesh):
    in_specs = (
        P("lat", "lon", None),
        P(("lon", "lat"), None, None),
        P(),
        P(),
        P(),
        P(),
        P(),
        P(),
        P(),
        P(),
        P("lat", "lon", None),
    )
    out_specs = (P("lat", "lon", None), P(("lon", "lat"), None, None), P(), P(), P(), P())
    return jax.shard_map(local, mesh=mesh, in_specs=in_specs, out_specs=out_specs, check_vma=False)
```

```python
import functools
import math

import jax
import jax.numpy as jnp
from jax import lax
from jax.experimental import pallas as pl
from jax.experimental.pallas import tpu as pltpu
from jax.sharding import PartitionSpec as P

MESH = pl.DeviceIdType.MESH
F32 = jnp.float32
BF16 = jnp.bfloat16

HEADS = 8
DEPTH = 32
CH = 256
WIDE = 1024
ROWS = 8
COLS = 64
CELLS = ROWS * COLS
NLON = 16
NLAT = 8
NYZ = 8
DEVICES = NLON * NLAT
BLOCKS_DEV = 96
SLOTS = 512
EPSILON = 1e-06
SCALE = 1.0 / math.sqrt(DEPTH)
LOG2_E = math.log2(math.e)
GELU_0 = math.sqrt(2.0 / math.pi)
GELU_1 = GELU_0 * 0.044715
PAD_ROWS = ROWS + 6
PAD_COLS = 80
BIG = 2048
ATT = BIG + 256


def mm(a, b):
    return jnp.dot(a, b, preferred_element_type=F32)


def mm_nt(a, b):
    return lax.dot_general(a, b, (((1,), (1,)), ((), ())), preferred_element_type=F32)


def mm_tn(a, b):
    return lax.dot_general(a, b, (((0,), (0,)), ((), ())), preferred_element_type=F32)


def loop(low, high, body):
    def step(index, carry):
        body(index)
        return carry

    lax.fori_loop(low, high, step, 0)


def aligned(value, by):
    return pl.multiple_of(value, by)


class Exchange:
    def __init__(
        self, place, lat_first, whole, source, half, level_1, part, level_2, total, sems, rows
    ):
        self.lon, self.lat, self.core, self.yz = place
        self.lat_first, self.whole = lat_first, whole
        self.first, self.second = (self.lat, self.yz) if lat_first else (self.yz, self.lat)
        self.source, self.half, self.level_1 = source, half, level_1
        self.part, self.level_2, self.total = part, level_2, total
        self.sems = sems
        self.r1, self.r2, self.r3 = rows // 2, rows // 16, rows // 128

    def copy(self, src, dst, index, device):
        return pltpu.make_async_remote_copy(
            src_ref=src,
            dst_ref=dst,
            send_sem=self.sems.at[0, index],
            recv_sem=self.sems.at[1, index],
            device_id=device,
            device_id_type=MESH,
        )

    def settle(self, phase, sent, arrived):
        self.copy(sent, sent, phase, (self.lon, self.lat)).wait_send()
        self.copy(arrived, arrived, phase, (self.lon, self.lat)).wait_recv()

    def pair(self):
        return (self.lon + 1 - 2 * self.core, self.lat)

    def device(self, on_lat, position):
        if on_lat:
            return (self.lon, position)
        return (position * 2 + self.core, self.lat)

    def to_first(self, k):
        return lax.rem(self.first + k, 8)

    def from_first(self, k):
        return lax.rem(self.first + 8 - k, 8)

    def to_second(self, k):
        return lax.rem(self.second + k, 8)

    def from_second(self, k):
        return lax.rem(self.second + 8 - k, 8)

    def copy_0(self):
        other = aligned((1 - self.core) * self.r1, self.r1)
        return self.copy(self.source.at[pl.ds(other, self.r1)], self.half, 0, self.pair())

    def start_0(self):
        self.copy_0().start()

    def copy_1(self, k):
        peer = self.to_first(k)
        return self.copy(
            self.half.at[pl.ds(aligned(peer * self.r2, self.r2), self.r2)],
            self.level_1.at[k],
            1,
            self.device(self.lat_first, peer),
        )

    def start_1(self):
        self.copy_0().wait()
        mine = aligned(self.core * self.r1, self.r1)
        step = self.r1 // 4

        def add(i):
            at = aligned(i * step, step)
            self.half[pl.ds(at, step)] = (
                self.half[pl.ds(at, step)].astype(F32)
                + self.source[pl.ds(aligned(mine + at, step), step)].astype(F32)
            ).astype(BF16)

        loop(0, 4, add)
        loop(1, 8, lambda k: self.copy_1(k).start())

    def copy_2(self, k):
        peer = self.to_second(k)
        device = self.device(not self.lat_first, peer)
        if self.whole:
            return self.copy(self.part, self.level_2.at[k], 2, device)
        return self.copy(
            self.part.at[pl.ds(aligned(peer * self.r3, self.r3), self.r3)],
            self.level_2.at[k],
            2,
            device,
        )

    def start_2(self):
        self.settle(1, self.half.at[pl.ds(0, 7 * self.r2)], self.level_1.at[pl.ds(1, 7)])
        total = self.half[pl.ds(aligned(self.first * self.r2, self.r2), self.r2)].astype(F32)
        for k in range(1, 8):
            total = total + self.level_1[k].astype(F32)
        self.part[...] = total.astype(BF16)
        loop(1, 8, lambda k: self.copy_2(k).start())

    def offset(self, first, second):
        return self.core * self.r1 + first * self.r2 + second * self.r3

    def copy_3(self, k):
        rows = pl.ds(aligned(self.offset(self.first, self.second), self.r3), self.r3)
        device = self.device(not self.lat_first, self.to_second(k))
        return self.copy(self.total.at[rows], self.total.at[rows], 3, device)

    def start_3(self):
        sent = self.half.at[pl.ds(0, 7 * self.r2)] if self.whole else self.part.at[pl.ds(0, 7 * self.r3)]
        self.settle(2, sent, self.level_2.at[pl.ds(1, 7)])
        if self.whole:
            self.level_2[0] = self.part[...]
            total = jnp.zeros(self.part.shape, F32)
            for index in range(8):
                total = total + self.level_2[lax.rem(self.second + 8 - index, 8)].astype(F32)
            rows = pl.ds(aligned(self.offset(self.first, 0), self.r2), self.r2)
            self.total[rows] = total.astype(BF16)
            loop(1, 8, lambda k: self.copy_4(k).start())
            return
        total = self.part[pl.ds(aligned(self.second * self.r3, self.r3), self.r3)].astype(F32)
        for k in range(1, 8):
            total = total + self.level_2[k].astype(F32)
        rows = pl.ds(aligned(self.offset(self.first, self.second), self.r3), self.r3)
        self.total[rows] = total.astype(BF16)
        loop(1, 8, lambda k: self.copy_3(k).start())

    def copy_4(self, k):
        rows = pl.ds(aligned(self.offset(self.first, 0), self.r2), self.r2)
        device = self.device(self.lat_first, self.to_first(k))
        return self.copy(self.total.at[rows], self.total.at[rows], 4, device)

    def start_4(self):
        rows = self.total.at[pl.ds(0, 7 * self.r3)]
        self.settle(3, rows, rows)
        loop(1, 8, lambda k: self.copy_4(k).start())

    def copy_5(self):
        rows = pl.ds(aligned(self.core * self.r1, self.r1), self.r1)
        return self.copy(self.total.at[rows], self.total.at[rows], 5, self.pair())

    def start_5(self):
        rows = self.total.at[pl.ds(0, 7 * self.r2)]
        self.settle(4, rows, rows)
        self.copy_5().start()

    def finish(self):
        rows = self.total.at[pl.ds(0, self.r1)]
        self.settle(5, rows, rows)


class Halo:
    def __init__(self, place, tile, packed, rows, cols, corners, sems):
        self.lon, self.lat = place[0], place[1]
        self.tile, self.packed, self.rows = tile, packed, rows
        self.cols, self.corners, self.sems = cols, corners, sems

    def copies(self, wanted=range(8)):
        east, west = lax.rem(self.lon + 1, NLON), lax.rem(self.lon + NLON - 1, NLON)
        south, north = lax.rem(self.lat + 1, NLAT), lax.rem(self.lat + NLAT - 1, NLAT)
        upper, lower = pl.ds(0, 16), pl.ds(16, 16)
        plan = [
            (self.tile.at[pl.ds(0, 3)], self.rows.at[1], self.lon, north),
            (self.tile.at[pl.ds(ROWS - 3, 3)], self.rows.at[0], self.lon, south),
            (self.packed.at[0], self.cols.at[1], west, self.lat),
            (self.packed.at[1], self.cols.at[0], east, self.lat),
            (self.packed.at[0, upper], self.corners.at[3], west, north),
            (self.packed.at[1, upper], self.corners.at[2], east, north),
            (self.packed.at[0, lower], self.corners.at[1], west, south),
            (self.packed.at[1, lower], self.corners.at[0], east, south),
        ]
        return [
            pltpu.make_async_remote_copy(
                src_ref=src,
                dst_ref=dst,
                send_sem=self.sems.at[0, (0, 0, 1, 1, 2, 2, 2, 2)[index]],
                recv_sem=self.sems.at[1, (0, 0, 1, 1, 2, 2, 2, 2)[index]],
                device_id=(lon, lat),
                device_id_type=MESH,
            )
            for index, (src, dst, lon, lat) in enumerate(plan)
            if index in wanted
        ]

    def settle(self, kind):
        buffer = (self.rows, self.cols, self.corners)[kind]
        copy = pltpu.make_async_remote_copy(
            src_ref=buffer,
            dst_ref=buffer,
            send_sem=self.sems.at[0, kind],
            recv_sem=self.sems.at[1, kind],
            device_id=(self.lon, self.lat),
            device_id_type=MESH,
        )
        copy.wait_send()
        copy.wait_recv()

    def start(self):
        for copy in self.copies((0, 1)):
            copy.start()
        first = [self.tile[row, 0:16, :].astype(F32)[0:4] for row in range(ROWS)]
        last = [self.tile[row, COLS - 16 : COLS, :].astype(F32)[12:16] for row in range(ROWS)]
        self.packed[0] = jnp.concatenate(first, axis=0).astype(BF16)
        self.packed[1] = jnp.concatenate(last, axis=0).astype(BF16)
        for copy in self.copies(range(2, 8)):
            copy.start()

    def fill_inner(self, padded):
        for row in range(ROWS):
            cells = self.tile[row].astype(F32)
            for half in range(2):
                padded[half, 3 + row, 8 : 8 + COLS, :] = cells[:, half * 128 : half * 128 + 128]

    def fill_sides(self, padded):
        self.settle(1)
        for side, col in ((0, 4), (1, 8 + COLS)):
            cells = self.cols[side].astype(F32)
            for row in range(ROWS):
                for half in range(2):
                    padded[half, 3 + row, col : col + 4, :] = cells[
                        row * 4 : row * 4 + 4, half * 128 : half * 128 + 128
                    ]

    def fill_ends(self, padded):
        self.settle(0)
        self.settle(2)
        has_north = jnp.where(self.lat > 0, 1.0, 0.0).astype(F32)
        has_south = jnp.where(self.lat < NLAT - 1, 1.0, 0.0).astype(F32)
        for end, there, start, skip in ((0, has_north, 0, 1), (1, has_south, 3 + ROWS, 0)):
            corners = [self.corners[2 * end + side].astype(F32) * there for side in range(2)]
            for row in range(3):
                cells = self.rows[end, row].astype(F32) * there
                at = (row + skip) * 4
                for half in range(2):
                    lanes = slice(half * 128, half * 128 + 128)
                    padded[half, start + row, 8 : 8 + COLS, :] = cells[:, lanes]
                    padded[half, start + row, 4:8, :] = corners[0][at : at + 4, lanes]
                    padded[half, start + row, 8 + COLS : 12 + COLS, :] = corners[1][at : at + 4, lanes]


def correlate(padded, taps, block, flipped, inside, result, chunks):
    def one_half(half):
        for chunk in chunks:
            cols = slice(chunk * 16, chunk * 16 + 16)
            sums = [None if inside else result[half, row, cols, :] for row in range(ROWS)]
            for b in range(7):
                rows = {}
                for a in range(7):
                    tap_id = (6 - a) * 7 + (6 - b) if flipped else a * 7 + b
                    tap = taps[half, tap_id, block : block + 1, :]
                    for row in range(ROWS):
                        if (3 <= row + a < 3 + ROWS) != inside:
                            continue
                        if row + a not in rows:
                            first = chunk * 16 + b + 5
                            rows[row + a] = padded[half, row + a, first : first + 16, :]
                        term = rows[row + a] * tap
                        sums[row] = term if sums[row] is None else sums[row] + term
            for row in range(ROWS):
                if inside or row < 3 or row >= ROWS - 3:
                    result[half, row, cols, :] = sums[row]

    loop(0, 2, one_half)


def kernel_grads(padded, inner, results, block):
    def one_half(half):
        for b in range(7):
            sums = [None] * 7
            for chunk in range(8):
                rows = [
                    padded[half, row, chunk * 8 + b + 5 : chunk * 8 + b + 13, :]
                    for row in range(PAD_ROWS)
                ]
                grads = [
                    inner[half, row, chunk * 8 : chunk * 8 + 8, :] for row in range(ROWS)
                ]
                for a in range(7):
                    for row in range(ROWS):
                        term = rows[row + a] * grads[row]
                        sums[a] = term if sums[a] is None else sums[a] + term
            for a in range(7):
                results[half, pl.ds((a * 7 + b) * 2 + block, 1), :] = jnp.sum(
                    sums[a], axis=0, keepdims=True
                )

    loop(0, 2, one_half)


def iota(shape, dim):
    return lax.broadcasted_iota(jnp.int32, shape, dim)


def one_hot(condition):
    return jnp.where(condition, 1.0, 0.0).astype(BF16)


def normalise(values):
    centred = values - jnp.mean(values, axis=-1, keepdims=True)
    spread = jnp.mean(centred * centred, axis=-1, keepdims=True)
    scale = lax.rsqrt(spread + EPSILON)
    return centred * scale, scale


def kernel(
    grid_hbm,
    enc_hbm,
    routes_hbm,
    wq_hbm,
    wk_hbm,
    wv_hbm,
    wo_hbm,
    kernels_hbm,
    we_hbm,
    wr_hbm,
    cot_hbm,
    analysis_hbm,
    grad_enc_hbm,
    attention_hbm,
    sums_1_hbm,
    sums_0_hbm,
    grid_ref,
    enc_ref,
    routes_ref,
    wq_ref,
    wk_ref,
    wv_ref,
    wo_ref,
    kernels_ref,
    we_ref,
    wr_ref,
    cot_ref,
    load_sems,
    analysis_ref,
    grad_enc_ref,
    out_attention,
    out_1,
    out_0,
    store_sems,
    chosen_ref,
    send_a,
    recv_a,
    send_b,
    recv_b,
    back_b,
    got_b,
    back_a,
    got_a,
    dead_ref,
    group_ref,
    normed_ref,
    qt_ref,
    qt_one_ref,
    k_ref,
    kt_ref,
    v_ref,
    vt_ref,
    probs_ref,
    ctx_t_ref,
    st_ref,
    gl_ref,
    pad_ref,
    pad_back,
    inner_ref,
    taps_ref,
    kgrad_ref,
    xhat_ref,
    rstd_ref,
    nrm_ref,
    wide_ref,
    dgelu_ref,
    gpre_ref,
    grad_ref,
    low_ref,
    gt_ref,
    dq_t_ref,
    dk_t_ref,
    dv_t_ref,
    scores_ref,
    halo_packed,
    halo_rows,
    halo_cols,
    halo_corners,
    x_attention,
    x_1,
    x_0,
    half_att,
    half_1,
    half_0,
    l1_att,
    l1_1,
    l1_0,
    part_att,
    part_1,
    part_0,
    l2_att,
    l2_1,
    l2_0,
    a2a_sems,
    halo_sems,
    sems_att,
    sems_1,
    sems_0,
):
    lon, lat = lax.axis_index("lon"), lax.axis_index("lat")
    core, yz = lax.rem(lon, 2), lon // 2
    place = (lon, lat, core, yz)
    me = lon * NLAT + lat

    pairs = (
        (routes_hbm, routes_ref),
        (enc_hbm, enc_ref),
        (grid_hbm, grid_ref),
        (wq_hbm, wq_ref),
        (kernels_hbm, kernels_ref),
        (wk_hbm, wk_ref),
        (wv_hbm, wv_ref),
        (wo_hbm, wo_ref),
        (we_hbm, we_ref),
        (wr_hbm, wr_ref),
        (cot_hbm, cot_ref),
    )
    loads = [
        pltpu.make_async_copy(source, target, load_sems.at[index])
        for index, (source, target) in enumerate(pairs)
    ]
    for load in loads:
        load.start()
    results = (
        (analysis_ref, analysis_hbm),
        (grad_enc_ref, grad_enc_hbm),
        (out_attention, attention_hbm),
        (out_1, sums_1_hbm),
        (out_0, sums_0_hbm),
    )
    stores = [
        pltpu.make_async_copy(source, target, store_sems.at[index])
        for index, (source, target) in enumerate(results)
    ]

    barrier = pltpu.get_barrier_semaphore()

    def greet(to_lon, to_lat):
        pl.semaphore_signal(barrier, inc=1, device_id=(to_lon, to_lat), device_id_type=MESH)

    loop(1, NLAT, lambda k: greet(lon, lax.rem(lat + k, NLAT)))
    loop(1, NLON, lambda k: greet(lax.rem(lon + k, NLON), lat))
    for dx in (1, NLON - 1):
        for dy in (1, NLAT - 1):
            greet(lax.rem(lon + dx, NLON), lax.rem(lat + dy, NLAT))

    loads[0].wait()
    loads[1].wait()
    chunk = jnp.minimum(me * BLOCKS_DEV // 128, DEVICES * BLOCKS_DEV // 128 - 2)
    shift = me * BLOCKS_DEV - chunk * 128
    window = routes_ref[:, pl.ds(aligned(chunk * 128, 128), 256)].astype(F32).astype(BF16)
    pick = one_hot(iota((256, BLOCKS_DEV), 0) == iota((256, BLOCKS_DEV), 1) + shift)
    own = mm(window, pick).astype(jnp.int32)
    row_id = iota((DEVICES, BLOCKS_DEV), 0)
    tile_id = lax.rem(row_id, NLON) * NLAT + row_id // NLON
    hits = (own[0:1] == tile_id) | (own[1:2] == tile_id)
    before = one_hot(iota((BLOCKS_DEV, BLOCKS_DEV), 0) < iota((BLOCKS_DEV, BLOCKS_DEV), 1))
    hot = one_hot(hits)
    earlier = mm(hot, before)
    tokens_f32 = enc_ref[...].astype(F32)
    for c in range(2):
        chosen = jnp.where(jnp.abs(earlier - c) < 0.5, hot.astype(F32), 0.0).astype(BF16)
        chosen_ref[c] = chosen
        for token in range(2):
            at = c * 512 + token * CH
            send_a[:, at : at + CH] = mm(chosen, tokens_f32[:, token, :].astype(BF16)).astype(BF16)

    pl.semaphore_wait(barrier, NLAT - 1 + NLON - 1 + 4)

    def a2a(src, dst, index, to_lon, to_lat):
        return pltpu.make_async_remote_copy(
            src_ref=src,
            dst_ref=dst,
            send_sem=a2a_sems.at[0, index],
            recv_sem=a2a_sems.at[1, index],
            device_id=(to_lon, to_lat),
            device_id_type=MESH,
        )

    def block(index):
        return pl.ds(aligned(index * 16, 16), 16)

    def along_lat(src, dst, hop, k):
        peer = lax.rem(lat + k, NLAT)
        return a2a(src.at[block(peer)], dst.at[block(lat)], hop, lon, peer)

    def along_lon(src, dst, hop, k):
        peer = lax.rem(lon + k, NLON)
        return a2a(src.at[block(peer)], dst.at[block(lon)], hop, peer, lat)

    def start_hop(route, src, dst, hop, count):
        loop(1, count, lambda k: route(src, dst, hop, k).start())

    def end_hop(src, dst, hop, count):
        rows = pl.ds(0, (count - 1) * 16)
        a2a(src.at[rows], src.at[rows], hop, lon, lat).wait_send()
        a2a(dst.at[rows], dst.at[rows], hop, lon, lat).wait_recv()

    start_hop(along_lat, send_a, recv_a, 0, NLAT)
    recv_a[block(lat)] = send_a[block(lat)]

    loads[2].wait()
    loads[3].wait()
    normed = normalise(grid_ref[...].astype(F32))[0].astype(BF16)
    normed_ref[...] = normed
    queries = mm(normed, wq_ref[...]).astype(BF16)
    queries_t = queries.T
    qt_ref[...] = queries_t
    for odd in range(2):
        row = DEPTH * (1 - odd)
        qt_one_ref[odd] = queries_t
        first = queries_t[row : row + 16].astype(F32)
        qt_one_ref[odd, row : row + 16, :] = jnp.where(iota((16, CELLS), 0) == 0, 1.0, first).astype(
            BF16
        )
    mine = jnp.sum(jnp.where(routes_ref[...] == me, 1.0, 0.0), axis=0, keepdims=True)
    for group in range(32):
        group_ref[group : group + 1, :] = mine[:, group * 384 : group * 384 + 384]
    fold = one_hot(iota((384, 128), 0) // BLOCKS_DEV == iota((384, 128), 1))
    counts = mm(group_ref[...].astype(BF16), fold).astype(BF16)
    slot = iota((256, 32), 0)
    source = (slot // 16) * NLAT + lax.rem(slot, NLAT)
    spread = mm(one_hot(source // 4 == iota((256, 32), 1)), counts)
    slot = iota((256, 128), 0)
    source = (slot // 16) * NLAT + lax.rem(slot, NLAT)
    count = jnp.sum(
        jnp.where(lax.rem(source, 4) == iota((256, 128), 1), spread, 0.0), axis=1, keepdims=True
    )
    rank = (lax.rem(iota((256, CH), 0), 16) // NLAT).astype(F32)
    for odd in range(2):
        silent = (jnp.broadcast_to(count, (256, CH)) < rank + 0.5) & (
            iota((256, CH), 1) == DEPTH * (1 - odd)
        )
        dead = jnp.where(silent, -1e30, 0.0).astype(BF16)
        dead_ref[odd, 0:256] = dead
        dead_ref[odd, 256:512] = dead
    loads[4].wait()
    for a in range(7):
        for b in range(7):
            tap = kernels_ref[a, b].astype(F32)
            for half in range(2):
                taps_ref[half, a * 7 + b] = tap[:, half * 128 : half * 128 + 128]

    out_row, in_row = iota((256, 256), 0), iota((256, 256), 1)
    shuffle = one_hot(
        (lax.rem(out_row, 16) // NLAT) * 128 + lax.rem(out_row, NLAT) * 16 + out_row // 16 == in_row
    )
    end_hop(send_a, recv_a, 0, NLAT)
    send_b[...] = (
        mm(shuffle[:, :128], recv_a[:, :512]) + mm(shuffle[:, 128:], recv_a[:, 512:])
    ).astype(BF16)
    start_hop(along_lon, send_b, recv_b, 1, NLON)
    recv_b[block(lon)] = send_b[block(lon)]
    end_hop(send_b, recv_b, 1, NLON)

    loads[5].wait()
    loads[6].wait()
    for token in range(2):
        tokens = recv_b[:, token * CH : token * CH + CH]
        rows = slice(token * 256, token * 256 + 256)
        k_ref[rows] = mm(tokens, wk_ref[...]).astype(BF16)
        v_ref[rows] = mm(tokens, wv_ref[...]).astype(BF16)
    kt_ref[...] = k_ref[...].T
    vt_ref[...] = v_ref[...].T

    def head_mask(head):
        return jnp.where(iota((1, CH), 1) // DEPTH == head, 1.0, 0.0).astype(BF16)

    def head_rows(head):
        return pl.ds(aligned(head * DEPTH, DEPTH), DEPTH)

    def attend(head_pair):
        for odd in range(2):
            head = head_pair * 2 + odd
            keys = k_ref[...] * head_mask(head) + dead_ref[odd]
            for part in range(2):
                cells = slice(part * 256, part * 256 + 256)
                raised = jnp.exp2(mm(keys, qt_one_ref[odd, :, cells]) * (SCALE * LOG2_E))
                weights = raised * (1.0 / jnp.sum(raised, axis=0, keepdims=True))
                probs = weights.astype(BF16)
                probs_ref[head, :, cells] = probs
                ctx_t_ref[head_rows(head), cells] = mm(vt_ref[head_rows(head), :], probs).astype(
                    BF16
                )

    loop(0, HEADS // 2, attend)

    for load in loads[7:]:
        load.wait()
    state = (grid_ref[...].astype(F32) + mm_tn(ctx_t_ref[...], wo_ref[...])).astype(BF16)
    st_ref[0] = state.reshape(ROWS, COLS, CH)

    def halo(index, tile):
        return Halo(
            place,
            tile,
            halo_packed.at[index],
            halo_rows.at[index],
            halo_cols.at[index],
            halo_corners.at[index],
            halo_sems.at[index],
        )

    for layer in range(2):
        edge = halo(layer, st_ref.at[layer])
        edge.start()
        padded = pad_ref.at[layer]
        edge.fill_inner(padded)

        correlate(padded, taps_ref, layer, False, True, inner_ref, (1, 2))
        edge.fill_sides(padded)
        correlate(padded, taps_ref, layer, False, True, inner_ref, (0, 3))
        edge.fill_ends(padded)
        correlate(padded, taps_ref, layer, False, False, inner_ref, range(4))

        def mix(row_pair):
            top = aligned(row_pair * 2, 2)
            mixed = jnp.concatenate(
                [inner_ref[0, pl.ds(top, 2)], inner_ref[1, pl.ds(top, 2)]], axis=-1
            ).reshape(128, CH)
            xhat, scale = normalise(mixed)
            rows = pl.ds(aligned(row_pair * 128, 128), 128)
            xhat_ref[layer, rows] = xhat
            rstd_ref[layer, rows] = jnp.broadcast_to(scale, (128, 128))
            normed_low = xhat.astype(BF16)
            nrm_ref[layer, rows] = normed_low
            pre = mm(normed_low, we_ref[layer])
            square = pre * pre
            curve = jnp.tanh(pre * (GELU_0 + GELU_1 * square))
            gate = 0.5 + 0.5 * curve
            wide = (pre * gate).astype(BF16)
            dgelu_ref[layer, rows] = gate + 0.5 * pre * (1.0 - curve * curve) * (
                GELU_0 + 3.0 * GELU_1 * square
            )
            wide_ref[layer, rows] = wide
            before_mix = st_ref[layer, pl.ds(top, 2)].reshape(128, CH).astype(F32)
            after = (before_mix + mm(wide, wr_ref[layer])).astype(BF16)
            if layer == 0:
                st_ref[1, pl.ds(top, 2)] = after.reshape(2, COLS, CH)
            else:
                analysis_ref[rows] = after

        loop(0, 4, mix)

    kgrad_ref[...] = jnp.zeros_like(kgrad_ref)
    stores[0].start()
    reduce_1 = Exchange(
        place, True, False, x_1, half_1, l1_1, part_1, l2_1, out_1, sems_1, BIG
    )
    reduce_0 = Exchange(
        place, False, False, x_0, half_0, l1_0, part_0, l2_0, out_0, sems_0, BIG
    )
    reduce_att = Exchange(
        place, True, True, x_attention, half_att, l1_att, part_att, l2_att, out_attention, sems_att, ATT
    )

    grad_ref[...] = cot_ref[...].astype(F32)
    for layer in (1, 0):
        sums = x_1 if layer == 1 else x_0

        def unmix(row_pair):
            top = aligned(row_pair * 2, 2)
            rows = pl.ds(aligned(row_pair * 128, 128), 128)
            low = grad_ref[rows].astype(BF16)
            low_ref[rows] = low
            grad_pre = (mm_nt(low, wr_ref[layer]) * dgelu_ref[layer, rows]).astype(BF16)
            gpre_ref[rows] = grad_pre
            grad_norm = mm_nt(grad_pre, we_ref[layer])
            xhat = xhat_ref[layer, rows]
            centred = (
                grad_norm
                - jnp.mean(grad_norm, axis=-1, keepdims=True)
                - xhat * jnp.mean(grad_norm * xhat, axis=-1, keepdims=True)
            )
            grad_mixed = (centred * rstd_ref[layer, rows][:, :1]).astype(BF16)
            gl_ref[layer, pl.ds(top, 2)] = grad_mixed.reshape(2, COLS, CH)

        loop(0, 4, unmix)
        edge = halo(2 + layer, gl_ref.at[layer])
        edge.start()
        edge.fill_inner(pad_back)

        for piece in range(4):
            lanes = slice(piece * 256, piece * 256 + 256)
            rows = slice(piece * 256, piece * 256 + 256)
            sums[rows] = mm_tn(nrm_ref[layer], gpre_ref[:, lanes]).astype(BF16)
            more = slice(1024 + piece * 256, 1280 + piece * 256)
            sums[more] = mm_tn(wide_ref[layer, :, lanes], low_ref[...]).astype(BF16)
        if layer == 1:
            reduce_1.start_0()
        else:
            reduce_0.start_0()
            reduce_1.start_2()

        for half in range(2):
            inner_ref[half] = pad_back[half, 3 : 3 + ROWS, 8 : 8 + COLS, :]
        kernel_grads(pad_ref.at[layer], inner_ref, kgrad_ref, layer)
        if layer == 1:
            reduce_1.start_1()
        else:
            reduce_0.start_1()

        correlate(pad_back, taps_ref, layer, True, True, inner_ref, (1, 2))
        edge.fill_sides(pad_back)
        correlate(pad_back, taps_ref, layer, True, True, inner_ref, (0, 3))
        edge.fill_ends(pad_back)
        correlate(pad_back, taps_ref, layer, True, False, inner_ref, range(4))
        for half in range(2):
            lanes = slice(half * 128, half * 128 + 128)
            grad_ref[:, lanes] = grad_ref[:, lanes] + inner_ref[half].reshape(CELLS, 128)

    for half in range(2):
        row = BIG + half * 128
        x_attention[row : row + 112] = kgrad_ref[half].astype(BF16)
        x_attention[row + 112 : row + 128] = jnp.zeros((16, 128), BF16)
    reduce_1.start_3()

    def put_attention(index, matrix):
        for half in range(2):
            row = (index * 2 + half) * 256
            x_attention[row : row + 256] = matrix[:, half * 128 : half * 128 + 128].astype(BF16)

    low = grad_ref[...].astype(BF16)
    put_attention(3, mm(ctx_t_ref[...], low))
    gctx = mm_nt(low, wo_ref[...]).astype(BF16)
    gt_ref[...] = gctx.T

    def unattend(head_pair):
        for odd in range(2):
            head = head_pair * 2 + odd
            mine = head_rows(head)
            values = v_ref[...] * head_mask(head)
            for part in range(2):
                cells = slice(part * 256, part * 256 + 256)
                weights = probs_ref[head, :, cells].astype(F32)
                grad_probs = mm(values, gt_ref[:, cells])
                mean = jnp.sum(weights * grad_probs, axis=0, keepdims=True)
                scores_ref[odd, :, cells] = (weights * (grad_probs - mean)).astype(BF16)
            dv_t_ref[mine, :] = mm_nt(gt_ref[mine, :], probs_ref[head]).astype(BF16)
            grad_scores = scores_ref[odd]
            dk_t_ref[mine, :] = (mm_nt(qt_ref[mine, :], grad_scores) * SCALE).astype(BF16)
            dq_t_ref[mine, :] = (mm(kt_ref[mine, :], grad_scores) * SCALE).astype(BF16)

    loop(0, 2, unattend)
    reduce_1.start_4()
    reduce_0.start_2()
    loop(2, 4, unattend)
    reduce_0.start_3()

    grad_keys = dk_t_ref[...].T
    grad_values = dv_t_ref[...].T
    for token in range(2):
        rows = slice(token * 256, token * 256 + 256)
        back_b[:, token * CH : token * CH + CH] = (
            mm_nt(grad_keys[rows], wk_ref[...]) + mm_nt(grad_values[rows], wv_ref[...])
        ).astype(BF16)
    start_hop(along_lon, back_b, got_b, 2, NLON)
    got_b[block(lon)] = back_b[block(lon)]

    put_attention(0, mm(dq_t_ref[...], normed_ref[...]).astype(BF16).T)
    for index, grads in ((1, dk_t_ref), (2, dv_t_ref)):
        sums = mm(grads[:, :256], recv_b[:, :CH]) + mm(grads[:, 256:], recv_b[:, CH:])
        put_attention(index, sums.astype(BF16).T)
    reduce_att.start_0()
    reduce_att.start_1()
    reduce_1.start_5()
    reduce_0.start_4()

    end_hop(back_b, got_b, 2, NLON)
    for c in range(2):
        back_a[:, c * 512 : c * 512 + 512] = mm_tn(
            shuffle[:, c * 128 : c * 128 + 128], got_b[...]
        ).astype(BF16)
    start_hop(along_lat, back_a, got_a, 3, NLAT)
    got_a[block(lat)] = back_a[block(lat)]
    reduce_att.start_2()
    end_hop(back_a, got_a, 3, NLAT)
    grad_enc_ref[...] = mm_tn(chosen_ref[0], got_a[:, :512]) + mm_tn(chosen_ref[1], got_a[:, 512:])
    stores[1].start()
    reduce_1.finish()
    stores[3].start()
    reduce_att.start_3()
    reduce_0.start_5()
    reduce_att.start_5()
    reduce_0.finish()
    stores[4].start()
    reduce_att.finish()
    stores[2].start()
    for store in stores:
        store.wait()


def fused(*operands):
    def b(*shape):
        return pltpu.VMEM(shape, BF16)

    def f(*shape):
        return pltpu.VMEM(shape, F32)

    def sem(*shape):
        return pltpu.SemaphoreType.DMA(shape)

    loaded = [pltpu.VMEM(operand.shape, operand.dtype) for operand in operands]
    results = [
        jax.ShapeDtypeStruct((CELLS, CH), BF16),
        jax.ShapeDtypeStruct((BLOCKS_DEV, 512), F32),
        jax.ShapeDtypeStruct((ATT, 128), BF16),
        jax.ShapeDtypeStruct((BIG, CH), BF16),
        jax.ShapeDtypeStruct((BIG, CH), BF16),
    ]
    scratch = loaded + [
        sem(len(operands)),
        *[pltpu.VMEM(result.shape, result.dtype) for result in results],
        sem(len(results)),
        b(2, DEVICES, BLOCKS_DEV),
        b(128, 1024),
        b(128, 1024),
        b(256, 512),
        b(256, 512),
        b(256, 512),
        b(256, 512),
        b(128, 1024),
        b(128, 1024),
        b(2, SLOTS, CH),
        f(32, 384),
        b(CELLS, CH),
        b(CH, CELLS),
        b(2, CH, CELLS),
        b(SLOTS, CH),
        b(CH, SLOTS),
        b(SLOTS, CH),
        b(CH, SLOTS),
        b(HEADS, SLOTS, CELLS),
        b(CH, CELLS),
        b(2, ROWS, COLS, CH),
        b(2, ROWS, COLS, CH),
        f(2, 2, PAD_ROWS, PAD_COLS, 128),
        f(2, PAD_ROWS, PAD_COLS, 128),
        f(2, ROWS, COLS, 128),
        f(2, 49, 2, 128),
        f(2, 112, 128),
        f(2, CELLS, CH),
        f(2, CELLS, 128),
        b(2, CELLS, CH),
        b(2, CELLS, WIDE),
        f(2, CELLS, WIDE),
        b(CELLS, WIDE),
        f(CELLS, CH),
        b(CELLS, CH),
        b(CH, CELLS),
        b(CH, CELLS),
        b(CH, SLOTS),
        b(CH, SLOTS),
        b(2, SLOTS, CELLS),
        b(4, 2, 32, CH),
        b(4, 2, 3, COLS, CH),
        b(4, 2, 32, CH),
        b(4, 4, 16, CH),
        b(ATT, 128),
        b(BIG, CH),
        b(BIG, CH),
        b(ATT // 2, 128),
        b(BIG // 2, CH),
        b(BIG // 2, CH),
        b(NLAT, ATT // 16, 128),
        b(NLAT, BIG // 16, CH),
        b(NLAT, BIG // 16, CH),
        b(ATT // 16, 128),
        b(BIG // 16, CH),
        b(BIG // 16, CH),
        b(NYZ, ATT // 16, 128),
        b(NYZ, BIG // 128, CH),
        b(NYZ, BIG // 128, CH),
        sem(2, 4),
        sem(4, 2, 3),
        sem(2, 6),
        sem(2, 6),
        sem(2, 6),
    ]
    return pl.pallas_call(
        kernel,
        out_shape=results,
        in_specs=[pl.BlockSpec(memory_space=pltpu.HBM)] * len(operands),
        out_specs=[pl.BlockSpec(memory_space=pltpu.HBM)] * 5,
        scratch_shapes=scratch,
        compiler_params=pltpu.CompilerParams(
            collective_id=0, has_side_effects=True, vmem_limit_bytes=56 * 1024 * 1024
        ),
        name="assimilate",
    )(*operands)


def finishing(
    analysis_hbm,
    grad_enc_hbm,
    attention_hbm,
    sums_1_hbm,
    sums_0_hbm,
    out_analysis,
    out_enc,
    out_attention,
    out_taps,
    out_expand,
    out_reduce,
    sums_in,
    attention_in,
    analysis_in,
    enc_in,
    expand,
    reduce,
    attention,
    taps,
    taps_f32,
    enc,
    in_sems,
    out_sems,
):
    expand_rows, reduce_rows = pl.ds(0, WIDE), pl.ds(WIDE, WIDE)
    inward = (
        (sums_0_hbm.at[expand_rows], sums_in.at[0, expand_rows]),
        (sums_0_hbm.at[reduce_rows], sums_in.at[0, reduce_rows]),
        (sums_1_hbm.at[expand_rows], sums_in.at[1, expand_rows]),
        (sums_1_hbm.at[reduce_rows], sums_in.at[1, reduce_rows]),
        (attention_hbm, attention_in),
        (grad_enc_hbm, enc_in),
        (analysis_hbm, analysis_in),
    )
    outward = (
        (expand.at[0], out_expand.at[0]),
        (reduce.at[0], out_reduce.at[0]),
        (expand.at[1], out_expand.at[1]),
        (reduce.at[1], out_reduce.at[1]),
        (attention, out_attention),
        (taps, out_taps),
        (enc, out_enc),
        (analysis_in, out_analysis),
    )
    loads = [
        pltpu.make_async_copy(source, target, in_sems.at[index])
        for index, (source, target) in enumerate(inward)
    ]
    stores = [
        pltpu.make_async_copy(source, target, out_sems.at[index])
        for index, (source, target) in enumerate(outward)
    ]
    for load in loads:
        load.start()
    for layer in range(2):
        loads[2 * layer].wait()
        for piece in range(4):
            rows = slice(piece * 256, piece * 256 + 256)
            expand[layer, :, rows] = sums_in[layer, rows].astype(F32)
        stores[2 * layer].start()
        loads[2 * layer + 1].wait()
        reduce[layer] = sums_in[layer, WIDE:].astype(F32)
        stores[2 * layer + 1].start()
    loads[4].wait()
    for index in range(4):
        for half in range(2):
            row = (index * 2 + half) * 256
            attention[index, :, half * 128 : half * 128 + 128] = attention_in[
                row : row + 256
            ].astype(F32)
    stores[4].start()
    for half in range(2):
        row = BIG + half * 128
        taps_f32[:, half * 128 : half * 128 + 128] = attention_in[row : row + 128].astype(F32)
    for a in range(7):
        for b in range(7):
            row = (a * 7 + b) * 2
            taps[a, b] = taps_f32[row : row + 2]
    stores[5].start()
    loads[6].wait()
    stores[7].start()
    loads[5].wait()
    for token in range(2):
        enc[:, token, :] = enc_in[:, token * CH : token * CH + CH]
    stores[6].start()
    for store in stores:
        store.wait()


def finished(*operands):
    hbm = pl.BlockSpec(memory_space=pltpu.HBM)
    return pl.pallas_call(
        finishing,
        out_shape=[
            jax.ShapeDtypeStruct((CELLS, CH), BF16),
            jax.ShapeDtypeStruct((BLOCKS_DEV, 2, CH), F32),
            jax.ShapeDtypeStruct((4, CH, CH), F32),
            jax.ShapeDtypeStruct((7, 7, 2, CH), F32),
            jax.ShapeDtypeStruct((2, CH, WIDE), F32),
            jax.ShapeDtypeStruct((2, WIDE, CH), F32),
        ],
        in_specs=[hbm] * 5,
        out_specs=[hbm] * 6,
        scratch_shapes=[
            pltpu.VMEM((2, BIG, CH), BF16),
            pltpu.VMEM((ATT, 128), BF16),
            pltpu.VMEM((CELLS, CH), BF16),
            pltpu.VMEM((BLOCKS_DEV, 512), F32),
            pltpu.VMEM((2, CH, WIDE), F32),
            pltpu.VMEM((2, WIDE, CH), F32),
            pltpu.VMEM((4, CH, CH), F32),
            pltpu.VMEM((7, 7, 2, CH), F32),
            pltpu.VMEM((128, CH), F32),
            pltpu.VMEM((BLOCKS_DEV, 2, CH), F32),
            pltpu.SemaphoreType.DMA((7,)),
            pltpu.SemaphoreType.DMA((8,)),
        ],
        compiler_params=pltpu.CompilerParams(vmem_limit_bytes=56 * 1024 * 1024),
        name="finish",
    )(*operands)


def local(
    grid_state,
    encodings,
    routes,
    w_query,
    w_key,
    w_value,
    w_out,
    kernels,
    w_expand,
    w_reduce,
    cotangent,
):
    results = fused(
        grid_state.reshape(CELLS, CH),
        encodings,
        routes.T,
        w_query,
        w_key,
        w_value,
        w_out,
        kernels.transpose(1, 2, 0, 3),
        w_expand,
        w_reduce,
        cotangent.reshape(CELLS, CH),
    )
    analysis, grad_enc, attention, taps, expand, reduce = finished(*results)
    return (
        analysis.reshape(ROWS, COLS, CH),
        grad_enc,
        attention,
        taps.transpose(2, 0, 1, 3),
        expand,
        reduce,
    )


def solution(mesh):
    in_specs = (
        P("lat", "lon", None),
        P(("lon", "lat"), None, None),
        P(),
        P(),
        P(),
        P(),
        P(),
        P(),
        P(),
        P(),
        P("lat", "lon", None),
    )
    out_specs = (P("lat", "lon", None), P(("lon", "lat"), None, None), P(), P(), P(), P())
    return jax.shard_map(local, mesh=mesh, in_specs=in_specs, out_specs=out_specs, check_vma=False)
```

```python
import functools
import math

import jax
import jax.numpy as jnp
from jax import lax
from jax.experimental import pallas as pl
from jax.experimental.pallas import tpu as pltpu
from jax.sharding import PartitionSpec as P

MESH = pl.DeviceIdType.MESH
F32 = jnp.float32
BF16 = jnp.bfloat16

HEADS = 8
DEPTH = 32
CH = 256
WIDE = 1024
ROWS = 8
COLS = 64
CELLS = ROWS * COLS
NLON = 16
NLAT = 8
NYZ = 8
DEVICES = NLON * NLAT
BLOCKS_DEV = 96
SLOTS = 512
EPSILON = 1e-06
SCALE = 1.0 / math.sqrt(DEPTH)
LOG2_E = math.log2(math.e)
GELU_0 = math.sqrt(2.0 / math.pi)
GELU_1 = GELU_0 * 0.044715
PAD_ROWS = ROWS + 6
PAD_COLS = 80
BIG = 2048
ATT = BIG + 256


def mm(a, b):
    return jnp.dot(a, b, preferred_element_type=F32)


def mm_nt(a, b):
    return lax.dot_general(a, b, (((1,), (1,)), ((), ())), preferred_element_type=F32)


def mm_tn(a, b):
    return lax.dot_general(a, b, (((0,), (0,)), ((), ())), preferred_element_type=F32)


def loop(low, high, body):
    def step(index, carry):
        body(index)
        return carry

    lax.fori_loop(low, high, step, 0)


def aligned(value, by):
    return pl.multiple_of(value, by)


class Exchange:
    def __init__(
        self, place, lat_first, whole, source, half, level_1, part, level_2, total, sems, rows
    ):
        self.lon, self.lat, self.core, self.yz = place
        self.lat_first, self.whole = lat_first, whole
        self.first, self.second = (self.lat, self.yz) if lat_first else (self.yz, self.lat)
        self.source, self.half, self.level_1 = source, half, level_1
        self.part, self.level_2, self.total = part, level_2, total
        self.sems = sems
        self.r1, self.r2, self.r3 = rows // 2, rows // 16, rows // 128

    def copy(self, src, dst, index, device):
        return pltpu.make_async_remote_copy(
            src_ref=src,
            dst_ref=dst,
            send_sem=self.sems.at[0, index],
            recv_sem=self.sems.at[1, index],
            device_id=device,
            device_id_type=MESH,
        )

    def settle(self, phase, sent, arrived):
        self.copy(sent, sent, phase, (self.lon, self.lat)).wait_send()
        self.copy(arrived, arrived, phase, (self.lon, self.lat)).wait_recv()

    def pair(self):
        return (self.lon + 1 - 2 * self.core, self.lat)

    def device(self, on_lat, position):
        if on_lat:
            return (self.lon, position)
        return (position * 2 + self.core, self.lat)

    def to_first(self, k):
        return lax.rem(self.first + k, 8)

    def from_first(self, k):
        return lax.rem(self.first + 8 - k, 8)

    def to_second(self, k):
        return lax.rem(self.second + k, 8)

    def from_second(self, k):
        return lax.rem(self.second + 8 - k, 8)

    def copy_0(self):
        other = aligned((1 - self.core) * self.r1, self.r1)
        return self.copy(self.source.at[pl.ds(other, self.r1)], self.half, 0, self.pair())

    def start_0(self):
        self.copy_0().start()

    def copy_1(self, k):
        peer = self.to_first(k)
        return self.copy(
            self.half.at[pl.ds(aligned(peer * self.r2, self.r2), self.r2)],
            self.level_1.at[k],
            1,
            self.device(self.lat_first, peer),
        )

    def start_1(self):
        self.copy_0().wait()
        mine = aligned(self.core * self.r1, self.r1)
        step = self.r1 // 4

        def add(i):
            at = aligned(i * step, step)
            self.half[pl.ds(at, step)] = (
                self.half[pl.ds(at, step)].astype(F32)
                + self.source[pl.ds(aligned(mine + at, step), step)].astype(F32)
            ).astype(BF16)

        loop(0, 4, add)
        loop(1, 8, lambda k: self.copy_1(k).start())

    def copy_2(self, k):
        peer = self.to_second(k)
        device = self.device(not self.lat_first, peer)
        if self.whole:
            return self.copy(self.part, self.level_2.at[k], 2, device)
        return self.copy(
            self.part.at[pl.ds(aligned(peer * self.r3, self.r3), self.r3)],
            self.level_2.at[k],
            2,
            device,
        )

    def start_2(self):
        self.settle(1, self.half.at[pl.ds(0, 7 * self.r2)], self.level_1.at[pl.ds(1, 7)])
        total = self.half[pl.ds(aligned(self.first * self.r2, self.r2), self.r2)].astype(F32)
        for k in range(1, 8):
            total = total + self.level_1[k].astype(F32)
        self.part[...] = total.astype(BF16)
        loop(1, 8, lambda k: self.copy_2(k).start())

    def offset(self, first, second):
        return self.core * self.r1 + first * self.r2 + second * self.r3

    def copy_3(self, k):
        rows = pl.ds(aligned(self.offset(self.first, self.second), self.r3), self.r3)
        device = self.device(not self.lat_first, self.to_second(k))
        return self.copy(self.total.at[rows], self.total.at[rows], 3, device)

    def start_3(self):
        sent = self.half.at[pl.ds(0, 7 * self.r2)] if self.whole else self.part.at[pl.ds(0, 7 * self.r3)]
        self.settle(2, sent, self.level_2.at[pl.ds(1, 7)])
        if self.whole:
            self.level_2[0] = self.part[...]
            total = jnp.zeros(self.part.shape, F32)
            for index in range(8):
                total = total + self.level_2[lax.rem(self.second + 8 - index, 8)].astype(F32)
            rows = pl.ds(aligned(self.offset(self.first, 0), self.r2), self.r2)
            self.total[rows] = total.astype(BF16)
            loop(1, 8, lambda k: self.copy_4(k).start())
            return
        total = self.part[pl.ds(aligned(self.second * self.r3, self.r3), self.r3)].astype(F32)
        for k in range(1, 8):
            total = total + self.level_2[k].astype(F32)
        rows = pl.ds(aligned(self.offset(self.first, self.second), self.r3), self.r3)
        self.total[rows] = total.astype(BF16)
        loop(1, 8, lambda k: self.copy_3(k).start())

    def copy_4(self, k):
        rows = pl.ds(aligned(self.offset(self.first, 0), self.r2), self.r2)
        device = self.device(self.lat_first, self.to_first(k))
        return self.copy(self.total.at[rows], self.total.at[rows], 4, device)

    def start_4(self):
        rows = self.total.at[pl.ds(0, 7 * self.r3)]
        self.settle(3, rows, rows)
        loop(1, 8, lambda k: self.copy_4(k).start())

    def copy_5(self):
        rows = pl.ds(aligned(self.core * self.r1, self.r1), self.r1)
        return self.copy(self.total.at[rows], self.total.at[rows], 5, self.pair())

    def start_5(self):
        rows = self.total.at[pl.ds(0, 7 * self.r2)]
        self.settle(4, rows, rows)
        self.copy_5().start()

    def finish(self):
        rows = self.total.at[pl.ds(0, self.r1)]
        self.settle(5, rows, rows)


class Halo:
    def __init__(self, place, tile, packed, rows, cols, corners, sems):
        self.lon, self.lat = place[0], place[1]
        self.tile, self.packed, self.rows = tile, packed, rows
        self.cols, self.corners, self.sems = cols, corners, sems

    def copies(self, wanted=range(8)):
        east, west = lax.rem(self.lon + 1, NLON), lax.rem(self.lon + NLON - 1, NLON)
        south, north = lax.rem(self.lat + 1, NLAT), lax.rem(self.lat + NLAT - 1, NLAT)
        upper, lower = pl.ds(0, 16), pl.ds(16, 16)
        plan = [
            (self.tile.at[pl.ds(0, 3)], self.rows.at[1], self.lon, north),
            (self.tile.at[pl.ds(ROWS - 3, 3)], self.rows.at[0], self.lon, south),
            (self.packed.at[0], self.cols.at[1], west, self.lat),
            (self.packed.at[1], self.cols.at[0], east, self.lat),
            (self.packed.at[0, upper], self.corners.at[3], west, north),
            (self.packed.at[1, upper], self.corners.at[2], east, north),
            (self.packed.at[0, lower], self.corners.at[1], west, south),
            (self.packed.at[1, lower], self.corners.at[0], east, south),
        ]
        return [
            pltpu.make_async_remote_copy(
                src_ref=src,
                dst_ref=dst,
                send_sem=self.sems.at[0, (0, 0, 1, 1, 2, 2, 2, 2)[index]],
                recv_sem=self.sems.at[1, (0, 0, 1, 1, 2, 2, 2, 2)[index]],
                device_id=(lon, lat),
                device_id_type=MESH,
            )
            for index, (src, dst, lon, lat) in enumerate(plan)
            if index in wanted
        ]

    def settle(self, kind):
        buffer = (self.rows, self.cols, self.corners)[kind]
        copy = pltpu.make_async_remote_copy(
            src_ref=buffer,
            dst_ref=buffer,
            send_sem=self.sems.at[0, kind],
            recv_sem=self.sems.at[1, kind],
            device_id=(self.lon, self.lat),
            device_id_type=MESH,
        )
        copy.wait_send()
        copy.wait_recv()

    def start(self):
        for copy in self.copies((0, 1)):
            copy.start()
        first = [self.tile[row, 0:16, :].astype(F32)[0:4] for row in range(ROWS)]
        last = [self.tile[row, COLS - 16 : COLS, :].astype(F32)[12:16] for row in range(ROWS)]
        self.packed[0] = jnp.concatenate(first, axis=0).astype(BF16)
        self.packed[1] = jnp.concatenate(last, axis=0).astype(BF16)
        for copy in self.copies(range(2, 8)):
            copy.start()

    def fill_inner(self, padded):
        for row in range(ROWS):
            cells = self.tile[row].astype(F32)
            for half in range(2):
                padded[half, 3 + row, 8 : 8 + COLS, :] = cells[:, half * 128 : half * 128 + 128]

    def fill_sides(self, padded):
        self.settle(1)
        for side, col in ((0, 4), (1, 8 + COLS)):
            cells = self.cols[side].astype(F32)
            for row in range(ROWS):
                for half in range(2):
                    padded[half, 3 + row, col : col + 4, :] = cells[
                        row * 4 : row * 4 + 4, half * 128 : half * 128 + 128
                    ]

    def fill_ends(self, padded):
        self.settle(0)
        self.settle(2)
        has_north = jnp.where(self.lat > 0, 1.0, 0.0).astype(F32)
        has_south = jnp.where(self.lat < NLAT - 1, 1.0, 0.0).astype(F32)
        for end, there, start, skip in ((0, has_north, 0, 1), (1, has_south, 3 + ROWS, 0)):
            corners = [self.corners[2 * end + side].astype(F32) * there for side in range(2)]
            for row in range(3):
                cells = self.rows[end, row].astype(F32) * there
                at = (row + skip) * 4
                for half in range(2):
                    lanes = slice(half * 128, half * 128 + 128)
                    padded[half, start + row, 8 : 8 + COLS, :] = cells[:, lanes]
                    padded[half, start + row, 4:8, :] = corners[0][at : at + 4, lanes]
                    padded[half, start + row, 8 + COLS : 12 + COLS, :] = corners[1][at : at + 4, lanes]


def correlate(padded, taps, block, flipped, inside, result, chunks):
    def one_half(half):
        for chunk in chunks:
            cols = slice(chunk * 16, chunk * 16 + 16)
            sums = [None if inside else result[half, row, cols, :] for row in range(ROWS)]
            for b in range(7):
                rows = {}
                for a in range(7):
                    tap_id = (6 - a) * 7 + (6 - b) if flipped else a * 7 + b
                    tap = taps[half, tap_id, block : block + 1, :]
                    for row in range(ROWS):
                        if (3 <= row + a < 3 + ROWS) != inside:
                            continue
                        if row + a not in rows:
                            first = chunk * 16 + b + 5
                            rows[row + a] = padded[half, row + a, first : first + 16, :]
                        term = rows[row + a] * tap
                        sums[row] = term if sums[row] is None else sums[row] + term
            for row in range(ROWS):
                if inside or row < 3 or row >= ROWS - 3:
                    result[half, row, cols, :] = sums[row]

    loop(0, 2, one_half)


def kernel_grads(padded, inner, results, block):
    def one_half(half):
        for b in range(7):
            sums = [None] * 7
            for chunk in range(8):
                rows = [
                    padded[half, row, chunk * 8 + b + 5 : chunk * 8 + b + 13, :]
                    for row in range(PAD_ROWS)
                ]
                grads = [
                    inner[half, row, chunk * 8 : chunk * 8 + 8, :] for row in range(ROWS)
                ]
                for a in range(7):
                    for row in range(ROWS):
                        term = rows[row + a] * grads[row]
                        sums[a] = term if sums[a] is None else sums[a] + term
            for a in range(7):
                results[half, pl.ds((a * 7 + b) * 2 + block, 1), :] = jnp.sum(
                    sums[a], axis=0, keepdims=True
                )

    loop(0, 2, one_half)


def iota(shape, dim):
    return lax.broadcasted_iota(jnp.int32, shape, dim)


def one_hot(condition):
    return jnp.where(condition, 1.0, 0.0).astype(BF16)


def gelu(values):
    square = values * values
    curve = jnp.tanh(values * (GELU_0 + GELU_1 * square))
    gate = 0.5 + 0.5 * curve
    slope = gate + 0.5 * values * (1.0 - curve * curve) * (GELU_0 + 3.0 * GELU_1 * square)
    return (values * gate).astype(BF16), slope


def normalise(values):
    centred = values - jnp.mean(values, axis=-1, keepdims=True)
    spread = jnp.mean(centred * centred, axis=-1, keepdims=True)
    scale = lax.rsqrt(spread + EPSILON)
    return centred * scale, scale


def kernel(
    grid_hbm,
    enc_hbm,
    routes_hbm,
    wq_hbm,
    wk_hbm,
    wv_hbm,
    wo_hbm,
    kernels_hbm,
    we_hbm,
    wr_hbm,
    cot_hbm,
    analysis_hbm,
    grad_enc_hbm,
    attention_hbm,
    sums_1_hbm,
    sums_0_hbm,
    grid_ref,
    enc_ref,
    routes_ref,
    wq_ref,
    wk_ref,
    wv_ref,
    wo_ref,
    kernels_ref,
    we_ref,
    wr_ref,
    cot_ref,
    load_sems,
    analysis_ref,
    grad_enc_ref,
    out_attention,
    out_1,
    out_0,
    store_sems,
    chosen_ref,
    send_a,
    recv_a,
    send_b,
    recv_b,
    back_b,
    got_b,
    back_a,
    got_a,
    dead_ref,
    group_ref,
    normed_ref,
    qt_ref,
    qt_one_ref,
    k_ref,
    kt_ref,
    v_ref,
    vt_ref,
    probs_ref,
    ctx_t_ref,
    st_ref,
    gl_ref,
    pad_ref,
    pad_back,
    inner_ref,
    taps_ref,
    kgrad_ref,
    xhat_ref,
    rstd_ref,
    nrm_ref,
    wide_ref,
    dgelu_ref,
    gpre_ref,
    grad_ref,
    low_ref,
    gt_ref,
    dq_t_ref,
    dk_t_ref,
    dv_t_ref,
    scores_ref,
    halo_packed,
    halo_rows,
    halo_cols,
    halo_corners,
    x_attention,
    x_1,
    x_0,
    half_att,
    half_1,
    half_0,
    l1_att,
    l1_1,
    l1_0,
    part_att,
    part_1,
    part_0,
    l2_att,
    l2_1,
    l2_0,
    a2a_sems,
    halo_sems,
    sems_att,
    sems_1,
    sems_0,
):
    lon, lat = lax.axis_index("lon"), lax.axis_index("lat")
    core, yz = lax.rem(lon, 2), lon // 2
    place = (lon, lat, core, yz)
    me = lon * NLAT + lat

    pairs = (
        (routes_hbm, routes_ref),
        (enc_hbm, enc_ref),
        (grid_hbm, grid_ref),
        (wq_hbm, wq_ref),
        (kernels_hbm, kernels_ref),
        (wk_hbm, wk_ref),
        (wv_hbm, wv_ref),
        (wo_hbm, wo_ref),
        (we_hbm, we_ref),
        (wr_hbm, wr_ref),
        (cot_hbm, cot_ref),
    )
    loads = [
        pltpu.make_async_copy(source, target, load_sems.at[index])
        for index, (source, target) in enumerate(pairs)
    ]
    for load in loads:
        load.start()
    results = (
        (analysis_ref, analysis_hbm),
        (grad_enc_ref, grad_enc_hbm),
        (out_attention, attention_hbm),
        (out_1, sums_1_hbm),
        (out_0, sums_0_hbm),
    )
    stores = [
        pltpu.make_async_copy(source, target, store_sems.at[index])
        for index, (source, target) in enumerate(results)
    ]

    barrier = pltpu.get_barrier_semaphore()

    def greet(to_lon, to_lat):
        pl.semaphore_signal(barrier, inc=1, device_id=(to_lon, to_lat), device_id_type=MESH)

    loop(1, NLAT, lambda k: greet(lon, lax.rem(lat + k, NLAT)))
    loop(1, NLON, lambda k: greet(lax.rem(lon + k, NLON), lat))
    for dx in (1, NLON - 1):
        for dy in (1, NLAT - 1):
            greet(lax.rem(lon + dx, NLON), lax.rem(lat + dy, NLAT))

    loads[0].wait()
    loads[1].wait()
    chunk = jnp.minimum(me * BLOCKS_DEV // 128, DEVICES * BLOCKS_DEV // 128 - 2)
    shift = me * BLOCKS_DEV - chunk * 128
    window = routes_ref[:, pl.ds(aligned(chunk * 128, 128), 256)].astype(F32).astype(BF16)
    pick = one_hot(iota((256, BLOCKS_DEV), 0) == iota((256, BLOCKS_DEV), 1) + shift)
    own = mm(window, pick).astype(jnp.int32)
    row_id = iota((DEVICES, BLOCKS_DEV), 0)
    tile_id = lax.rem(row_id, NLON) * NLAT + row_id // NLON
    hits = (own[0:1] == tile_id) | (own[1:2] == tile_id)
    before = one_hot(iota((BLOCKS_DEV, BLOCKS_DEV), 0) < iota((BLOCKS_DEV, BLOCKS_DEV), 1))
    hot = one_hot(hits)
    earlier = mm(hot, before)
    tokens_f32 = enc_ref[...].astype(F32)
    for c in range(2):
        chosen = jnp.where(jnp.abs(earlier - c) < 0.5, hot.astype(F32), 0.0).astype(BF16)
        chosen_ref[c] = chosen
        for token in range(2):
            at = c * 512 + token * CH
            send_a[:, at : at + CH] = mm(chosen, tokens_f32[:, token, :].astype(BF16)).astype(BF16)

    pl.semaphore_wait(barrier, NLAT - 1 + NLON - 1 + 4)

    def a2a(src, dst, index, to_lon, to_lat):
        return pltpu.make_async_remote_copy(
            src_ref=src,
            dst_ref=dst,
            send_sem=a2a_sems.at[0, index],
            recv_sem=a2a_sems.at[1, index],
            device_id=(to_lon, to_lat),
            device_id_type=MESH,
        )

    def block(index):
        return pl.ds(aligned(index * 16, 16), 16)

    def along_lat(src, dst, hop, k):
        peer = lax.rem(lat + k, NLAT)
        return a2a(src.at[block(peer)], dst.at[block(lat)], hop, lon, peer)

    def along_lon(src, dst, hop, k):
        peer = lax.rem(lon + k, NLON)
        return a2a(src.at[block(peer)], dst.at[block(lon)], hop, peer, lat)

    def start_hop(route, src, dst, hop, count):
        loop(1, count, lambda k: route(src, dst, hop, k).start())

    def end_hop(src, dst, hop, count):
        rows = pl.ds(0, (count - 1) * 16)
        a2a(src.at[rows], src.at[rows], hop, lon, lat).wait_send()
        a2a(dst.at[rows], dst.at[rows], hop, lon, lat).wait_recv()

    start_hop(along_lat, send_a, recv_a, 0, NLAT)
    recv_a[block(lat)] = send_a[block(lat)]

    loads[2].wait()
    loads[3].wait()
    normed = normalise(grid_ref[...].astype(F32))[0].astype(BF16)
    normed_ref[...] = normed
    queries = mm(normed, wq_ref[...]).astype(BF16)
    queries_t = queries.T
    qt_ref[...] = queries_t
    for odd in range(2):
        row = DEPTH * (1 - odd)
        qt_one_ref[odd] = queries_t
        first = queries_t[row : row + 16].astype(F32)
        qt_one_ref[odd, row : row + 16, :] = jnp.where(iota((16, CELLS), 0) == 0, 1.0, first).astype(
            BF16
        )
    mine = jnp.sum(jnp.where(routes_ref[...] == me, 1.0, 0.0), axis=0, keepdims=True)
    for group in range(32):
        group_ref[group : group + 1, :] = mine[:, group * 384 : group * 384 + 384]
    fold = one_hot(iota((384, 128), 0) // BLOCKS_DEV == iota((384, 128), 1))
    counts = mm(group_ref[...].astype(BF16), fold).astype(BF16)
    slot = iota((256, 32), 0)
    source = (slot // 16) * NLAT + lax.rem(slot, NLAT)
    spread = mm(one_hot(source // 4 == iota((256, 32), 1)), counts)
    slot = iota((256, 128), 0)
    source = (slot // 16) * NLAT + lax.rem(slot, NLAT)
    count = jnp.sum(
        jnp.where(lax.rem(source, 4) == iota((256, 128), 1), spread, 0.0), axis=1, keepdims=True
    )
    rank = (lax.rem(iota((256, CH), 0), 16) // NLAT).astype(F32)
    for odd in range(2):
        silent = (jnp.broadcast_to(count, (256, CH)) < rank + 0.5) & (
            iota((256, CH), 1) == DEPTH * (1 - odd)
        )
        dead = jnp.where(silent, -1e30, 0.0).astype(BF16)
        dead_ref[odd, 0:256] = dead
        dead_ref[odd, 256:512] = dead
    loads[4].wait()
    for a in range(7):
        for b in range(7):
            tap = kernels_ref[a, b].astype(F32)
            for half in range(2):
                taps_ref[half, a * 7 + b] = tap[:, half * 128 : half * 128 + 128]

    out_row, in_row = iota((256, 256), 0), iota((256, 256), 1)
    shuffle = one_hot(
        (lax.rem(out_row, 16) // NLAT) * 128 + lax.rem(out_row, NLAT) * 16 + out_row // 16 == in_row
    )
    end_hop(send_a, recv_a, 0, NLAT)
    send_b[...] = (
        mm(shuffle[:, :128], recv_a[:, :512]) + mm(shuffle[:, 128:], recv_a[:, 512:])
    ).astype(BF16)
    start_hop(along_lon, send_b, recv_b, 1, NLON)
    recv_b[block(lon)] = send_b[block(lon)]
    end_hop(send_b, recv_b, 1, NLON)

    loads[5].wait()
    loads[6].wait()
    for token in range(2):
        tokens = recv_b[:, token * CH : token * CH + CH]
        rows = slice(token * 256, token * 256 + 256)
        k_ref[rows] = mm(tokens, wk_ref[...]).astype(BF16)
        v_ref[rows] = mm(tokens, wv_ref[...]).astype(BF16)
    vt_ref[...] = v_ref[...].T

    def head_mask(head):
        return jnp.where(iota((1, CH), 1) // DEPTH == head, 1.0, 0.0).astype(BF16)

    def head_rows(head):
        return pl.ds(aligned(head * DEPTH, DEPTH), DEPTH)

    def attend(head_pair):
        for odd in range(2):
            head = head_pair * 2 + odd
            keys = k_ref[...] * head_mask(head) + dead_ref[odd]
            for part in range(2):
                cells = slice(part * 256, part * 256 + 256)
                raised = jnp.exp2(mm(keys, qt_one_ref[odd, :, cells]) * (SCALE * LOG2_E))
                weights = raised * (1.0 / jnp.sum(raised, axis=0, keepdims=True))
                probs = weights.astype(BF16)
                probs_ref[head, :, cells] = probs
                ctx_t_ref[head_rows(head), cells] = mm(vt_ref[head_rows(head), :], probs).astype(
                    BF16
                )

    loop(0, HEADS // 2, attend)

    for load in loads[7:]:
        load.wait()
    state = (grid_ref[...].astype(F32) + mm_tn(ctx_t_ref[...], wo_ref[...])).astype(BF16)
    st_ref[0] = state.reshape(ROWS, COLS, CH)

    def halo(index, tile):
        return Halo(
            place,
            tile,
            halo_packed.at[index],
            halo_rows.at[index],
            halo_cols.at[index],
            halo_corners.at[index],
            halo_sems.at[index],
        )

    for layer in range(2):
        edge = halo(layer, st_ref.at[layer])
        edge.start()
        padded = pad_ref.at[layer]
        edge.fill_inner(padded)
        if layer == 0:
            kt_ref[...] = k_ref[...].T
        else:

            def slopes(part):
                rows = pl.ds(aligned(part * 128, 128), 128)
                dgelu_ref[0, rows] = gelu(dgelu_ref[0, rows])[1]

            loop(0, 4, slopes)
        correlate(padded, taps_ref, layer, False, True, inner_ref, (1, 2))
        edge.fill_sides(padded)
        correlate(padded, taps_ref, layer, False, True, inner_ref, (0, 3))
        edge.fill_ends(padded)
        correlate(padded, taps_ref, layer, False, False, inner_ref, range(4))

        def mix(part):
            top = aligned(part * 8, 8)
            mixed = jnp.concatenate(
                [inner_ref[0, pl.ds(top, 8)], inner_ref[1, pl.ds(top, 8)]], axis=-1
            ).reshape(512, CH)
            xhat, scale = normalise(mixed)
            rows = pl.ds(aligned(part * 512, 512), 512)
            xhat_ref[layer, rows] = xhat
            rstd_ref[layer, rows] = jnp.broadcast_to(scale, (512, 128))
            normed_low = xhat.astype(BF16)
            nrm_ref[layer, rows] = normed_low
            pre = mm(normed_low, we_ref[layer])
            wide, slope = gelu(pre)
            dgelu_ref[layer, rows] = pre if layer == 0 else slope
            wide_ref[layer, rows] = wide
            before_mix = st_ref[layer, pl.ds(top, 8)].reshape(512, CH).astype(F32)
            after = (before_mix + mm(wide, wr_ref[layer])).astype(BF16)
            if layer == 0:
                st_ref[1, pl.ds(top, 8)] = after.reshape(8, COLS, CH)
            else:
                analysis_ref[rows] = after

        loop(0, 1, mix)

    kgrad_ref[...] = jnp.zeros_like(kgrad_ref)
    stores[0].start()
    reduce_1 = Exchange(
        place, True, False, x_1, half_1, l1_1, part_1, l2_1, out_1, sems_1, BIG
    )
    reduce_0 = Exchange(
        place, False, False, x_0, half_0, l1_0, part_0, l2_0, out_0, sems_0, BIG
    )
    reduce_att = Exchange(
        place, True, True, x_attention, half_att, l1_att, part_att, l2_att, out_attention, sems_att, ATT
    )

    grad_ref[...] = cot_ref[...].astype(F32)
    for layer in (1, 0):
        sums = x_1 if layer == 1 else x_0

        def unmix(part):
            top = aligned(part * 8, 8)
            rows = pl.ds(aligned(part * 512, 512), 512)
            low = grad_ref[rows].astype(BF16)
            low_ref[rows] = low
            grad_pre = (mm_nt(low, wr_ref[layer]) * dgelu_ref[layer, rows]).astype(BF16)
            gpre_ref[rows] = grad_pre
            grad_norm = mm_nt(grad_pre, we_ref[layer])
            xhat = xhat_ref[layer, rows]
            centred = (
                grad_norm
                - jnp.mean(grad_norm, axis=-1, keepdims=True)
                - xhat * jnp.mean(grad_norm * xhat, axis=-1, keepdims=True)
            )
            grad_mixed = (centred * rstd_ref[layer, rows][:, :1]).astype(BF16)
            gl_ref[layer, pl.ds(top, 8)] = grad_mixed.reshape(8, COLS, CH)

        loop(0, 1, unmix)
        edge = halo(2 + layer, gl_ref.at[layer])
        edge.start()
        edge.fill_inner(pad_back)

        for piece in range(4):
            lanes = slice(piece * 256, piece * 256 + 256)
            rows = slice(piece * 256, piece * 256 + 256)
            sums[rows] = mm_tn(nrm_ref[layer], gpre_ref[:, lanes]).astype(BF16)
            more = slice(1024 + piece * 256, 1280 + piece * 256)
            sums[more] = mm_tn(wide_ref[layer, :, lanes], low_ref[...]).astype(BF16)
        if layer == 1:
            reduce_1.start_0()
        else:
            reduce_0.start_0()
            reduce_1.start_2()

        for half in range(2):
            inner_ref[half] = pad_back[half, 3 : 3 + ROWS, 8 : 8 + COLS, :]
        kernel_grads(pad_ref.at[layer], inner_ref, kgrad_ref, layer)
        if layer == 1:
            reduce_1.start_1()
        else:
            reduce_0.start_1()

        correlate(pad_back, taps_ref, layer, True, True, inner_ref, (1, 2))
        edge.fill_sides(pad_back)
        correlate(pad_back, taps_ref, layer, True, True, inner_ref, (0, 3))
        edge.fill_ends(pad_back)
        correlate(pad_back, taps_ref, layer, True, False, inner_ref, range(4))
        for half in range(2):
            lanes = slice(half * 128, half * 128 + 128)
            grad_ref[:, lanes] = grad_ref[:, lanes] + inner_ref[half].reshape(CELLS, 128)

    for half in range(2):
        row = BIG + half * 128
        x_attention[row : row + 112] = kgrad_ref[half].astype(BF16)
        x_attention[row + 112 : row + 128] = jnp.zeros((16, 128), BF16)
    reduce_1.start_3()

    def put_attention(index, matrix):
        for half in range(2):
            row = (index * 2 + half) * 256
            x_attention[row : row + 256] = matrix[:, half * 128 : half * 128 + 128].astype(BF16)

    low = grad_ref[...].astype(BF16)
    put_attention(3, mm(ctx_t_ref[...], low))
    gctx = mm_nt(low, wo_ref[...]).astype(BF16)
    gt_ref[...] = gctx.T

    def unattend(head_pair):
        for odd in range(2):
            head = head_pair * 2 + odd
            mine = head_rows(head)
            values = v_ref[...] * head_mask(head)
            for part in range(2):
                cells = slice(part * 256, part * 256 + 256)
                weights = probs_ref[head, :, cells].astype(F32)
                grad_probs = mm(values, gt_ref[:, cells])
                mean = jnp.sum(weights * grad_probs, axis=0, keepdims=True)
                scores_ref[odd, :, cells] = (weights * (grad_probs - mean)).astype(BF16)
            dv_t_ref[mine, :] = mm_nt(gt_ref[mine, :], probs_ref[head]).astype(BF16)
            grad_scores = scores_ref[odd]
            dk_t_ref[mine, :] = (mm_nt(qt_ref[mine, :], grad_scores) * SCALE).astype(BF16)
            dq_t_ref[mine, :] = (mm(kt_ref[mine, :], grad_scores) * SCALE).astype(BF16)

    loop(0, 2, unattend)
    reduce_1.start_4()
    reduce_0.start_2()
    loop(2, 4, unattend)
    reduce_0.start_3()

    grad_keys = dk_t_ref[...].T
    grad_values = dv_t_ref[...].T
    for token in range(2):
        rows = slice(token * 256, token * 256 + 256)
        back_b[:, token * CH : token * CH + CH] = (
            mm_nt(grad_keys[rows], wk_ref[...]) + mm_nt(grad_values[rows], wv_ref[...])
        ).astype(BF16)
    start_hop(along_lon, back_b, got_b, 2, NLON)
    got_b[block(lon)] = back_b[block(lon)]

    put_attention(0, mm(dq_t_ref[...], normed_ref[...]).astype(BF16).T)
    for index, grads in ((1, dk_t_ref), (2, dv_t_ref)):
        sums = mm(grads[:, :256], recv_b[:, :CH]) + mm(grads[:, 256:], recv_b[:, CH:])
        put_attention(index, sums.astype(BF16).T)
    reduce_att.start_0()
    reduce_att.start_1()
    reduce_1.start_5()

    end_hop(back_b, got_b, 2, NLON)
    for c in range(2):
        back_a[:, c * 512 : c * 512 + 512] = mm_tn(
            shuffle[:, c * 128 : c * 128 + 128], got_b[...]
        ).astype(BF16)
    start_hop(along_lat, back_a, got_a, 3, NLAT)
    got_a[block(lat)] = back_a[block(lat)]
    reduce_att.start_2()
    reduce_0.start_4()
    end_hop(back_a, got_a, 3, NLAT)
    grad_enc_ref[...] = mm_tn(chosen_ref[0], got_a[:, :512]) + mm_tn(chosen_ref[1], got_a[:, 512:])
    stores[1].start()
    reduce_1.finish()
    stores[3].start()
    reduce_att.start_3()
    reduce_0.start_5()
    reduce_att.start_5()
    reduce_0.finish()
    stores[4].start()
    reduce_att.finish()
    stores[2].start()
    for store in stores:
        store.wait()


def fused(*operands):
    def b(*shape):
        return pltpu.VMEM(shape, BF16)

    def f(*shape):
        return pltpu.VMEM(shape, F32)

    def sem(*shape):
        return pltpu.SemaphoreType.DMA(shape)

    loaded = [pltpu.VMEM(operand.shape, operand.dtype) for operand in operands]
    results = [
        jax.ShapeDtypeStruct((CELLS, CH), BF16),
        jax.ShapeDtypeStruct((BLOCKS_DEV, 512), F32),
        jax.ShapeDtypeStruct((ATT, 128), BF16),
        jax.ShapeDtypeStruct((BIG, CH), BF16),
        jax.ShapeDtypeStruct((BIG, CH), BF16),
    ]
    scratch = loaded + [
        sem(len(operands)),
        *[pltpu.VMEM(result.shape, result.dtype) for result in results],
        sem(len(results)),
        b(2, DEVICES, BLOCKS_DEV),
        b(128, 1024),
        b(128, 1024),
        b(256, 512),
        b(256, 512),
        b(256, 512),
        b(256, 512),
        b(128, 1024),
        b(128, 1024),
        b(2, SLOTS, CH),
        f(32, 384),
        b(CELLS, CH),
        b(CH, CELLS),
        b(2, CH, CELLS),
        b(SLOTS, CH),
        b(CH, SLOTS),
        b(SLOTS, CH),
        b(CH, SLOTS),
        b(HEADS, SLOTS, CELLS),
        b(CH, CELLS),
        b(2, ROWS, COLS, CH),
        b(2, ROWS, COLS, CH),
        f(2, 2, PAD_ROWS, PAD_COLS, 128),
        f(2, PAD_ROWS, PAD_COLS, 128),
        f(2, ROWS, COLS, 128),
        f(2, 49, 2, 128),
        f(2, 112, 128),
        f(2, CELLS, CH),
        f(2, CELLS, 128),
        b(2, CELLS, CH),
        b(2, CELLS, WIDE),
        f(2, CELLS, WIDE),
        b(CELLS, WIDE),
        f(CELLS, CH),
        b(CELLS, CH),
        b(CH, CELLS),
        b(CH, CELLS),
        b(CH, SLOTS),
        b(CH, SLOTS),
        b(2, SLOTS, CELLS),
        b(4, 2, 32, CH),
        b(4, 2, 3, COLS, CH),
        b(4, 2, 32, CH),
        b(4, 4, 16, CH),
        b(ATT, 128),
        b(BIG, CH),
        b(BIG, CH),
        b(ATT // 2, 128),
        b(BIG // 2, CH),
        b(BIG // 2, CH),
        b(NLAT, ATT // 16, 128),
        b(NLAT, BIG // 16, CH),
        b(NLAT, BIG // 16, CH),
        b(ATT // 16, 128),
        b(BIG // 16, CH),
        b(BIG // 16, CH),
        b(NYZ, ATT // 16, 128),
        b(NYZ, BIG // 128, CH),
        b(NYZ, BIG // 128, CH),
        sem(2, 4),
        sem(4, 2, 3),
        sem(2, 6),
        sem(2, 6),
        sem(2, 6),
    ]
    return pl.pallas_call(
        kernel,
        out_shape=results,
        in_specs=[pl.BlockSpec(memory_space=pltpu.HBM)] * len(operands),
        out_specs=[pl.BlockSpec(memory_space=pltpu.HBM)] * 5,
        scratch_shapes=scratch,
        compiler_params=pltpu.CompilerParams(
            collective_id=0, has_side_effects=True, vmem_limit_bytes=56 * 1024 * 1024
        ),
        name="assimilate",
    )(*operands)


def finishing(
    analysis_hbm,
    grad_enc_hbm,
    attention_hbm,
    sums_1_hbm,
    sums_0_hbm,
    out_analysis,
    out_enc,
    out_attention,
    out_taps,
    out_expand,
    out_reduce,
    sums_in,
    attention_in,
    analysis_in,
    enc_in,
    expand,
    reduce,
    attention,
    taps,
    taps_f32,
    enc,
    in_sems,
    out_sems,
):
    expand_rows, reduce_rows = pl.ds(0, WIDE), pl.ds(WIDE, WIDE)
    inward = (
        (sums_0_hbm.at[expand_rows], sums_in.at[0, expand_rows]),
        (sums_0_hbm.at[reduce_rows], sums_in.at[0, reduce_rows]),
        (sums_1_hbm.at[expand_rows], sums_in.at[1, expand_rows]),
        (sums_1_hbm.at[reduce_rows], sums_in.at[1, reduce_rows]),
        (attention_hbm, attention_in),
        (grad_enc_hbm, enc_in),
        (analysis_hbm, analysis_in),
    )
    outward = (
        (expand.at[0], out_expand.at[0]),
        (reduce.at[0], out_reduce.at[0]),
        (expand.at[1], out_expand.at[1]),
        (reduce.at[1], out_reduce.at[1]),
        (attention, out_attention),
        (taps, out_taps),
        (enc, out_enc),
        (analysis_in, out_analysis),
    )
    loads = [
        pltpu.make_async_copy(source, target, in_sems.at[index])
        for index, (source, target) in enumerate(inward)
    ]
    stores = [
        pltpu.make_async_copy(source, target, out_sems.at[index])
        for index, (source, target) in enumerate(outward)
    ]
    for load in loads:
        load.start()
    for layer in range(2):
        loads[2 * layer].wait()
        for piece in range(4):
            rows = slice(piece * 256, piece * 256 + 256)
            expand[layer, :, rows] = sums_in[layer, rows].astype(F32)
        stores[2 * layer].start()
        loads[2 * layer + 1].wait()
        reduce[layer] = sums_in[layer, WIDE:].astype(F32)
        stores[2 * layer + 1].start()
    loads[4].wait()
    for index in range(4):
        for half in range(2):
            row = (index * 2 + half) * 256
            attention[index, :, half * 128 : half * 128 + 128] = attention_in[
                row : row + 256
            ].astype(F32)
    stores[4].start()
    for half in range(2):
        row = BIG + half * 128
        taps_f32[:, half * 128 : half * 128 + 128] = attention_in[row : row + 128].astype(F32)
    for a in range(7):
        for b in range(7):
            row = (a * 7 + b) * 2
            taps[a, b] = taps_f32[row : row + 2]
    stores[5].start()
    loads[6].wait()
    stores[7].start()
    loads[5].wait()
    for token in range(2):
        enc[:, token, :] = enc_in[:, token * CH : token * CH + CH]
    stores[6].start()
    for store in stores:
        store.wait()


def finished(*operands):
    hbm = pl.BlockSpec(memory_space=pltpu.HBM)
    return pl.pallas_call(
        finishing,
        out_shape=[
            jax.ShapeDtypeStruct((CELLS, CH), BF16),
            jax.ShapeDtypeStruct((BLOCKS_DEV, 2, CH), F32),
            jax.ShapeDtypeStruct((4, CH, CH), F32),
            jax.ShapeDtypeStruct((7, 7, 2, CH), F32),
            jax.ShapeDtypeStruct((2, CH, WIDE), F32),
            jax.ShapeDtypeStruct((2, WIDE, CH), F32),
        ],
        in_specs=[hbm] * 5,
        out_specs=[hbm] * 6,
        scratch_shapes=[
            pltpu.VMEM((2, BIG, CH), BF16),
            pltpu.VMEM((ATT, 128), BF16),
            pltpu.VMEM((CELLS, CH), BF16),
            pltpu.VMEM((BLOCKS_DEV, 512), F32),
            pltpu.VMEM((2, CH, WIDE), F32),
            pltpu.VMEM((2, WIDE, CH), F32),
            pltpu.VMEM((4, CH, CH), F32),
            pltpu.VMEM((7, 7, 2, CH), F32),
            pltpu.VMEM((128, CH), F32),
            pltpu.VMEM((BLOCKS_DEV, 2, CH), F32),
            pltpu.SemaphoreType.DMA((7,)),
            pltpu.SemaphoreType.DMA((8,)),
        ],
        compiler_params=pltpu.CompilerParams(vmem_limit_bytes=56 * 1024 * 1024),
        name="finish",
    )(*operands)


def local(
    grid_state,
    encodings,
    routes,
    w_query,
    w_key,
    w_value,
    w_out,
    kernels,
    w_expand,
    w_reduce,
    cotangent,
):
    results = fused(
        grid_state.reshape(CELLS, CH),
        encodings,
        routes.T,
        w_query,
        w_key,
        w_value,
        w_out,
        kernels.transpose(1, 2, 0, 3),
        w_expand,
        w_reduce,
        cotangent.reshape(CELLS, CH),
    )
    analysis, grad_enc, attention, taps, expand, reduce = finished(*results)
    return (
        analysis.reshape(ROWS, COLS, CH),
        grad_enc,
        attention,
        taps.transpose(2, 0, 1, 3),
        expand,
        reduce,
    )


def solution(mesh):
    in_specs = (
        P("lat", "lon", None),
        P(("lon", "lat"), None, None),
        P(),
        P(),
        P(),
        P(),
        P(),
        P(),
        P(),
        P(),
        P("lat", "lon", None),
    )
    out_specs = (P("lat", "lon", None), P(("lon", "lat"), None, None), P(), P(), P(), P())
    return jax.shard_map(local, mesh=mesh, in_specs=in_specs, out_specs=out_specs, check_vma=False)
```

```python
import functools
import math

import jax
import jax.numpy as jnp
from jax import lax
from jax.experimental import pallas as pl
from jax.experimental.pallas import tpu as pltpu
from jax.sharding import PartitionSpec as P

MESH = pl.DeviceIdType.MESH
F32 = jnp.float32
BF16 = jnp.bfloat16

HEADS = 8
DEPTH = 32
CH = 256
WIDE = 1024
ROWS = 8
COLS = 64
CELLS = ROWS * COLS
NLON = 16
NLAT = 8
NYZ = 8
DEVICES = NLON * NLAT
BLOCKS_DEV = 96
SLOTS = 512
EPSILON = 1e-06
SCALE = 1.0 / math.sqrt(DEPTH)
LOG2_E = math.log2(math.e)
GELU_0 = math.sqrt(2.0 / math.pi)
GELU_1 = GELU_0 * 0.044715
PAD_ROWS = ROWS + 6
PAD_COLS = 80
BIG = 2048
ATT = BIG + 256


def mm(a, b):
    return jnp.dot(a, b, preferred_element_type=F32)


def mm_nt(a, b):
    return lax.dot_general(a, b, (((1,), (1,)), ((), ())), preferred_element_type=F32)


def mm_tn(a, b):
    return lax.dot_general(a, b, (((0,), (0,)), ((), ())), preferred_element_type=F32)


def loop(low, high, body):
    def step(index, carry):
        body(index)
        return carry

    lax.fori_loop(low, high, step, 0)


def aligned(value, by):
    return pl.multiple_of(value, by)


class Exchange:
    def __init__(
        self, place, lat_first, whole, source, half, level_1, part, level_2, total, sems, rows
    ):
        self.lon, self.lat, self.core, self.yz = place
        self.lat_first, self.whole = lat_first, whole
        self.first, self.second = (self.lat, self.yz) if lat_first else (self.yz, self.lat)
        self.source, self.half, self.level_1 = source, half, level_1
        self.part, self.level_2, self.total = part, level_2, total
        self.sems = sems
        self.r1, self.r2, self.r3 = rows // 2, rows // 16, rows // 128

    def copy(self, src, dst, index, device):
        return pltpu.make_async_remote_copy(
            src_ref=src,
            dst_ref=dst,
            send_sem=self.sems.at[0, index],
            recv_sem=self.sems.at[1, index],
            device_id=device,
            device_id_type=MESH,
        )

    def settle(self, phase, sent, arrived):
        self.copy(sent, sent, phase, (self.lon, self.lat)).wait_send()
        self.copy(arrived, arrived, phase, (self.lon, self.lat)).wait_recv()

    def pair(self):
        return (self.lon + 1 - 2 * self.core, self.lat)

    def device(self, on_lat, position):
        if on_lat:
            return (self.lon, position)
        return (position * 2 + self.core, self.lat)

    def to_first(self, k):
        return lax.rem(self.first + k, 8)

    def from_first(self, k):
        return lax.rem(self.first + 8 - k, 8)

    def to_second(self, k):
        return lax.rem(self.second + k, 8)

    def from_second(self, k):
        return lax.rem(self.second + 8 - k, 8)

    def copy_0(self):
        other = aligned((1 - self.core) * self.r1, self.r1)
        return self.copy(self.source.at[pl.ds(other, self.r1)], self.half, 0, self.pair())

    def start_0(self):
        self.copy_0().start()

    def copy_1(self, k):
        peer = self.to_first(k)
        return self.copy(
            self.half.at[pl.ds(aligned(peer * self.r2, self.r2), self.r2)],
            self.level_1.at[k],
            1,
            self.device(self.lat_first, peer),
        )

    def start_1(self):
        self.copy_0().wait()
        mine = aligned(self.core * self.r1, self.r1)
        step = self.r1 // 4

        def add(i):
            at = aligned(i * step, step)
            self.half[pl.ds(at, step)] = (
                self.half[pl.ds(at, step)].astype(F32)
                + self.source[pl.ds(aligned(mine + at, step), step)].astype(F32)
            ).astype(BF16)

        loop(0, 4, add)
        loop(1, 8, lambda k: self.copy_1(k).start())

    def copy_2(self, k):
        peer = self.to_second(k)
        device = self.device(not self.lat_first, peer)
        if self.whole:
            return self.copy(self.part, self.level_2.at[k], 2, device)
        return self.copy(
            self.part.at[pl.ds(aligned(peer * self.r3, self.r3), self.r3)],
            self.level_2.at[k],
            2,
            device,
        )

    def start_2(self):
        self.settle(1, self.half.at[pl.ds(0, 7 * self.r2)], self.level_1.at[pl.ds(1, 7)])
        total = self.half[pl.ds(aligned(self.first * self.r2, self.r2), self.r2)].astype(F32)
        for k in range(1, 8):
            total = total + self.level_1[k].astype(F32)
        self.part[...] = total.astype(BF16)
        loop(1, 8, lambda k: self.copy_2(k).start())

    def offset(self, first, second):
        return self.core * self.r1 + first * self.r2 + second * self.r3

    def copy_3(self, k):
        rows = pl.ds(aligned(self.offset(self.first, self.second), self.r3), self.r3)
        device = self.device(not self.lat_first, self.to_second(k))
        return self.copy(self.total.at[rows], self.total.at[rows], 3, device)

    def start_3(self):
        sent = self.half.at[pl.ds(0, 7 * self.r2)] if self.whole else self.part.at[pl.ds(0, 7 * self.r3)]
        self.settle(2, sent, self.level_2.at[pl.ds(1, 7)])
        if self.whole:
            self.level_2[0] = self.part[...]
            total = jnp.zeros(self.part.shape, F32)
            for index in range(8):
                total = total + self.level_2[lax.rem(self.second + 8 - index, 8)].astype(F32)
            rows = pl.ds(aligned(self.offset(self.first, 0), self.r2), self.r2)
            self.total[rows] = total.astype(BF16)
            loop(1, 8, lambda k: self.copy_4(k).start())
            return
        total = self.part[pl.ds(aligned(self.second * self.r3, self.r3), self.r3)].astype(F32)
        for k in range(1, 8):
            total = total + self.level_2[k].astype(F32)
        rows = pl.ds(aligned(self.offset(self.first, self.second), self.r3), self.r3)
        self.total[rows] = total.astype(BF16)
        loop(1, 8, lambda k: self.copy_3(k).start())

    def copy_4(self, k):
        rows = pl.ds(aligned(self.offset(self.first, 0), self.r2), self.r2)
        device = self.device(self.lat_first, self.to_first(k))
        return self.copy(self.total.at[rows], self.total.at[rows], 4, device)

    def start_4(self):
        rows = self.total.at[pl.ds(0, 7 * self.r3)]
        self.settle(3, rows, rows)
        loop(1, 8, lambda k: self.copy_4(k).start())

    def copy_5(self):
        rows = pl.ds(aligned(self.core * self.r1, self.r1), self.r1)
        return self.copy(self.total.at[rows], self.total.at[rows], 5, self.pair())

    def start_5(self):
        rows = self.total.at[pl.ds(0, 7 * self.r2)]
        self.settle(4, rows, rows)
        self.copy_5().start()

    def finish(self):
        rows = self.total.at[pl.ds(0, self.r1)]
        self.settle(5, rows, rows)


class Halo:
    def __init__(self, place, tile, packed, rows, cols, corners, sems):
        self.lon, self.lat = place[0], place[1]
        self.tile, self.packed, self.rows = tile, packed, rows
        self.cols, self.corners, self.sems = cols, corners, sems

    def copies(self, wanted=range(8)):
        east, west = lax.rem(self.lon + 1, NLON), lax.rem(self.lon + NLON - 1, NLON)
        south, north = lax.rem(self.lat + 1, NLAT), lax.rem(self.lat + NLAT - 1, NLAT)
        upper, lower = pl.ds(0, 16), pl.ds(16, 16)
        plan = [
            (self.tile.at[pl.ds(0, 3)], self.rows.at[1], self.lon, north),
            (self.tile.at[pl.ds(ROWS - 3, 3)], self.rows.at[0], self.lon, south),
            (self.packed.at[0], self.cols.at[1], west, self.lat),
            (self.packed.at[1], self.cols.at[0], east, self.lat),
            (self.packed.at[0, upper], self.corners.at[3], west, north),
            (self.packed.at[1, upper], self.corners.at[2], east, north),
            (self.packed.at[0, lower], self.corners.at[1], west, south),
            (self.packed.at[1, lower], self.corners.at[0], east, south),
        ]
        return [
            pltpu.make_async_remote_copy(
                src_ref=src,
                dst_ref=dst,
                send_sem=self.sems.at[0, (0, 0, 1, 1, 2, 2, 2, 2)[index]],
                recv_sem=self.sems.at[1, (0, 0, 1, 1, 2, 2, 2, 2)[index]],
                device_id=(lon, lat),
                device_id_type=MESH,
            )
            for index, (src, dst, lon, lat) in enumerate(plan)
            if index in wanted
        ]

    def settle(self, kind):
        buffer = (self.rows, self.cols, self.corners)[kind]
        copy = pltpu.make_async_remote_copy(
            src_ref=buffer,
            dst_ref=buffer,
            send_sem=self.sems.at[0, kind],
            recv_sem=self.sems.at[1, kind],
            device_id=(self.lon, self.lat),
            device_id_type=MESH,
        )
        copy.wait_send()
        copy.wait_recv()

    def start(self):
        for copy in self.copies((0, 1)):
            copy.start()
        first = [self.tile[row, 0:16, :].astype(F32)[0:4] for row in range(ROWS)]
        last = [self.tile[row, COLS - 16 : COLS, :].astype(F32)[12:16] for row in range(ROWS)]
        self.packed[0] = jnp.concatenate(first, axis=0).astype(BF16)
        self.packed[1] = jnp.concatenate(last, axis=0).astype(BF16)
        for copy in self.copies(range(2, 8)):
            copy.start()

    def fill_inner(self, padded):
        for row in range(ROWS):
            cells = self.tile[row].astype(F32)
            for half in range(2):
                padded[half, 3 + row, 8 : 8 + COLS, :] = cells[:, half * 128 : half * 128 + 128]

    def fill_sides(self, padded):
        self.settle(1)
        for side, col in ((0, 4), (1, 8 + COLS)):
            cells = self.cols[side].astype(F32)
            for row in range(ROWS):
                for half in range(2):
                    padded[half, 3 + row, col : col + 4, :] = cells[
                        row * 4 : row * 4 + 4, half * 128 : half * 128 + 128
                    ]

    def fill_ends(self, padded):
        self.settle(0)
        self.settle(2)
        has_north = jnp.where(self.lat > 0, 1.0, 0.0).astype(F32)
        has_south = jnp.where(self.lat < NLAT - 1, 1.0, 0.0).astype(F32)
        for end, there, start, skip in ((0, has_north, 0, 1), (1, has_south, 3 + ROWS, 0)):
            corners = [self.corners[2 * end + side].astype(F32) * there for side in range(2)]
            for row in range(3):
                cells = self.rows[end, row].astype(F32) * there
                at = (row + skip) * 4
                for half in range(2):
                    lanes = slice(half * 128, half * 128 + 128)
                    padded[half, start + row, 8 : 8 + COLS, :] = cells[:, lanes]
                    padded[half, start + row, 4:8, :] = corners[0][at : at + 4, lanes]
                    padded[half, start + row, 8 + COLS : 12 + COLS, :] = corners[1][at : at + 4, lanes]


def correlate(padded, taps, block, flipped, inside, result, chunks):
    def one_half(half):
        for chunk in chunks:
            cols = slice(chunk * 16, chunk * 16 + 16)
            sums = [None if inside else result[half, row, cols, :] for row in range(ROWS)]
            for b in range(7):
                rows = {}
                for a in range(7):
                    tap_id = (6 - a) * 7 + (6 - b) if flipped else a * 7 + b
                    tap = taps[half, tap_id, block : block + 1, :]
                    for row in range(ROWS):
                        if (3 <= row + a < 3 + ROWS) != inside:
                            continue
                        if row + a not in rows:
                            first = chunk * 16 + b + 5
                            rows[row + a] = padded[half, row + a, first : first + 16, :]
                        term = rows[row + a] * tap
                        sums[row] = term if sums[row] is None else sums[row] + term
            for row in range(ROWS):
                if inside or row < 3 or row >= ROWS - 3:
                    result[half, row, cols, :] = sums[row]

    loop(0, 2, one_half)


def kernel_grads(padded, inner, results, block):
    def one_half(half):
        for b in range(7):
            sums = [None] * 7
            for chunk in range(8):
                rows = [
                    padded[half, row, chunk * 8 + b + 5 : chunk * 8 + b + 13, :]
                    for row in range(PAD_ROWS)
                ]
                grads = [
                    inner[half, row, chunk * 8 : chunk * 8 + 8, :] for row in range(ROWS)
                ]
                for a in range(7):
                    for row in range(ROWS):
                        term = rows[row + a] * grads[row]
                        sums[a] = term if sums[a] is None else sums[a] + term
            for a in range(7):
                results[half, pl.ds((a * 7 + b) * 2 + block, 1), :] = jnp.sum(
                    sums[a], axis=0, keepdims=True
                )

    loop(0, 2, one_half)


def iota(shape, dim):
    return lax.broadcasted_iota(jnp.int32, shape, dim)


def one_hot(condition):
    return jnp.where(condition, 1.0, 0.0).astype(BF16)


def gelu(values):
    square = values * values
    curve = jnp.tanh(values * (GELU_0 + GELU_1 * square))
    gate = 0.5 + 0.5 * curve
    slope = gate + 0.5 * values * (1.0 - curve * curve) * (GELU_0 + 3.0 * GELU_1 * square)
    return (values * gate).astype(BF16), slope


def normalise(values):
    centred = values - jnp.mean(values, axis=-1, keepdims=True)
    spread = jnp.mean(centred * centred, axis=-1, keepdims=True)
    scale = lax.rsqrt(spread + EPSILON)
    return centred * scale, scale


def kernel(
    grid_hbm,
    enc_hbm,
    routes_hbm,
    wq_hbm,
    wk_hbm,
    wv_hbm,
    wo_hbm,
    kernels_hbm,
    we_hbm,
    wr_hbm,
    cot_hbm,
    analysis_hbm,
    grad_enc_hbm,
    attention_hbm,
    sums_1_hbm,
    sums_0_hbm,
    grid_ref,
    enc_ref,
    routes_ref,
    wq_ref,
    wk_ref,
    wv_ref,
    wo_ref,
    kernels_ref,
    we_ref,
    wr_ref,
    cot_ref,
    load_sems,
    analysis_ref,
    grad_enc_ref,
    out_attention,
    out_1,
    out_0,
    store_sems,
    chosen_ref,
    send_a,
    recv_a,
    send_b,
    recv_b,
    back_b,
    got_b,
    back_a,
    got_a,
    dead_ref,
    group_ref,
    normed_ref,
    qt_ref,
    qt_one_ref,
    k_ref,
    kt_ref,
    v_ref,
    vt_ref,
    probs_ref,
    ctx_t_ref,
    st_ref,
    gl_ref,
    pad_ref,
    pad_back,
    inner_ref,
    taps_ref,
    kgrad_ref,
    xhat_ref,
    rstd_ref,
    nrm_ref,
    wide_ref,
    dgelu_ref,
    gpre_ref,
    grad_ref,
    low_ref,
    gt_ref,
    dq_t_ref,
    dk_t_ref,
    dv_t_ref,
    scores_ref,
    halo_packed,
    halo_rows,
    halo_cols,
    halo_corners,
    x_attention,
    x_1,
    x_0,
    half_att,
    half_1,
    half_0,
    l1_att,
    l1_1,
    l1_0,
    part_att,
    part_1,
    part_0,
    l2_att,
    l2_1,
    l2_0,
    a2a_sems,
    halo_sems,
    sems_att,
    sems_1,
    sems_0,
):
    lon, lat = lax.axis_index("lon"), lax.axis_index("lat")
    core, yz = lax.rem(lon, 2), lon // 2
    place = (lon, lat, core, yz)
    me = lon * NLAT + lat

    pairs = (
        (routes_hbm, routes_ref),
        (enc_hbm, enc_ref),
        (grid_hbm, grid_ref),
        (wq_hbm, wq_ref),
        (kernels_hbm, kernels_ref),
        (wk_hbm, wk_ref),
        (wv_hbm, wv_ref),
        (wo_hbm, wo_ref),
        (we_hbm, we_ref),
        (wr_hbm, wr_ref),
        (cot_hbm, cot_ref),
    )
    loads = [
        pltpu.make_async_copy(source, target, load_sems.at[index])
        for index, (source, target) in enumerate(pairs)
    ]
    for load in loads:
        load.start()
    results = (
        (analysis_ref, analysis_hbm),
        (grad_enc_ref, grad_enc_hbm),
        (out_attention, attention_hbm),
        (out_1, sums_1_hbm),
        (out_0, sums_0_hbm),
    )
    stores = [
        pltpu.make_async_copy(source, target, store_sems.at[index])
        for index, (source, target) in enumerate(results)
    ]

    barrier = pltpu.get_barrier_semaphore()

    def greet(to_lon, to_lat):
        pl.semaphore_signal(barrier, inc=1, device_id=(to_lon, to_lat), device_id_type=MESH)

    loop(1, NLAT, lambda k: greet(lon, lax.rem(lat + k, NLAT)))
    loop(1, NLON, lambda k: greet(lax.rem(lon + k, NLON), lat))
    for dx in (1, NLON - 1):
        for dy in (1, NLAT - 1):
            greet(lax.rem(lon + dx, NLON), lax.rem(lat + dy, NLAT))

    loads[0].wait()
    loads[1].wait()
    chunk = jnp.minimum(me * BLOCKS_DEV // 128, DEVICES * BLOCKS_DEV // 128 - 2)
    shift = me * BLOCKS_DEV - chunk * 128
    window = routes_ref[:, pl.ds(aligned(chunk * 128, 128), 256)].astype(F32).astype(BF16)
    pick = one_hot(iota((256, BLOCKS_DEV), 0) == iota((256, BLOCKS_DEV), 1) + shift)
    own = mm(window, pick).astype(jnp.int32)
    row_id = iota((DEVICES, BLOCKS_DEV), 0)
    tile_id = lax.rem(row_id, NLON) * NLAT + row_id // NLON
    hits = (own[0:1] == tile_id) | (own[1:2] == tile_id)
    before = one_hot(iota((BLOCKS_DEV, BLOCKS_DEV), 0) < iota((BLOCKS_DEV, BLOCKS_DEV), 1))
    hot = one_hot(hits)
    earlier = mm(hot, before)
    tokens_f32 = enc_ref[...].astype(F32)
    for c in range(2):
        chosen = jnp.where(jnp.abs(earlier - c) < 0.5, hot.astype(F32), 0.0).astype(BF16)
        chosen_ref[c] = chosen
        for token in range(2):
            at = c * 512 + token * CH
            send_a[:, at : at + CH] = mm(chosen, tokens_f32[:, token, :].astype(BF16)).astype(BF16)

    pl.semaphore_wait(barrier, NLAT - 1 + NLON - 1 + 4)

    def a2a(src, dst, index, to_lon, to_lat):
        return pltpu.make_async_remote_copy(
            src_ref=src,
            dst_ref=dst,
            send_sem=a2a_sems.at[0, index],
            recv_sem=a2a_sems.at[1, index],
            device_id=(to_lon, to_lat),
            device_id_type=MESH,
        )

    def block(index):
        return pl.ds(aligned(index * 16, 16), 16)

    def along_lat(src, dst, hop, k):
        peer = lax.rem(lat + k, NLAT)
        return a2a(src.at[block(peer)], dst.at[block(lat)], hop, lon, peer)

    def along_lon(src, dst, hop, k):
        peer = lax.rem(lon + k, NLON)
        return a2a(src.at[block(peer)], dst.at[block(lon)], hop, peer, lat)

    def start_hop(route, src, dst, hop, count):
        loop(1, count, lambda k: route(src, dst, hop, k).start())

    def end_hop(src, dst, hop, count):
        rows = pl.ds(0, (count - 1) * 16)
        a2a(src.at[rows], src.at[rows], hop, lon, lat).wait_send()
        a2a(dst.at[rows], dst.at[rows], hop, lon, lat).wait_recv()

    start_hop(along_lat, send_a, recv_a, 0, NLAT)
    recv_a[block(lat)] = send_a[block(lat)]

    loads[2].wait()
    loads[3].wait()
    normed = normalise(grid_ref[...].astype(F32))[0].astype(BF16)
    normed_ref[...] = normed
    queries = mm(normed, wq_ref[...]).astype(BF16)
    queries_t = queries.T
    qt_ref[...] = queries_t
    for odd in range(2):
        row = DEPTH * (1 - odd)
        qt_one_ref[odd] = queries_t
        first = queries_t[row : row + 16].astype(F32)
        qt_one_ref[odd, row : row + 16, :] = jnp.where(iota((16, CELLS), 0) == 0, 1.0, first).astype(
            BF16
        )
    mine = jnp.sum(jnp.where(routes_ref[...] == me, 1.0, 0.0), axis=0, keepdims=True)
    for group in range(32):
        group_ref[group : group + 1, :] = mine[:, group * 384 : group * 384 + 384]
    fold = one_hot(iota((384, 128), 0) // BLOCKS_DEV == iota((384, 128), 1))
    counts = mm(group_ref[...].astype(BF16), fold).astype(BF16)
    slot = iota((256, 32), 0)
    source = (slot // 16) * NLAT + lax.rem(slot, NLAT)
    spread = mm(one_hot(source // 4 == iota((256, 32), 1)), counts)
    slot = iota((256, 128), 0)
    source = (slot // 16) * NLAT + lax.rem(slot, NLAT)
    count = jnp.sum(
        jnp.where(lax.rem(source, 4) == iota((256, 128), 1), spread, 0.0), axis=1, keepdims=True
    )
    rank = (lax.rem(iota((256, CH), 0), 16) // NLAT).astype(F32)
    for odd in range(2):
        silent = (jnp.broadcast_to(count, (256, CH)) < rank + 0.5) & (
            iota((256, CH), 1) == DEPTH * (1 - odd)
        )
        dead = jnp.where(silent, -1e30, 0.0).astype(BF16)
        dead_ref[odd, 0:256] = dead
        dead_ref[odd, 256:512] = dead
    loads[4].wait()
    for a in range(7):
        for b in range(7):
            tap = kernels_ref[a, b].astype(F32)
            for half in range(2):
                taps_ref[half, a * 7 + b] = tap[:, half * 128 : half * 128 + 128]

    out_row, in_row = iota((256, 256), 0), iota((256, 256), 1)
    shuffle = one_hot(
        (lax.rem(out_row, 16) // NLAT) * 128 + lax.rem(out_row, NLAT) * 16 + out_row // 16 == in_row
    )
    end_hop(send_a, recv_a, 0, NLAT)
    send_b[...] = (
        mm(shuffle[:, :128], recv_a[:, :512]) + mm(shuffle[:, 128:], recv_a[:, 512:])
    ).astype(BF16)
    start_hop(along_lon, send_b, recv_b, 1, NLON)
    recv_b[block(lon)] = send_b[block(lon)]
    end_hop(send_b, recv_b, 1, NLON)

    loads[5].wait()
    loads[6].wait()
    for token in range(2):
        tokens = recv_b[:, token * CH : token * CH + CH]
        rows = slice(token * 256, token * 256 + 256)
        k_ref[rows] = mm(tokens, wk_ref[...]).astype(BF16)
        v_ref[rows] = mm(tokens, wv_ref[...]).astype(BF16)
    vt_ref[...] = v_ref[...].T

    def head_mask(head):
        return jnp.where(iota((1, CH), 1) // DEPTH == head, 1.0, 0.0).astype(BF16)

    def head_rows(head):
        return pl.ds(aligned(head * DEPTH, DEPTH), DEPTH)

    def attend(head_pair):
        for odd in range(2):
            head = head_pair * 2 + odd
            keys = k_ref[...] * head_mask(head) + dead_ref[odd]
            for part in range(2):
                cells = slice(part * 256, part * 256 + 256)
                raised = jnp.exp2(mm(keys, qt_one_ref[odd, :, cells]) * (SCALE * LOG2_E))
                weights = raised * (1.0 / jnp.sum(raised, axis=0, keepdims=True))
                probs = weights.astype(BF16)
                probs_ref[head, :, cells] = probs
                ctx_t_ref[head_rows(head), cells] = mm(vt_ref[head_rows(head), :], probs).astype(
                    BF16
                )

    loop(0, HEADS // 2, attend)

    for load in loads[7:]:
        load.wait()
    state = (grid_ref[...].astype(F32) + mm_tn(ctx_t_ref[...], wo_ref[...])).astype(BF16)
    st_ref[0] = state.reshape(ROWS, COLS, CH)

    def halo(index, tile):
        return Halo(
            place,
            tile,
            halo_packed.at[index],
            halo_rows.at[index],
            halo_cols.at[index],
            halo_corners.at[index],
            halo_sems.at[index],
        )

    for layer in range(2):
        edge = halo(layer, st_ref.at[layer])
        edge.start()
        padded = pad_ref.at[layer]
        edge.fill_inner(padded)
        if layer == 0:
            kt_ref[...] = k_ref[...].T
        else:

            def slopes(part):
                rows = pl.ds(aligned(part * 128, 128), 128)
                dgelu_ref[0, rows] = gelu(dgelu_ref[0, rows])[1]

            loop(0, 4, slopes)
        correlate(padded, taps_ref, layer, False, True, inner_ref, (1, 2))
        edge.fill_sides(padded)
        correlate(padded, taps_ref, layer, False, True, inner_ref, (0, 3))
        edge.fill_ends(padded)
        correlate(padded, taps_ref, layer, False, False, inner_ref, range(4))

        def mix(part):
            top = aligned(part * 8, 8)
            mixed = jnp.concatenate(
                [inner_ref[0, pl.ds(top, 8)], inner_ref[1, pl.ds(top, 8)]], axis=-1
            ).reshape(512, CH)
            xhat, scale = normalise(mixed)
            rows = pl.ds(aligned(part * 512, 512), 512)
            xhat_ref[layer, rows] = xhat
            rstd_ref[layer, rows] = jnp.broadcast_to(scale, (512, 128))
            normed_low = xhat.astype(BF16)
            nrm_ref[layer, rows] = normed_low
            pre = mm(normed_low, we_ref[layer])
            wide, slope = gelu(pre)
            dgelu_ref[layer, rows] = pre if layer == 0 else slope
            wide_ref[layer, rows] = wide
            before_mix = st_ref[layer, pl.ds(top, 8)].reshape(512, CH).astype(F32)
            after = (before_mix + mm(wide, wr_ref[layer])).astype(BF16)
            if layer == 0:
                st_ref[1, pl.ds(top, 8)] = after.reshape(8, COLS, CH)
            else:
                analysis_ref[rows] = after

        loop(0, 1, mix)

    kgrad_ref[...] = jnp.zeros_like(kgrad_ref)
    stores[0].start()
    reduce_1 = Exchange(
        place, True, False, x_1, half_1, l1_1, part_1, l2_1, out_1, sems_1, BIG
    )
    reduce_0 = Exchange(
        place, False, False, x_0, half_0, l1_0, part_0, l2_0, out_0, sems_0, BIG
    )
    reduce_att = Exchange(
        place, True, True, x_attention, half_att, l1_att, part_att, l2_att, out_attention, sems_att, ATT
    )

    grad_ref[...] = cot_ref[...].astype(F32)
    for layer in (1, 0):
        sums = x_1 if layer == 1 else x_0

        def unmix(part):
            top = aligned(part * 8, 8)
            rows = pl.ds(aligned(part * 512, 512), 512)
            low = grad_ref[rows].astype(BF16)
            low_ref[rows] = low
            grad_pre = (mm_nt(low, wr_ref[layer]) * dgelu_ref[layer, rows]).astype(BF16)
            gpre_ref[rows] = grad_pre
            grad_norm = mm_nt(grad_pre, we_ref[layer])
            xhat = xhat_ref[layer, rows]
            centred = (
                grad_norm
                - jnp.mean(grad_norm, axis=-1, keepdims=True)
                - xhat * jnp.mean(grad_norm * xhat, axis=-1, keepdims=True)
            )
            grad_mixed = (centred * rstd_ref[layer, rows][:, :1]).astype(BF16)
            gl_ref[layer, pl.ds(top, 8)] = grad_mixed.reshape(8, COLS, CH)

        loop(0, 1, unmix)
        edge = halo(2 + layer, gl_ref.at[layer])
        edge.start()
        edge.fill_inner(pad_back)

        for piece in range(4):
            lanes = slice(piece * 256, piece * 256 + 256)
            rows = slice(piece * 256, piece * 256 + 256)
            sums[rows] = mm_tn(nrm_ref[layer], gpre_ref[:, lanes]).astype(BF16)
            more = slice(1024 + piece * 256, 1280 + piece * 256)
            sums[more] = mm_tn(wide_ref[layer, :, lanes], low_ref[...]).astype(BF16)
        if layer == 1:
            reduce_1.start_0()
        else:
            reduce_0.start_0()
            reduce_1.start_2()

        for half in range(2):
            inner_ref[half] = pad_back[half, 3 : 3 + ROWS, 8 : 8 + COLS, :]
        kernel_grads(pad_ref.at[layer], inner_ref, kgrad_ref, layer)
        if layer == 1:
            reduce_1.start_1()
        else:
            reduce_0.start_1()

        correlate(pad_back, taps_ref, layer, True, True, inner_ref, (1, 2))
        edge.fill_sides(pad_back)
        correlate(pad_back, taps_ref, layer, True, True, inner_ref, (0, 3))
        edge.fill_ends(pad_back)
        correlate(pad_back, taps_ref, layer, True, False, inner_ref, range(4))
        for half in range(2):
            lanes = slice(half * 128, half * 128 + 128)
            grad_ref[:, lanes] = grad_ref[:, lanes] + inner_ref[half].reshape(CELLS, 128)

    for half in range(2):
        row = BIG + half * 128
        x_attention[row : row + 112] = kgrad_ref[half].astype(BF16)
        x_attention[row + 112 : row + 128] = jnp.zeros((16, 128), BF16)
    reduce_1.start_3()

    def put_attention(index, matrix):
        for half in range(2):
            row = (index * 2 + half) * 256
            x_attention[row : row + 256] = matrix[:, half * 128 : half * 128 + 128].astype(BF16)

    low = grad_ref[...].astype(BF16)
    put_attention(3, mm(ctx_t_ref[...], low))
    gctx = mm_nt(low, wo_ref[...]).astype(BF16)
    gt_ref[...] = gctx.T

    def unattend(head_pair):
        for odd in range(2):
            head = head_pair * 2 + odd
            mine = head_rows(head)
            values = v_ref[...] * head_mask(head)
            for part in range(2):
                cells = slice(part * 256, part * 256 + 256)
                weights = probs_ref[head, :, cells].astype(F32)
                grad_probs = mm(values, gt_ref[:, cells])
                mean = jnp.sum(weights * grad_probs, axis=0, keepdims=True)
                scores_ref[odd, :, cells] = (weights * (grad_probs - mean)).astype(BF16)
            dv_t_ref[mine, :] = mm_nt(gt_ref[mine, :], probs_ref[head]).astype(BF16)
            grad_scores = scores_ref[odd]
            dk_t_ref[mine, :] = (mm_nt(qt_ref[mine, :], grad_scores) * SCALE).astype(BF16)
            dq_t_ref[mine, :] = (mm(kt_ref[mine, :], grad_scores) * SCALE).astype(BF16)

    loop(0, 2, unattend)
    reduce_0.start_2()
    reduce_1.start_4()
    loop(2, 4, unattend)
    reduce_0.start_3()

    put_attention(0, mm(dq_t_ref[...], normed_ref[...]).astype(BF16).T)
    for index, grads in ((1, dk_t_ref), (2, dv_t_ref)):
        sums = mm(grads[:, :256], recv_b[:, :CH]) + mm(grads[:, 256:], recv_b[:, CH:])
        put_attention(index, sums.astype(BF16).T)
    reduce_att.start_0()
    grad_keys = dk_t_ref[...].T
    grad_values = dv_t_ref[...].T
    for token in range(2):
        rows = slice(token * 256, token * 256 + 256)
        back_b[:, token * CH : token * CH + CH] = (
            mm_nt(grad_keys[rows], wk_ref[...]) + mm_nt(grad_values[rows], wv_ref[...])
        ).astype(BF16)
    reduce_att.start_1()
    start_hop(along_lon, back_b, got_b, 2, NLON)
    got_b[block(lon)] = back_b[block(lon)]
    reduce_1.start_5()
    reduce_att.start_2()
    reduce_0.start_4()

    end_hop(back_b, got_b, 2, NLON)
    for c in range(2):
        back_a[:, c * 512 : c * 512 + 512] = mm_tn(
            shuffle[:, c * 128 : c * 128 + 128], got_b[...]
        ).astype(BF16)
    start_hop(along_lat, back_a, got_a, 3, NLAT)
    got_a[block(lat)] = back_a[block(lat)]
    reduce_1.finish()
    stores[3].start()
    reduce_att.start_3()
    end_hop(back_a, got_a, 3, NLAT)
    grad_enc_ref[...] = mm_tn(chosen_ref[0], got_a[:, :512]) + mm_tn(chosen_ref[1], got_a[:, 512:])
    stores[1].start()
    reduce_0.start_5()
    reduce_att.start_5()
    reduce_0.finish()
    stores[4].start()
    reduce_att.finish()
    stores[2].start()
    for store in stores:
        store.wait()


def fused(*operands):
    def b(*shape):
        return pltpu.VMEM(shape, BF16)

    def f(*shape):
        return pltpu.VMEM(shape, F32)

    def sem(*shape):
        return pltpu.SemaphoreType.DMA(shape)

    loaded = [pltpu.VMEM(operand.shape, operand.dtype) for operand in operands]
    results = [
        jax.ShapeDtypeStruct((CELLS, CH), BF16),
        jax.ShapeDtypeStruct((BLOCKS_DEV, 512), F32),
        jax.ShapeDtypeStruct((ATT, 128), BF16),
        jax.ShapeDtypeStruct((BIG, CH), BF16),
        jax.ShapeDtypeStruct((BIG, CH), BF16),
    ]
    scratch = loaded + [
        sem(len(operands)),
        *[pltpu.VMEM(result.shape, result.dtype) for result in results],
        sem(len(results)),
        b(2, DEVICES, BLOCKS_DEV),
        b(128, 1024),
        b(128, 1024),
        b(256, 512),
        b(256, 512),
        b(256, 512),
        b(256, 512),
        b(128, 1024),
        b(128, 1024),
        b(2, SLOTS, CH),
        f(32, 384),
        b(CELLS, CH),
        b(CH, CELLS),
        b(2, CH, CELLS),
        b(SLOTS, CH),
        b(CH, SLOTS),
        b(SLOTS, CH),
        b(CH, SLOTS),
        b(HEADS, SLOTS, CELLS),
        b(CH, CELLS),
        b(2, ROWS, COLS, CH),
        b(2, ROWS, COLS, CH),
        f(2, 2, PAD_ROWS, PAD_COLS, 128),
        f(2, PAD_ROWS, PAD_COLS, 128),
        f(2, ROWS, COLS, 128),
        f(2, 49, 2, 128),
        f(2, 112, 128),
        f(2, CELLS, CH),
        f(2, CELLS, 128),
        b(2, CELLS, CH),
        b(2, CELLS, WIDE),
        f(2, CELLS, WIDE),
        b(CELLS, WIDE),
        f(CELLS, CH),
        b(CELLS, CH),
        b(CH, CELLS),
        b(CH, CELLS),
        b(CH, SLOTS),
        b(CH, SLOTS),
        b(2, SLOTS, CELLS),
        b(4, 2, 32, CH),
        b(4, 2, 3, COLS, CH),
        b(4, 2, 32, CH),
        b(4, 4, 16, CH),
        b(ATT, 128),
        b(BIG, CH),
        b(BIG, CH),
        b(ATT // 2, 128),
        b(BIG // 2, CH),
        b(BIG // 2, CH),
        b(NLAT, ATT // 16, 128),
        b(NLAT, BIG // 16, CH),
        b(NLAT, BIG // 16, CH),
        b(ATT // 16, 128),
        b(BIG // 16, CH),
        b(BIG // 16, CH),
        b(NYZ, ATT // 16, 128),
        b(NYZ, BIG // 128, CH),
        b(NYZ, BIG // 128, CH),
        sem(2, 4),
        sem(4, 2, 3),
        sem(2, 6),
        sem(2, 6),
        sem(2, 6),
    ]
    return pl.pallas_call(
        kernel,
        out_shape=results,
        in_specs=[pl.BlockSpec(memory_space=pltpu.HBM)] * len(operands),
        out_specs=[pl.BlockSpec(memory_space=pltpu.HBM)] * 5,
        scratch_shapes=scratch,
        compiler_params=pltpu.CompilerParams(
            collective_id=0, has_side_effects=True, vmem_limit_bytes=56 * 1024 * 1024
        ),
        name="assimilate",
    )(*operands)


def finishing(
    analysis_hbm,
    grad_enc_hbm,
    attention_hbm,
    sums_1_hbm,
    sums_0_hbm,
    out_analysis,
    out_enc,
    out_attention,
    out_taps,
    out_expand,
    out_reduce,
    sums_in,
    attention_in,
    analysis_in,
    enc_in,
    expand,
    reduce,
    attention,
    taps,
    taps_f32,
    enc,
    in_sems,
    out_sems,
):
    expand_rows, reduce_rows = pl.ds(0, WIDE), pl.ds(WIDE, WIDE)
    inward = (
        (sums_0_hbm.at[expand_rows], sums_in.at[0, expand_rows]),
        (sums_0_hbm.at[reduce_rows], sums_in.at[0, reduce_rows]),
        (sums_1_hbm.at[expand_rows], sums_in.at[1, expand_rows]),
        (sums_1_hbm.at[reduce_rows], sums_in.at[1, reduce_rows]),
        (attention_hbm, attention_in),
        (grad_enc_hbm, enc_in),
        (analysis_hbm, analysis_in),
    )
    outward = (
        (expand.at[0], out_expand.at[0]),
        (reduce.at[0], out_reduce.at[0]),
        (expand.at[1], out_expand.at[1]),
        (reduce.at[1], out_reduce.at[1]),
        (attention, out_attention),
        (taps, out_taps),
        (enc, out_enc),
        (analysis_in, out_analysis),
    )
    loads = [
        pltpu.make_async_copy(source, target, in_sems.at[index])
        for index, (source, target) in enumerate(inward)
    ]
    stores = [
        pltpu.make_async_copy(source, target, out_sems.at[index])
        for index, (source, target) in enumerate(outward)
    ]
    for load in loads:
        load.start()
    for layer in range(2):
        loads[2 * layer].wait()
        for piece in range(4):
            rows = slice(piece * 256, piece * 256 + 256)
            expand[layer, :, rows] = sums_in[layer, rows].astype(F32)
        stores[2 * layer].start()
        loads[2 * layer + 1].wait()
        reduce[layer] = sums_in[layer, WIDE:].astype(F32)
        stores[2 * layer + 1].start()
    loads[4].wait()
    for index in range(4):
        for half in range(2):
            row = (index * 2 + half) * 256
            attention[index, :, half * 128 : half * 128 + 128] = attention_in[
                row : row + 256
            ].astype(F32)
    stores[4].start()
    for half in range(2):
        row = BIG + half * 128
        taps_f32[:, half * 128 : half * 128 + 128] = attention_in[row : row + 128].astype(F32)
    for a in range(7):
        for b in range(7):
            row = (a * 7 + b) * 2
            taps[a, b] = taps_f32[row : row + 2]
    stores[5].start()
    loads[6].wait()
    stores[7].start()
    loads[5].wait()
    for token in range(2):
        enc[:, token, :] = enc_in[:, token * CH : token * CH + CH]
    stores[6].start()
    for store in stores:
        store.wait()


def finished(*operands):
    hbm = pl.BlockSpec(memory_space=pltpu.HBM)
    return pl.pallas_call(
        finishing,
        out_shape=[
            jax.ShapeDtypeStruct((CELLS, CH), BF16),
            jax.ShapeDtypeStruct((BLOCKS_DEV, 2, CH), F32),
            jax.ShapeDtypeStruct((4, CH, CH), F32),
            jax.ShapeDtypeStruct((7, 7, 2, CH), F32),
            jax.ShapeDtypeStruct((2, CH, WIDE), F32),
            jax.ShapeDtypeStruct((2, WIDE, CH), F32),
        ],
        in_specs=[hbm] * 5,
        out_specs=[hbm] * 6,
        scratch_shapes=[
            pltpu.VMEM((2, BIG, CH), BF16),
            pltpu.VMEM((ATT, 128), BF16),
            pltpu.VMEM((CELLS, CH), BF16),
            pltpu.VMEM((BLOCKS_DEV, 512), F32),
            pltpu.VMEM((2, CH, WIDE), F32),
            pltpu.VMEM((2, WIDE, CH), F32),
            pltpu.VMEM((4, CH, CH), F32),
            pltpu.VMEM((7, 7, 2, CH), F32),
            pltpu.VMEM((128, CH), F32),
            pltpu.VMEM((BLOCKS_DEV, 2, CH), F32),
            pltpu.SemaphoreType.DMA((7,)),
            pltpu.SemaphoreType.DMA((8,)),
        ],
        compiler_params=pltpu.CompilerParams(vmem_limit_bytes=56 * 1024 * 1024),
        name="finish",
    )(*operands)


def local(
    grid_state,
    encodings,
    routes,
    w_query,
    w_key,
    w_value,
    w_out,
    kernels,
    w_expand,
    w_reduce,
    cotangent,
):
    results = fused(
        grid_state.reshape(CELLS, CH),
        encodings,
        routes.T,
        w_query,
        w_key,
        w_value,
        w_out,
        kernels.transpose(1, 2, 0, 3),
        w_expand,
        w_reduce,
        cotangent.reshape(CELLS, CH),
    )
    analysis, grad_enc, attention, taps, expand, reduce = finished(*results)
    return (
        analysis.reshape(ROWS, COLS, CH),
        grad_enc,
        attention,
        taps.transpose(2, 0, 1, 3),
        expand,
        reduce,
    )


def solution(mesh):
    in_specs = (
        P("lat", "lon", None),
        P(("lon", "lat"), None, None),
        P(),
        P(),
        P(),
        P(),
        P(),
        P(),
        P(),
        P(),
        P("lat", "lon", None),
    )
    out_specs = (P("lat", "lon", None), P(("lon", "lat"), None, None), P(), P(), P(), P())
    return jax.shard_map(local, mesh=mesh, in_specs=in_specs, out_specs=out_specs, check_vma=False)
```
